32 devices in a mesh: step: 8 (over z, y), space: 4 (over x, core).
Axes of the slice: x: 2, y: 2, z: 4, core: 2. Of those that a mesh axis runs over, the one named last changes fastest.
Arguments:
- guesses: float32 [8, 64, 4, 2560], P('step', None, None, 'space'), may hold values from -6 to 6
- noise: float32 [8, 64, 4, 2560], P('step', None, None, 'space'), may hold values from -6 to 6
- timesteps: int32 [8, 2], P('step'), may hold values from 1 to 999, as said below
- conv_first: bfloat16 [3, 256, 576], replicated, may hold values from -0.15625 to 0.15625
- conv_second: bfloat16 [3, 64, 2304], replicated, may hold values from -0.078125 to 0.078125
- time_weight: float32 [64, 256], replicated, may hold values from -0.75 to 0.75
Outputs:
- states: float32 [8, 64, 4, 2560], P('step', None, None, 'space')
- changes: float32 [8], P('step')
The draws below stay inside these ranges and needn't reach their ends.
Inputs may be any that keep to these rules, and one draw needn't show every extreme that they name: Row k holds the timesteps before and after step k: the first entry of row 0 is 999, the second entry of the last row is 1, each row's second entry equals the next row's first, and the first entries fall strictly.
All inputs are finite; a program needn't handle non-finite values.
Results may differ from the reference program's by a relative error of at most 0.0019.
Values may be sent and summed in bfloat16 or wider, within the bound.
No kernel may reach another device: no remote copies, remote signals or barrier semaphores. Data moves between devices by JAX's collectives and lax.ppermute only.
A program may use at most 64 MiB of HBM per device.

```python
import math
import jax
import jax.numpy as jnp
from jax import lax

C = 64
HID = 256
FRAMES = 4
COLS = 80
STEPS = 8
ROWS = 32


def draw_timesteps(key, part):
    order = jax.random.permutation(jax.random.fold_in(key, 7), 997)
    middle = (order[:STEPS - 1] + 2).astype(jnp.int32)
    middle = -jnp.sort(-middle)
    chain = jnp.concatenate([jnp.array([999], jnp.int32), middle, jnp.array([1], jnp.int32)])
    return jnp.stack([chain[:-1], chain[1:]], axis=1)


def levels(own_key, dims, shards, low, largest):
    gain, own = 1.0, jax.random.fold_in(own_key, 6)
    for position, shards_of in shards:
        steps = jnp.exp(jax.random.uniform(jax.random.fold_in(own, position), (shards_of,), jnp.float32, low / len(shards), largest / len(shards)))
        gain = gain * jnp.repeat(steps, dims[position] // shards_of).reshape([-1 if axis == position else 1 for axis in range(len(dims))])
    return gain


def bell_draw(stream_key, shape, width, most, pieces=(), kind=jnp.bfloat16):
    values = jax.random.normal(stream_key, shape, jnp.float32) * width
    if len(pieces) > 0:
        values = levels(stream_key, shape, pieces, -0.22, 0.18) * values
    return jnp.clip(values, min=-most, max=most).astype(kind)


def setup_inputs(seed: int = 0) -> dict:
    seeds = jax.random.split(jax.random.key(seed), 7)
    guesses = bell_draw(seeds[0], (STEPS, C, FRAMES, ROWS * COLS), 1.0, 6.0, ((0, 8), (3, 4)), jnp.float32)
    noise = bell_draw(seeds[1], (STEPS, C, FRAMES, ROWS * COLS), 1.0, 6.0, ((0, 8), (3, 4)), jnp.float32)
    timesteps = draw_timesteps(jax.random.fold_in(seeds[6], 71), 0)
    conv_first = bell_draw(seeds[3], (3, HID, 9 * C), (27 * C) ** -0.5, 0.15625)
    conv_second = bell_draw(seeds[4], (3, C, 9 * HID), (27 * HID) ** -0.5, 0.078125)
    time_weight = bell_draw(seeds[5], (C, HID), C ** -0.5, 0.75, (), jnp.float32)
    return {"guesses": guesses, "noise": noise, "timesteps": timesteps, "conv_first": conv_first, "conv_second": conv_second, "time_weight": time_weight}


def plan(timestep):
    scaled = timestep.astype(jnp.float32) / 1000.0
    return -(0.1 * scaled + 9.95 * scaled * scaled)

def coefficients(timestep_pair):
    log_from = plan(timestep_pair[0])
    log_to = plan(timestep_pair[1])
    half_gap = 0.5 * (log_to - log_from)
    decay_gain = jnp.expm1(half_gap)
    remain_from = -jnp.expm1(log_from)
    remain_to = -jnp.expm1(log_to)
    ratio_term = -jnp.expm1(log_from - log_to)
    noise_gain = -jnp.exp(half_gap) * jnp.sqrt(remain_from) + remain_to * jnp.exp(-half_gap) / jnp.sqrt(remain_from)
    spread_gain = jnp.sqrt(remain_to / remain_from * ratio_term)
    return (decay_gain, noise_gain, spread_gain)

def time_embed(timestep, time_weight):
    half_count = C // 2
    frequency = jnp.exp(-math.log(10000.0) * jnp.arange(half_count, dtype=jnp.float32) / half_count)
    angles = timestep.astype(jnp.float32) * frequency
    features = jnp.concatenate([jnp.sin(angles), jnp.cos(angles)])
    return jnp.dot(features, time_weight, preferred_element_type=jnp.float32, precision=lax.Precision.HIGHEST)

def convolve(volume, weight):
    out_count = weight.shape[1]
    in_count = weight.shape[2] // 9
    kernel = weight.astype(jnp.float32).reshape(3, out_count, 3, 3, in_count).transpose(1, 4, 0, 2, 3)
    result = lax.conv_general_dilated(volume[None], kernel, (1, 1, 1), ((1, 1), (1, 1), (1, 1)), dimension_numbers=('NCDHW', 'OIDHW', 'NCDHW'), precision=lax.Precision.HIGHEST)
    return result[0]

def drift_of(latent, noise_step, timestep_pair, conv_first, conv_second, time_weight):
    decay_gain, noise_gain, spread_gain = coefficients(timestep_pair)
    temb = time_embed(timestep_pair[0], time_weight)
    rounded = lax.optimization_barrier(latent.astype(jnp.bfloat16)).astype(jnp.float32)
    volume = rounded.reshape(C, FRAMES, ROWS, COLS)
    preact = convolve(volume, conv_first) + temb[:, None, None, None]
    hidden = lax.optimization_barrier(jax.nn.silu(preact).astype(jnp.bfloat16)).astype(jnp.float32)
    predicted = convolve(hidden, conv_second).reshape(C, FRAMES, ROWS * COLS)
    return decay_gain * latent + noise_gain * predicted + spread_gain * noise_step

def picard_sweep(trajectory, noise, timesteps, conv_first, conv_second, time_weight):

    def advance(running, inputs):
        latent, noise_step, timestep_pair = inputs
        drift = drift_of(latent, noise_step, timestep_pair, conv_first, conv_second, time_weight)
        reached = running + drift
        return (reached, (running, reached))
    _, (entering, reached) = lax.scan(advance, trajectory[0], (trajectory, noise, timesteps))
    return (entering, reached)

def reference(guesses, noise, timesteps, conv_first, conv_second, time_weight):
    entering_one, reached_one = picard_sweep(guesses, noise, timesteps, conv_first, conv_second, time_weight)
    entering_two, reached_two = picard_sweep(entering_one, noise, timesteps, conv_first, conv_second, time_weight)
    difference = reached_two - reached_one
    changes = jnp.sqrt(lax.optimization_barrier(jnp.mean(difference * difference, axis=(1, 2, 3))))
    return (reached_two, changes)
```

```python
import math

import jax
import jax.numpy as jnp
from jax import lax
from jax.experimental import pallas as pl
from jax.experimental.pallas import tpu as pltpu
from jax.sharding import PartitionSpec as P

C = 64
COLS = 80
LANES = 256
NT = (((1,), (1,)), ((), ()))


def plan(timestep):
    scaled = timestep.astype(jnp.float32) / 1000.0
    return -(0.1 * scaled + 9.95 * scaled * scaled)


def coefficients(timestep_pair):
    log_from = plan(timestep_pair[0])
    log_to = plan(timestep_pair[1])
    half_gap = 0.5 * (log_to - log_from)
    decay_gain = jnp.expm1(half_gap)
    remain_from = -jnp.expm1(log_from)
    remain_to = -jnp.expm1(log_to)
    ratio_term = -jnp.expm1(log_from - log_to)
    noise_gain = -jnp.exp(half_gap) * jnp.sqrt(remain_from) + remain_to * jnp.exp(
        -half_gap
    ) / jnp.sqrt(remain_from)
    spread_gain = jnp.sqrt(remain_to / remain_from * ratio_term)
    return (decay_gain, noise_gain, spread_gain)


def time_embed(timestep, time_weight):
    half_count = C // 2
    frequency = jnp.exp(-math.log(10000.0) * jnp.arange(half_count, dtype=jnp.float32) / half_count)
    angles = timestep.astype(jnp.float32) * frequency
    features = jnp.concatenate([jnp.sin(angles), jnp.cos(angles)])
    return jnp.dot(
        features, time_weight, preferred_element_type=jnp.float32, precision=lax.Precision.HIGHEST
    )


def denoise_kernel(scalars, latent, inner, outer, noise, first, second, temb, drift, largest, shifted, hidden):
    channels, frames, length = latent.shape
    count = temb.shape[1]
    edge = 2 * COLS
    extended = length + 2 * COLS
    chunk = extended // 2
    keep, gain, spread = scalars[0], scalars[1], scalars[2]
    top, bottom = scalars[3], scalars[4]
    even = scalars[5] > 0.5

    def spread_columns(values, at, frame):
        width = values.shape[1]
        column = lax.broadcasted_iota(jnp.int32, (1, width), 1) % COLS
        before = jnp.where(column >= 1, pltpu.roll(values, 1, 1), 0.0)
        after = jnp.where(column <= COLS - 2, pltpu.roll(values, width - 1, 1), 0.0)
        stack = jnp.concatenate([before, values, after, jnp.zeros_like(values)], axis=0)
        shifted[frame, pl.ds(at, width), :] = stack.astype(jnp.bfloat16).T

    def taps_of(frame):
        return [(a, b) for a in range(3) if 0 <= frame + a - 1 < frames for b in range(3)]

    def first_conv(frame):
        taps = taps_of(frame)
        weights = jnp.concatenate([first[a, :, b * LANES : (b + 1) * LANES] for a, b in taps], axis=1)
        for start in range(0, extended, chunk):
            cells = jnp.concatenate(
                [shifted[frame + a - 1, pl.ds(b * COLS + start, chunk), :] for a, b in taps], axis=1
            )
            value = lax.dot_general(cells, weights, NT, preferred_element_type=jnp.float32) + temb[...]
            active = value / (1.0 + jnp.exp(-value))
            place = start + lax.broadcasted_iota(jnp.int32, (chunk, 1), 0)
            inside = jnp.where(place < COLS, 1.0 - top, jnp.where(place >= extended - COLS, 1.0 - bottom, 1.0))
            active = jnp.where(inside > 0.5, active, 0.0)
            hidden[frame, pl.ds(start, chunk), :] = active.astype(jnp.bfloat16)

    def second_conv(frame):
        taps = taps_of(frame)
        cells = jnp.concatenate([hidden[frame + a - 1, pl.ds(b * COLS, length), :] for a, b in taps], axis=1)
        weights = jnp.concatenate(
            [
                jnp.concatenate(
                    [second[a, :, (b * 3 + e) * count : (b * 3 + e + 1) * count] for e in range(3)], axis=0
                )
                for a, b in taps
            ],
            axis=1,
        )
        parts = lax.dot_general(cells, weights, NT, preferred_element_type=jnp.float32).T
        column = lax.broadcasted_iota(jnp.int32, (1, length), 1) % COLS
        before = jnp.where(column >= 1, pltpu.roll(parts[:channels], 1, 1), 0.0)
        after = jnp.where(
            column <= COLS - 2, pltpu.roll(parts[2 * channels : 3 * channels], length - 1, 1), 0.0
        )
        predicted = before + parts[channels : 2 * channels] + after
        result = keep * latent[:, frame, :] + gain * predicted + spread * noise[:, frame, :]
        drift[:, frame, :] = result
        return jnp.max(jnp.abs(result), axis=0, keepdims=True)

    for frame in range(frames):
        near = inner[:, frame, :].astype(jnp.float32)
        far = outer[:, frame, :].astype(jnp.float32)
        spread_columns(jnp.where(even, far, near), 0, frame)
        spread_columns(latent[:, frame, :], edge, frame)
        spread_columns(jnp.where(even, near, far), edge + length, frame)
    peaks = []
    for frame in range(frames):
        first_conv(frame)
        if frame >= 1:
            peaks.append(second_conv(frame - 1))
    peaks.append(second_conv(frames - 1))
    peak = peaks[0]
    for other in peaks[1:]:
        peak = jnp.maximum(peak, other)
    largest[0] = jnp.max(peak)


def denoise(scalars, latent, inner, outer, noise, first, second, temb):
    channels, frames, length = latent.shape
    whole = pl.BlockSpec(memory_space=pltpu.VMEM)
    words = pl.BlockSpec(memory_space=pltpu.SMEM)
    return pl.pallas_call(
        denoise_kernel,
        out_shape=(
            jax.ShapeDtypeStruct(latent.shape, jnp.float32),
            jax.ShapeDtypeStruct((1,), jnp.float32),
        ),
        in_specs=[words] + [whole] * 7,
        out_specs=(whole, words),
        scratch_shapes=[
            pltpu.VMEM((frames, length + 4 * COLS, LANES), jnp.bfloat16),
            pltpu.VMEM((frames, length + 2 * COLS, temb.shape[1]), jnp.bfloat16),
        ],
        compiler_params=pltpu.CompilerParams(vmem_limit_bytes=24 * 2**20),
        cost_estimate=pl.CostEstimate(
            flops=5_000_000_000, bytes_accessed=4_000_000, transcendentals=1_000_000
        ),
        name="denoise",
    )(scalars, latent, inner, outer, noise, first, second, temb)


def exponent_of(largest):
    return jnp.clip(jnp.ceil(jnp.log2(largest)) + 1.0, -100.0, 126.0)


def send(values, exponent, pairs):
    small = (values * jnp.exp2(14.0 - exponent)).astype(jnp.float16)
    mark = jnp.full((1,) + values.shape[1:], exponent, jnp.float16)
    return lax.ppermute(jnp.concatenate([small, mark], axis=0), "step", pairs)


def receive(message):
    exponent = message[-1, 0, 0].astype(jnp.float32)
    return message[:-1].astype(jnp.float32) * jnp.exp2(exponent - 14.0), exponent


def prefix(term, largest, step_index):
    steps = lax.axis_size("step")
    half = term.shape[0] // 2
    odd = step_index % 2
    swap = [(i, i ^ 1) for i in range(steps)]
    exponent = exponent_of(largest)
    mine = lax.dynamic_slice_in_dim(term, odd * half, half, 0)
    yours = lax.dynamic_slice_in_dim(term, (1 - odd) * half, half, 0)
    partner, partner_exponent = receive(send(yours, exponent, swap))
    total = mine + partner
    reach = jnp.maximum(exponent, partner_exponent) + 1.0
    before = jnp.zeros_like(total)
    distance = 2
    while distance < steps:
        pairs = [(i, i + distance) for i in range(steps - distance)]
        got, got_exponent = receive(send(total, reach, pairs))
        total = total + got
        before = before + got
        reach = jnp.maximum(reach, got_exponent) + 1.0
        distance *= 2
    keep = before + jnp.where(odd == 1, partner, 0.0)
    give = before + jnp.where(odd == 0, mine, 0.0)
    other, _ = receive(send(give, reach, swap))
    low = jnp.where(odd == 0, keep, other)
    high = jnp.where(odd == 0, other, keep)
    return jnp.concatenate([low, high], axis=0)


def local(guesses, noise, timesteps, conv_first, conv_second, time_weight):
    step_index = lax.axis_index("step")
    row_block = lax.axis_index("space")
    space = lax.axis_size("space")
    start_latent = guesses[0]
    noise_step = noise[0]
    timestep_pair = timesteps[0]
    is_anchor = step_index == 0
    even = row_block % 2 == 0
    inner_pairs = [pair for i in range(0, space - 1, 2) for pair in ((i, i + 1), (i + 1, i))]
    outer_pairs = [pair for i in range(1, space - 1, 2) for pair in ((i, i + 1), (i + 1, i))]

    decay_gain, noise_gain, spread_gain = coefficients(timestep_pair)
    temb = time_embed(timestep_pair[0], time_weight).reshape(1, -1)
    scalars = jnp.stack(
        [
            decay_gain,
            noise_gain,
            spread_gain,
            (row_block == 0).astype(jnp.float32),
            (row_block == space - 1).astype(jnp.float32),
            even.astype(jnp.float32),
        ]
    )
    offsets, count, _ = conv_first.shape
    first = jnp.pad(
        conv_first.reshape(offsets, count, 3, 3 * C), ((0, 0), (0, 0), (0, 0), (0, LANES - 3 * C))
    ).reshape(offsets, count, 3 * LANES)

    def sweep(latent):
        edge = 2 * COLS
        head = latent[:, :, :edge].astype(jnp.bfloat16)
        tail = latent[:, :, latent.shape[2] - edge :].astype(jnp.bfloat16)
        inner = lax.ppermute(jnp.where(even, tail, head), "space", inner_pairs)
        outer = lax.ppermute(jnp.where(even, head, tail), "space", outer_pairs)
        drift, largest = denoise(scalars, latent, inner, outer, noise_step, first, conv_second, temb)
        term = drift + jnp.where(is_anchor, latent, 0.0)
        before = prefix(term, largest[0] + 8.0, step_index)
        entering = jnp.where(is_anchor, latent, before)
        return entering, entering + drift

    entering_one, reached_one = sweep(start_latent)
    _, reached_two = sweep(entering_one)
    difference = reached_two - reached_one
    norm_total = lax.psum(jnp.sum(difference * difference), "space")
    cell_count = difference.shape[0] * difference.shape[1] * difference.shape[2] * space
    changes = jnp.sqrt(norm_total / cell_count).reshape(1)
    return (reached_two[None], changes)


def solution(mesh):
    in_specs = (
        P("step", None, None, "space"),
        P("step", None, None, "space"),
        P("step", None),
        P(),
        P(),
        P(),
    )
    out_specs = (P("step", None, None, "space"), P("step"))
    return jax.shard_map(local, mesh=mesh, in_specs=in_specs, out_specs=out_specs, check_vma=False)
```

```python
import functools
import math

import jax
import jax.numpy as jnp
from jax import lax
from jax.experimental import pallas as pl
from jax.experimental.pallas import tpu as pltpu
from jax.sharding import PartitionSpec as P

C = 64
COLS = 80
SUB = 8
NT = (((1,), (1,)), ((), ()))
MEGA = 2**20


def plan(timestep):
    scaled = timestep.astype(jnp.float32) / 1000.0
    return -(0.1 * scaled + 9.95 * scaled * scaled)


def coefficients(timestep_pair):
    log_from = plan(timestep_pair[0])
    log_to = plan(timestep_pair[1])
    half_gap = 0.5 * (log_to - log_from)
    decay_gain = jnp.expm1(half_gap)
    remain_from = -jnp.expm1(log_from)
    remain_to = -jnp.expm1(log_to)
    ratio_term = -jnp.expm1(log_from - log_to)
    noise_gain = -jnp.exp(half_gap) * jnp.sqrt(remain_from) + remain_to * jnp.exp(
        -half_gap
    ) / jnp.sqrt(remain_from)
    spread_gain = jnp.sqrt(remain_to / remain_from * ratio_term)
    return (decay_gain, noise_gain, spread_gain)


def time_embed(timestep, time_weight):
    half_count = C // 2
    frequency = jnp.exp(-math.log(10000.0) * jnp.arange(half_count, dtype=jnp.float32) / half_count)
    angles = timestep.astype(jnp.float32) * frequency
    features = jnp.concatenate([jnp.sin(angles), jnp.cos(angles)])
    return jnp.dot(
        features, time_weight, preferred_element_type=jnp.float32, precision=lax.Precision.HIGHEST
    )


class Frames:
    def __init__(self, odd, parity):
        self.odd, self.parity = odd, parity

    def pick(self, ref, v):
        count = ref.shape[1]
        return jnp.where(self.odd, ref[:, v, :], ref[:, count - 1 - v, :])

    def slot(self, v):
        return jnp.where(self.parity == 1, v % 2, (v + 1) % 2)

    def load(self, ref, v):
        tiles = C // SUB
        return ref[pl.ds(self.slot(v) * tiles, tiles)].reshape(C, ref.shape[2])

    def store(self, ref, v, value):
        tiles = C // SUB
        ref[pl.ds(self.slot(v) * tiles, tiles)] = value.reshape(tiles, SUB, ref.shape[2])

    def tap(self, a):
        return jnp.where(self.parity == 1, a, 2 - a)


def entering_of(frames, flags, guesses, halves, v):
    start = frames.pick(guesses, v)
    if halves is None:
        return start
    other, keep = halves
    return jnp.where(flags.anchor, start, frames.load(other if v < 2 else keep, v))


class Flags:
    def __init__(self, whole, real):
        self.parity = whole[0]
        self.odd = whole[0] == 1
        self.even_block = whole[1] == 0
        self.anchor = whole[2] == 1
        self.keep, self.gain, self.spread = real[0], real[1], real[2]
        self.top, self.bottom = whole[3], whole[4]


def denoise_kernel(later, whole, real, guesses, *refs):
    halves = None
    if later:
        other, keep, *refs = refs
        halves = (other, keep)
    inner, outer, noise, first, second, temb, yours, mine, shifted, hidden = refs
    flags = Flags(whole, real)
    frames = Frames(flags.odd, flags.parity)
    channels, count, length = guesses.shape
    width = temb.shape[1]
    edge = 2 * COLS
    extended = length + 2 * COLS
    chunk = extended // 2
    top, bottom = flags.top == 1, flags.bottom == 1

    def spread_columns(values, at, v):
        n = values.shape[1]
        column = lax.broadcasted_iota(jnp.int32, (1, n), 1) % COLS
        before = jnp.where(column >= 1, pltpu.roll(values, 1, 1), 0.0).astype(jnp.bfloat16)
        after = jnp.where(column <= COLS - 2, pltpu.roll(values, n - 1, 1), 0.0).astype(jnp.bfloat16)
        center = values.astype(jnp.bfloat16)
        shifted[v, pl.ds(at, n), 0:128] = jnp.concatenate([before, center], axis=0).T
        shifted[v, pl.ds(at, n), 256:384] = jnp.concatenate([center, after], axis=0).T
        mixed = jnp.concatenate([after, before], axis=0).T
        shifted[v, pl.ds(at, n), 128:192] = mixed[:, :64]
        if at >= COLS:
            shifted[v, pl.ds(at - COLS, n), 192:256] = mixed[:, 64:]
        else:
            shifted[v, pl.ds(0, n - COLS), 192:256] = mixed[COLS:, 64:]

    def halo(ref, v):
        tiles = C // SUB
        at = (0 if v < 2 else 2 * tiles) + frames.slot(v) * tiles
        return ref[pl.ds(at, tiles)].astype(jnp.float32).reshape(C, ref.shape[2])

    def prepare(v):
        shifted[v, pl.ds(length + 3 * COLS, COLS), 128:256] = jnp.zeros((COLS, 128), jnp.bfloat16)
        near, far = halo(inner, v), halo(outer, v)
        spread_columns(jnp.where(flags.even_block, far, near), 0, v)
        spread_columns(entering_of(frames, flags, guesses, halves, v), edge, v)
        spread_columns(jnp.where(flags.even_block, near, far), edge + length, v)

    def near_frames(v):
        return [a for a in range(3) if 0 <= v + a - 1 < count]

    def first_conv(v):
        weights = []
        for a in near_frames(v):
            w = first[frames.tap(a)]
            weights += [w[:, :512], w[:, 512:], jnp.zeros((width, 64), jnp.bfloat16)]
        weights = jnp.concatenate(weights, axis=1)
        for start in range(0, extended, chunk):
            cells = []
            for a in near_frames(v):
                for b, low, high in ((0, 0, 256), (1, 256, 384), (2, 0, 256)):
                    cells.append(shifted[v + a - 1, pl.ds(b * COLS + start, chunk), low:high])
            cells = jnp.concatenate(cells, axis=1)
            value = lax.dot_general(cells, weights, NT, preferred_element_type=jnp.float32) + temb[...]
            active = value / (1.0 + jnp.exp(-value))
            place = start + lax.broadcasted_iota(jnp.int32, (chunk, 1), 0)
            outside = jnp.logical_or(
                jnp.logical_and(place < COLS, top), jnp.logical_and(place >= extended - COLS, bottom)
            )
            hidden[v, pl.ds(start, chunk), :] = jnp.where(outside, 0.0, active).astype(jnp.bfloat16)

    def second_conv(v):
        taps = [(a, b) for a in near_frames(v) for b in range(3)]
        cells = jnp.concatenate([hidden[v + a - 1, pl.ds(b * COLS, length), :] for a, b in taps], axis=1)
        weights = jnp.concatenate(
            [
                jnp.concatenate(
                    [
                        second[frames.tap(a), :, (b * 3 + e) * width : (b * 3 + e + 1) * width]
                        for e in range(3)
                    ],
                    axis=0,
                )
                for a, b in taps
            ],
            axis=1,
        )
        parts = lax.dot_general(cells, weights, NT, preferred_element_type=jnp.float32).T
        column = lax.broadcasted_iota(jnp.int32, (1, length), 1) % COLS
        before = jnp.where(column >= 1, pltpu.roll(parts[:channels], 1, 1), 0.0)
        after = jnp.where(
            column <= COLS - 2, pltpu.roll(parts[2 * channels : 3 * channels], length - 1, 1), 0.0
        )
        predicted = before + parts[channels : 2 * channels] + after
        latent = entering_of(frames, flags, guesses, halves, v)
        result = flags.keep * latent + flags.gain * predicted + flags.spread * frames.pick(noise, v)
        result = result + jnp.where(flags.anchor, latent, 0.0)
        frames.store(yours if v < 2 else mine, v, result)
        return jnp.max(jnp.abs(result), axis=0, keepdims=True)

    def mark(ref, peaks):
        peak = jnp.max(functools.reduce(jnp.maximum, peaks), axis=1, keepdims=True)
        exponent = jnp.clip(jnp.ceil(jnp.log(peak) * (1.0 / math.log(2.0))) + 1.0, -100.0, 126.0)
        ref[ref.shape[0] - 1] = jnp.broadcast_to(exponent, (SUB, length))

    prepare(0)
    prepare(1)
    peaks = []
    for v in range(count):
        first_conv(v)
        if v + 2 < count:
            prepare(v + 2)
        if v >= 1:
            peaks.append(second_conv(v - 1))
    peaks.append(second_conv(count - 1))
    mark(yours, peaks[: count // 2])
    mark(mine, peaks[count // 2 :])


WHOLE = pl.BlockSpec(memory_space=pltpu.VMEM)
WORDS = pl.BlockSpec(memory_space=pltpu.SMEM)


def denoise(whole, real, guesses, halves, inner, outer, noise, first, second, temb):
    channels, frames, length = guesses.shape
    half = jax.ShapeDtypeStruct((frames // 2 * channels // SUB + 1, SUB, length), jnp.float32)
    later = halves is not None
    operands = (whole, real, guesses) + (halves if later else ()) + (inner, outer, noise, first, second, temb)
    return pl.pallas_call(
        functools.partial(denoise_kernel, later),
        out_shape=(half, half),
        in_specs=[WORDS] * 2 + [WHOLE] * (len(operands) - 2),
        out_specs=(WHOLE, WHOLE),
        scratch_shapes=[
            pltpu.VMEM((frames, length + 4 * COLS, 384), jnp.bfloat16),
            pltpu.VMEM((frames, length + 2 * COLS, temb.shape[1]), jnp.bfloat16),
        ],
        compiler_params=pltpu.CompilerParams(vmem_limit_bytes=24 * MEGA),
        cost_estimate=pl.CostEstimate(flops=5_000_000_000, bytes_accessed=4_000_000, transcendentals=1_000_000),
        name="denoise",
    )(*operands)


def finish_kernel(whole, real, guesses, other1, keep1, yours1, mine1, other2, keep2, yours2, mine2, states, total):
    flags = Flags(whole, real)
    frames = Frames(flags.odd, flags.parity)
    count = guesses.shape[1]
    square = jnp.zeros((C, guesses.shape[2]), jnp.float32)
    for frame in range(count):
        low = frame < count // 2
        slot = (frame % 2) * (C // SUB)

        def part(first_ref, second_ref):
            one = first_ref[pl.ds(slot, C // SUB)].reshape(C, guesses.shape[2])
            two = second_ref[pl.ds(slot, C // SUB)].reshape(C, guesses.shape[2])
            return jnp.where(flags.odd, one, two) if low else jnp.where(flags.odd, two, one)

        before1 = jnp.where(flags.anchor, 0.0, part(other1, keep1))
        before2 = jnp.where(flags.anchor, 0.0, part(other2, keep2))
        reached1 = before1 + part(yours1, mine1)
        reached2 = before2 + part(yours2, mine2)
        states[:, frame, :] = reached2
        change = reached2 - reached1
        square = square + change * change
    total[...] = jnp.broadcast_to(jnp.sum(jnp.sum(square, axis=0, keepdims=True), axis=1, keepdims=True), total.shape)


def finish(whole, real, guesses, *halves):
    return pl.pallas_call(
        finish_kernel,
        out_shape=(
            jax.ShapeDtypeStruct(guesses.shape, jnp.float32),
            jax.ShapeDtypeStruct((SUB, 128), jnp.float32),
        ),
        in_specs=[WORDS] * 2 + [WHOLE] * 9,
        out_specs=(WHOLE, WHOLE),
        compiler_params=pltpu.CompilerParams(vmem_limit_bytes=24 * MEGA),
        cost_estimate=pl.CostEstimate(flops=4_000_000, bytes_accessed=7_000_000, transcendentals=0),
        name="finish",
    )(whole, real, guesses, *halves)


def is_mark(half):
    return lax.broadcasted_iota(jnp.int32, half.shape, 0) == half.shape[0] - 1


def coded(half):
    exponent = half[-1:]
    return jnp.where(is_mark(half), half, half * jnp.exp2(14.0 - exponent)).astype(jnp.float16)


def decoded(message):
    half = message.astype(jnp.float32)
    return jnp.where(is_mark(half), half, half * jnp.exp2(half[-1:] - 14.0))


def added(one, two):
    return jnp.where(is_mark(one), jnp.maximum(one, two) + 1.0, one + two)


def masked(half, condition):
    return jnp.where(condition, half, jnp.where(is_mark(half), -100.0, 0.0))


def exchange(half, distance):
    steps = lax.axis_size("step")
    return decoded(lax.ppermute(coded(half), "step", [(i, i ^ distance) for i in range(steps)]))


def prefix(yours, mine, step_index):
    steps = lax.axis_size("step")
    odd = step_index % 2 == 1
    partner = exchange(yours, 1)
    total = added(mine, partner)
    before = masked(total, False)
    distance = 2
    while distance < steps:
        got = exchange(total, distance)
        before = added(before, masked(got, (step_index // distance) % 2 == 1))
        total = added(total, got)
        distance *= 2
    keep = added(before, masked(partner, odd))
    give = added(before, masked(mine, jnp.logical_not(odd)))
    return exchange(give, 1), keep


def local(guesses, noise, timesteps, conv_first, conv_second, time_weight):
    step_index = lax.axis_index("step")
    row_block = lax.axis_index("space")
    space = lax.axis_size("space")
    start_latent = guesses[0]
    noise_step = noise[0]
    timestep_pair = timesteps[0]
    edge = 2 * COLS
    length = start_latent.shape[2]
    even = row_block % 2 == 0
    inner_pairs = [pair for i in range(0, space - 1, 2) for pair in ((i, i + 1), (i + 1, i))]
    outer_pairs = [pair for i in range(1, space - 1, 2) for pair in ((i, i + 1), (i + 1, i))]

    real = jnp.stack(coefficients(timestep_pair))
    temb = time_embed(timestep_pair[0], time_weight).reshape(1, -1)
    whole = jnp.stack([step_index % 2, row_block % 2, step_index == 0, row_block == 0, row_block == space - 1])
    whole = whole.astype(jnp.int32)

    def halos(head, tail):
        inner = lax.ppermute(jnp.where(even, tail, head), "space", inner_pairs)
        outer = lax.ppermute(jnp.where(even, head, tail), "space", outer_pairs)
        return inner, outer

    def ends(values):
        rounded = values.astype(jnp.bfloat16)
        return rounded[..., :edge], rounded[..., length - edge :]

    def ordered(values):
        moved = values.transpose(1, 0, 2)
        count = moved.shape[0] // 2
        turned = jnp.concatenate([moved[count:], moved[:count]], axis=0)
        return jnp.where(step_index % 2 == 1, moved, turned).reshape(-1, SUB, edge)

    head1, tail1 = (ordered(side) for side in ends(start_latent))
    inner, outer = halos(head1, tail1)
    yours1, mine1 = denoise(whole, real, start_latent, None, inner, outer, noise_step, conv_first, conv_second, temb)
    other1, keep1 = prefix(yours1, mine1, step_index)
    heads, tails = zip(ends(other1[:-1]), ends(keep1[:-1]))
    is_anchor = step_index == 0
    head2 = jnp.where(is_anchor, head1, jnp.concatenate(heads, axis=0))
    tail2 = jnp.where(is_anchor, tail1, jnp.concatenate(tails, axis=0))
    inner2, outer2 = halos(head2, tail2)
    yours2, mine2 = denoise(
        whole, real, start_latent, (other1, keep1), inner2, outer2, noise_step, conv_first, conv_second, temb
    )
    other2, keep2 = prefix(yours2, mine2, step_index)
    states, total = finish(whole, real, start_latent, other1, keep1, yours1, mine1, other2, keep2, yours2, mine2)
    norm_total = lax.psum(total[0, 0], "space")
    cell_count = start_latent.size * space
    changes = jnp.sqrt(norm_total / cell_count).reshape(1)
    return (states[None], changes)


def solution(mesh):
    in_specs = (
        P("step", None, None, "space"),
        P("step", None, None, "space"),
        P("step", None),
        P(),
        P(),
        P(),
    )
    out_specs = (P("step", None, None, "space"), P("step"))
    return jax.shard_map(local, mesh=mesh, in_specs=in_specs, out_specs=out_specs, check_vma=False)
```

```python
import functools
import math

import jax
import jax.numpy as jnp
from jax import lax
from jax.experimental import pallas as pl
from jax.experimental.pallas import tpu as pltpu
from jax.sharding import PartitionSpec as P

C = 64
COLS = 80
SUB = 8
NT = (((1,), (1,)), ((), ()))
MEGA = 2**20


def plan(timestep):
    scaled = timestep.astype(jnp.float32) / 1000.0
    return -(0.1 * scaled + 9.95 * scaled * scaled)


def coefficients(timestep_pair):
    log_from = plan(timestep_pair[0])
    log_to = plan(timestep_pair[1])
    half_gap = 0.5 * (log_to - log_from)
    decay_gain = jnp.expm1(half_gap)
    remain_from = -jnp.expm1(log_from)
    remain_to = -jnp.expm1(log_to)
    ratio_term = -jnp.expm1(log_from - log_to)
    noise_gain = -jnp.exp(half_gap) * jnp.sqrt(remain_from) + remain_to * jnp.exp(
        -half_gap
    ) / jnp.sqrt(remain_from)
    spread_gain = jnp.sqrt(remain_to / remain_from * ratio_term)
    return (decay_gain, noise_gain, spread_gain)


def time_embed(timestep, time_weight):
    half_count = C // 2
    frequency = jnp.exp(-math.log(10000.0) * jnp.arange(half_count, dtype=jnp.float32) / half_count)
    angles = timestep.astype(jnp.float32) * frequency
    features = jnp.concatenate([jnp.sin(angles), jnp.cos(angles)])
    return jnp.dot(
        features, time_weight, preferred_element_type=jnp.float32, precision=lax.Precision.HIGHEST
    )


class Frames:
    def __init__(self, odd, parity):
        self.odd, self.parity = odd, parity

    def pick(self, ref, v):
        count = ref.shape[1]
        return jnp.where(self.odd, ref[:, v, :], ref[:, count - 1 - v, :])

    def slot(self, v):
        return jnp.where(self.parity == 1, v % 2, (v + 1) % 2)

    def load(self, ref, v):
        tiles = C // SUB
        return ref[pl.ds(self.slot(v) * tiles, tiles)].reshape(C, ref.shape[2])

    def store(self, ref, v, value):
        tiles = C // SUB
        ref[pl.ds(self.slot(v) * tiles, tiles)] = value.reshape(tiles, SUB, ref.shape[2])

    def tap(self, a):
        return jnp.where(self.parity == 1, a, 2 - a)


def entering_of(frames, flags, guesses, halves, v):
    start = frames.pick(guesses, v)
    if halves is None:
        return start
    other, keep = halves
    return jnp.where(flags.anchor, start, frames.load(other if v < 2 else keep, v))


class Flags:
    def __init__(self, whole, real):
        self.parity = whole[0]
        self.odd = whole[0] == 1
        self.even_block = whole[1] == 0
        self.anchor = whole[2] == 1
        self.keep, self.gain, self.spread = real[0], real[1], real[2]
        self.top, self.bottom = whole[3], whole[4]


def halo_slot(frames, v):
    tiles = C // SUB
    return pl.ds((0 if v < 2 else 2 * tiles) + frames.slot(v) * tiles, tiles)


def edges_kernel(later, whole, real, guesses, *refs):
    halves = None
    if later:
        other, keep, *refs = refs
        halves = (other, keep)
    inner, outer = refs
    flags = Flags(whole, real)
    frames = Frames(flags.odd, flags.parity)
    count, length = guesses.shape[1:]
    edge = 2 * COLS
    for v in range(count):
        latent = entering_of(frames, flags, guesses, halves, v).astype(jnp.bfloat16)
        shape = (C // SUB, SUB, edge)
        head, tail = latent[:, :edge].reshape(shape), latent[:, length - edge :].reshape(shape)
        at = halo_slot(frames, v)
        inner[at] = jnp.where(flags.even_block, tail, head)
        outer[at] = jnp.where(flags.even_block, head, tail)


class Shared:
    def __init__(self, flags, frames, halves, guesses, noise, first, second, temb, shifted, hidden):
        self.flags, self.frames, self.halves, self.guesses, self.noise = flags, frames, halves, guesses, noise
        self.first, self.second, self.temb, self.shifted, self.hidden = first, second, temb, shifted, hidden
        self.channels, self.count, self.length = guesses.shape
        self.width = temb.shape[1]
        self.extended = self.length + 2 * COLS

    def entering(self, v):
        return entering_of(self.frames, self.flags, self.guesses, self.halves, v)

    def spread_columns(self, values, at, v):
        ref, i = self.shifted[v]
        n = values.shape[1]
        column = lax.broadcasted_iota(jnp.int32, (1, n), 1) % COLS
        before = jnp.where(column >= 1, pltpu.roll(values, 1, 1), 0.0).astype(jnp.bfloat16)
        after = jnp.where(column <= COLS - 2, pltpu.roll(values, n - 1, 1), 0.0).astype(jnp.bfloat16)
        center = values.astype(jnp.bfloat16)
        ref[i, pl.ds(at, n), 0:128] = jnp.concatenate([before, center], axis=0).T
        ref[i, pl.ds(at, n), 256:384] = jnp.concatenate([center, after], axis=0).T
        mixed = jnp.concatenate([after, before], axis=0).T
        ref[i, pl.ds(at, n), 128:192] = mixed[:, :64]
        if at >= COLS:
            ref[i, pl.ds(at - COLS, n), 192:256] = mixed[:, 64:]
        else:
            ref[i, pl.ds(0, n - COLS), 192:256] = mixed[COLS:, 64:]

    def prepare(self, v, inner, outer):
        ref, i = self.shifted[v]
        ref[i, pl.ds(self.length + 3 * COLS, COLS), 128:256] = jnp.zeros((COLS, 128), jnp.bfloat16)
        at = halo_slot(self.frames, v)
        edge = 2 * COLS
        near = inner[at].astype(jnp.float32).reshape(C, edge)
        far = outer[at].astype(jnp.float32).reshape(C, edge)
        even = self.flags.even_block
        self.spread_columns(jnp.where(even, far, near), 0, v)
        self.spread_columns(self.entering(v), edge, v)
        self.spread_columns(jnp.where(even, near, far), edge + self.length, v)

    def near_frames(self, v):
        return [a for a in range(3) if 0 <= v + a - 1 < self.count]

    def first_conv(self, v):
        extended, chunk = self.extended, self.extended // 2
        top, bottom = self.flags.top == 1, self.flags.bottom == 1
        weights = []
        for a in self.near_frames(v):
            weights += [self.first[self.frames.tap(a)], jnp.zeros((64, self.width), jnp.bfloat16)]
        weights = jnp.concatenate(weights, axis=0)
        out, place_of = self.hidden[v]
        for start in range(0, extended, chunk):
            cells = []
            for a in self.near_frames(v):
                ref, i = self.shifted[v + a - 1]
                for b, low, high in ((0, 0, 256), (1, 256, 384), (2, 0, 256)):
                    cells.append(ref[i, pl.ds(b * COLS + start, chunk), low:high])
            cells = jnp.concatenate(cells, axis=1)
            value = jnp.dot(cells, weights, preferred_element_type=jnp.float32) + self.temb[...]
            active = value / (1.0 + jnp.exp(-value))
            place = start + lax.broadcasted_iota(jnp.int32, (chunk, 1), 0)
            outside = jnp.logical_or(
                jnp.logical_and(place < COLS, top), jnp.logical_and(place >= extended - COLS, bottom)
            )
            out[place_of, pl.ds(start, chunk), :] = jnp.where(outside, 0.0, active).astype(jnp.bfloat16)

    def second_conv(self, v, out):
        channels, length, width, flags = self.channels, self.length, self.width, self.flags
        cells, weights = [], []
        for a in self.near_frames(v):
            ref, i = self.hidden[v + a - 1]
            tap = self.frames.tap(a)
            for b in range(3):
                cells.append(ref[i, pl.ds(b * COLS, length), :])
                columns = [
                    self.second[tap, :, (b * 3 + e) * width : (b * 3 + e + 1) * width] for e in range(3)
                ]
                weights.append(jnp.concatenate(columns, axis=0))
        cells, weights = jnp.concatenate(cells, axis=1), jnp.concatenate(weights, axis=1)
        parts = lax.dot_general(cells, weights, NT, preferred_element_type=jnp.float32).T
        column = lax.broadcasted_iota(jnp.int32, (1, length), 1) % COLS
        before = jnp.where(column >= 1, pltpu.roll(parts[:channels], 1, 1), 0.0)
        after = jnp.where(
            column <= COLS - 2, pltpu.roll(parts[2 * channels : 3 * channels], length - 1, 1), 0.0
        )
        predicted = before + parts[channels : 2 * channels] + after
        latent = self.entering(v)
        result = flags.keep * latent + flags.gain * predicted + flags.spread * self.frames.pick(self.noise, v)
        result = result + jnp.where(flags.anchor, latent, 0.0)
        self.frames.store(out, v, result)
        return jnp.max(jnp.abs(result), axis=0, keepdims=True)

    def mark(self, ref, peaks):
        peak = jnp.max(functools.reduce(jnp.maximum, peaks), axis=1, keepdims=True)
        exponent = jnp.clip(jnp.ceil(jnp.log(peak) * (1.0 / math.log(2.0))) + 1.0, -100.0, 126.0)
        ref[ref.shape[0] - 1] = jnp.broadcast_to(exponent, (SUB, self.length))


def sending_kernel(later, whole, real, guesses, *refs):
    halves = None
    if later:
        other, keep, *refs = refs
        halves = (other, keep)
    inner, outer, noise, first, second, temb, yours, spread_out, hidden_out, spread_own, hidden_own = refs
    flags = Flags(whole, real)
    frames = Frames(flags.odd, flags.parity)
    shifted = {0: (spread_own, 0), 1: (spread_own, 1), 2: (spread_out, 0), 3: (spread_out, 1)}
    hidden = {0: (hidden_own, 0), 1: (hidden_out, 0), 2: (hidden_out, 1)}
    work = Shared(flags, frames, halves, guesses, noise, first, second, temb, shifted, hidden)
    work.prepare(0, inner, outer)
    work.prepare(1, inner, outer)
    work.first_conv(0)
    work.prepare(2, inner, outer)
    work.first_conv(1)
    work.prepare(3, inner, outer)
    peaks = [work.second_conv(0, yours)]
    work.first_conv(2)
    peaks.append(work.second_conv(1, yours))
    work.mark(yours, peaks)


def keeping_kernel(later, whole, real, guesses, *refs):
    halves = None
    if later:
        other, keep, *refs = refs
        halves = (other, keep)
    spread_in, hidden_in, noise, first, second, temb, mine, hidden_own = refs
    flags = Flags(whole, real)
    frames = Frames(flags.odd, flags.parity)
    shifted = {2: (spread_in, 0), 3: (spread_in, 1)}
    hidden = {1: (hidden_in, 0), 2: (hidden_in, 1), 3: (hidden_own, 0)}
    work = Shared(flags, frames, halves, guesses, noise, first, second, temb, shifted, hidden)
    work.first_conv(3)
    peaks = [work.second_conv(2, mine), work.second_conv(3, mine)]
    work.mark(mine, peaks)


WHOLE = pl.BlockSpec(memory_space=pltpu.VMEM)
WORDS = pl.BlockSpec(memory_space=pltpu.SMEM)


def call(kernel, name, operands, out_shape, scratch, flops):
    return pl.pallas_call(
        kernel,
        out_shape=out_shape,
        in_specs=[WORDS] * 2 + [WHOLE] * (len(operands) - 2),
        out_specs=tuple(WHOLE for _ in out_shape),
        scratch_shapes=scratch,
        compiler_params=pltpu.CompilerParams(vmem_limit_bytes=24 * MEGA),
        cost_estimate=pl.CostEstimate(flops=flops, bytes_accessed=4_000_000, transcendentals=100_000),
        name=name,
    )(*operands)


def edges(whole, real, guesses, halves):
    channels, frames, _ = guesses.shape
    shape = jax.ShapeDtypeStruct((frames * channels // SUB, SUB, 2 * COLS), jnp.bfloat16)
    operands = (whole, real, guesses) + (halves or ())
    return call(functools.partial(edges_kernel, halves is not None), "edges", operands, (shape, shape), [], 100_000)


def denoise(whole, real, guesses, halves, inner, outer, noise, first, second, temb):
    channels, frames, length = guesses.shape
    half = jax.ShapeDtypeStruct((frames // 2 * channels // SUB + 1, SUB, length), jnp.float32)
    spread = (2, length + 4 * COLS, 384)
    hidden = (2, length + 2 * COLS, temb.shape[1])
    later = halves is not None
    start = (whole, real, guesses) + (halves or ())
    yours, spread_mid, hidden_mid = call(
        functools.partial(sending_kernel, later),
        "sending",
        start + (inner, outer, noise, first, second, temb),
        (half, jax.ShapeDtypeStruct(spread, jnp.bfloat16), jax.ShapeDtypeStruct(hidden, jnp.bfloat16)),
        [pltpu.VMEM(spread, jnp.bfloat16), pltpu.VMEM((1,) + hidden[1:], jnp.bfloat16)],
        3_000_000_000,
    )
    (mine,) = call(
        functools.partial(keeping_kernel, later),
        "keeping",
        start + (spread_mid, hidden_mid, noise, first, second, temb),
        (half,),
        [pltpu.VMEM((1,) + hidden[1:], jnp.bfloat16)],
        2_000_000_000,
    )
    return yours, mine


def finish_kernel(whole, real, guesses, other, keep, yours, mine, states):
    flags = Flags(whole, real)
    count, length = guesses.shape[1:]
    tiles = C // SUB
    for frame in range(count):
        low = frame < count // 2
        at = pl.ds((frame % 2) * tiles, tiles)

        def part(first_ref, second_ref):
            one, two = first_ref[at].reshape(C, length), second_ref[at].reshape(C, length)
            return jnp.where(flags.odd, one, two) if low else jnp.where(flags.odd, two, one)

        before = jnp.where(flags.anchor, 0.0, part(other, keep))
        states[:, frame, :] = before + part(yours, mine)


def finish(whole, real, guesses, *halves):
    shape = jax.ShapeDtypeStruct(guesses.shape, jnp.float32)
    (states,) = call(finish_kernel, "finish", (whole, real, guesses) + halves, (shape,), [], 1_000_000)
    return states


def changes_kernel(whole, real, *refs):
    *sweeps, own, theirs = refs
    tiles = 2 * C // SUB

    def reached(before, term):
        return before[pl.ds(0, tiles)] + term[pl.ds(0, tiles)]

    for out, at in ((own, 0), (theirs, 2)):
        change = reached(sweeps[4 + at], sweeps[5 + at]) - reached(sweeps[at], sweeps[1 + at])
        square = jnp.sum(change * change, axis=0)
        total = jnp.sum(jnp.sum(square, axis=0, keepdims=True), axis=1, keepdims=True)
        out[...] = jnp.broadcast_to(total, out.shape)


def change_sums(whole, real, one, two):
    shape = jax.ShapeDtypeStruct((SUB, 128), jnp.float32)
    return call(changes_kernel, "changes", (whole, real) + one + two, (shape, shape), [], 1_000_000)


def is_mark(half):
    return lax.broadcasted_iota(jnp.int32, half.shape, 0) == half.shape[0] - 1


def coded(half):
    exponent = half[-1:]
    return jnp.where(is_mark(half), half, half * jnp.exp2(14.0 - exponent)).astype(jnp.float16)


def decoded(message):
    half = message.astype(jnp.float32)
    return jnp.where(is_mark(half), half, half * jnp.exp2(half[-1:] - 14.0))


def added(one, two):
    return jnp.where(is_mark(one), jnp.maximum(one, two) + 1.0, one + two)


def masked(half, condition):
    return jnp.where(condition, half, jnp.where(is_mark(half), -100.0, 0.0))


def exchange(half, distance):
    steps = lax.axis_size("step")
    return decoded(lax.ppermute(coded(half), "step", [(i, i ^ distance) for i in range(steps)]))


def prefix(yours, mine, step_index):
    steps = lax.axis_size("step")
    odd = step_index % 2 == 1
    partner = exchange(yours, 1)
    total = added(mine, partner)
    before = masked(total, False)
    distance = 2
    while distance < steps:
        got = exchange(total, distance)
        before = added(before, masked(got, (step_index // distance) % 2 == 1))
        total = added(total, got)
        distance *= 2
    keep = added(before, masked(partner, odd))
    give = added(before, masked(mine, jnp.logical_not(odd)))
    return exchange(give, 1), keep, (keep, mine, give, partner)


def local(guesses, noise, timesteps, conv_first, conv_second, time_weight):
    step_index = lax.axis_index("step")
    row_block = lax.axis_index("space")
    space = lax.axis_size("space")
    start_latent = guesses[0]
    noise_step = noise[0]
    timestep_pair = timesteps[0]
    inner_pairs = [pair for i in range(0, space - 1, 2) for pair in ((i, i + 1), (i + 1, i))]
    outer_pairs = [pair for i in range(1, space - 1, 2) for pair in ((i, i + 1), (i + 1, i))]

    real = jnp.stack(coefficients(timestep_pair))
    temb = time_embed(timestep_pair[0], time_weight).reshape(1, -1)
    whole = jnp.stack([step_index % 2, row_block % 2, step_index == 0, row_block == 0, row_block == space - 1])
    whole = whole.astype(jnp.int32)

    first = conv_first.transpose(0, 2, 1)

    def sweep(halves):
        near, far = edges(whole, real, start_latent, halves)
        inner = lax.ppermute(near, "space", inner_pairs)
        outer = lax.ppermute(far, "space", outer_pairs)
        yours, mine = denoise(
            whole, real, start_latent, halves, inner, outer, noise_step, first, conv_second, temb
        )
        return yours, mine, prefix(yours, mine, step_index)

    _, _, (other1, keep1, reached1) = sweep(None)
    yours2, mine2, (other2, keep2, reached2) = sweep((other1, keep1))
    own, theirs = change_sums(whole, real, reached1, reached2)
    total = own + lax.ppermute(theirs, "step", [(i, i ^ 1) for i in range(lax.axis_size("step"))])
    if space & (space - 1):
        total = lax.psum(total, "space")
    else:
        distance = 1
        while distance < space:
            total = total + lax.ppermute(total, "space", [(i, i ^ distance) for i in range(space)])
            distance *= 2
    states = finish(whole, real, start_latent, other2, keep2, yours2, mine2)
    cell_count = start_latent.size * space
    changes = jnp.sqrt(total[0, :1] / cell_count)
    return (states[None], changes)


def solution(mesh):
    in_specs = (
        P("step", None, None, "space"),
        P("step", None, None, "space"),
        P("step", None),
        P(),
        P(),
        P(),
    )
    out_specs = (P("step", None, None, "space"), P("step"))
    return jax.shard_map(local, mesh=mesh, in_specs=in_specs, out_specs=out_specs, check_vma=False)
```

```python
import functools
import math

import jax
import jax.numpy as jnp
from jax import lax
from jax.experimental import pallas as pl
from jax.experimental.pallas import tpu as pltpu
from jax.sharding import PartitionSpec as P

C = 64
COLS = 80
SUB = 8
NT = (((1,), (1,)), ((), ()))
MEGA = 2**20


def plan(timestep):
    scaled = timestep.astype(jnp.float32) / 1000.0
    return -(0.1 * scaled + 9.95 * scaled * scaled)


def coefficients(timestep_pair):
    log_from = plan(timestep_pair[0])
    log_to = plan(timestep_pair[1])
    half_gap = 0.5 * (log_to - log_from)
    decay_gain = jnp.expm1(half_gap)
    remain_from = -jnp.expm1(log_from)
    remain_to = -jnp.expm1(log_to)
    ratio_term = -jnp.expm1(log_from - log_to)
    noise_gain = -jnp.exp(half_gap) * jnp.sqrt(remain_from) + remain_to * jnp.exp(
        -half_gap
    ) / jnp.sqrt(remain_from)
    spread_gain = jnp.sqrt(remain_to / remain_from * ratio_term)
    return (decay_gain, noise_gain, spread_gain)


def time_embed(timestep, time_weight):
    half_count = C // 2
    frequency = jnp.exp(-math.log(10000.0) * jnp.arange(half_count, dtype=jnp.float32) / half_count)
    angles = timestep.astype(jnp.float32) * frequency
    features = jnp.concatenate([jnp.sin(angles), jnp.cos(angles)])
    return jnp.dot(
        features, time_weight, preferred_element_type=jnp.float32, precision=lax.Precision.HIGHEST
    )


class Frames:
    def __init__(self, odd, parity):
        self.odd, self.parity = odd, parity

    def pick(self, ref, v):
        count = ref.shape[1]
        return jnp.where(self.odd, ref[:, v, :], ref[:, count - 1 - v, :])

    def slot(self, v):
        return jnp.where(self.parity == 1, v % 2, (v + 1) % 2)

    def load(self, ref, v):
        tiles = C // SUB
        return ref[pl.ds(self.slot(v) * tiles, tiles)].reshape(C, ref.shape[2])

    def store(self, ref, v, value):
        tiles = C // SUB
        ref[pl.ds(self.slot(v) * tiles, tiles)] = value.reshape(tiles, SUB, ref.shape[2])

    def tap(self, a):
        return jnp.where(self.parity == 1, a, 2 - a)


def entering_of(frames, flags, guesses, halves, v):
    start = frames.pick(guesses, v)
    if halves is None:
        return start
    other, keep = halves
    return jnp.where(flags.anchor, start, frames.load(other if v < 2 else keep, v))


class Flags:
    def __init__(self, real=None):
        step, block = lax.axis_index("step"), lax.axis_index("space")
        self.parity = lax.rem(step, 2)
        self.odd = self.parity == 1
        self.even_block = lax.rem(block, 2) == 0
        self.anchor = step == 0
        if real is not None:
            self.keep, self.gain, self.spread = (real[i : i + 1, 0:1] for i in range(3))
        self.top, self.bottom = block == 0, block == lax.axis_size("space") - 1


def halo_slot(frames, v):
    return (0 if v < 2 else 2) + frames.slot(v)


def edges_kernel(later, *refs):
    flags = Flags()
    frames = Frames(flags.odd, flags.parity)
    edge = 2 * COLS
    if later:
        guesses, other, keep, inner, outer = refs
        count, length = guesses.shape[1:]
    else:
        low, high, inner, outer = refs
        count, wide = low.shape[1:]
    for v in range(count):
        if later:
            latent = entering_of(frames, flags, guesses, (other, keep), v)
            head, tail = latent[:, :edge], latent[:, length - edge :]
        else:
            head = frames.pick(low, v)[:, :edge]
            tail = frames.pick(high, v)[:, wide - edge :]
        head, tail = head.astype(jnp.bfloat16), tail.astype(jnp.bfloat16)
        at = halo_slot(frames, v)
        inner[at] = jnp.where(flags.even_block, tail, head)
        outer[at] = jnp.where(flags.even_block, head, tail)


def near_frames(v, count):
    return [a for a in range(3) if 0 <= v + a - 1 < count]


def spread_columns(values):
    n = values.shape[1]
    column = lax.broadcasted_iota(jnp.int32, (1, n), 1) % COLS
    before = jnp.where(column >= 1, pltpu.roll(values, 1, 1), 0.0).astype(jnp.bfloat16)
    after = jnp.where(column <= COLS - 2, pltpu.roll(values, n - 1, 1), 0.0).astype(jnp.bfloat16)
    center = values.astype(jnp.bfloat16)
    pairs = ((before, center), (after, before), (center, after))
    return [jnp.concatenate(pair, axis=0).T for pair in pairs]


def first_weights(frames, first, v, count):
    return jnp.concatenate([first[frames.tap(a)] for a in near_frames(v, count)], axis=0)


WINDOWS = ((0, 0, 256), (1, 256, 384), (2, 0, 256))


def silu(value):
    return value / (1.0 + jnp.exp(-value))


def interior_kernel(later, guesses, *refs):
    flags = Flags()
    frames = Frames(flags.odd, flags.parity)
    halves, refs = split(later, refs)
    first, temb, hidden, own, spread = refs
    count, length = guesses.shape[1:]
    edge = 2 * COLS
    inside = length - edge

    def prepare(v):
        left, mixed, right = spread_columns(entering_of(frames, flags, guesses, halves, v))
        spread[v, :, 0:128] = left
        spread[v, :, 128:192] = mixed[:, :64]
        spread[v, pl.ds(0, length - COLS), 192:256] = mixed[COLS:, 64:]
        spread[v, pl.ds(length - COLS, COLS), 192:256] = jnp.zeros((COLS, 64), jnp.bfloat16)
        spread[v, :, 256:384] = right

    prepare(0)
    prepare(1)
    for v in range(count):
        if v + 2 < count:
            prepare(v + 2)
        cells = jnp.concatenate(
            [
                spread[v + a - 1, pl.ds(b * COLS, inside), low:high]
                for a in near_frames(v, count)
                for b, low, high in WINDOWS
            ],
            axis=1,
        )
        value = jnp.dot(cells, first_weights(frames, first, v, count), preferred_element_type=jnp.float32)
        hidden[v] = silu(value + temb[...]).astype(jnp.bfloat16)
        own[v, pl.ds(0, edge), :] = spread[v, pl.ds(0, edge), :]
        own[v, pl.ds(edge, edge), :] = spread[v, pl.ds(inside, edge), :]


class Rest:
    def __init__(self, real, guesses, halves, noise, first, second, temb, inside, ends):
        self.flags = Flags(real)
        self.frames = Frames(self.flags.odd, self.flags.parity)
        self.guesses, self.halves, self.noise = guesses, halves, noise
        self.first, self.second, self.temb, self.inside, self.ends = first, second, temb, inside, ends
        self.channels, self.count, self.length = guesses.shape

    def entering(self, v):
        return entering_of(self.frames, self.flags, self.guesses, self.halves, v)

    def prepare(self, v, inner, outer, own, spread):
        edge = 2 * COLS
        at = halo_slot(self.frames, v)
        near, far = inner[at].astype(jnp.float32), outer[at].astype(jnp.float32)
        even = self.flags.even_block
        both = jnp.concatenate([jnp.where(even, far, near), jnp.where(even, near, far)], axis=1)
        left, mixed, right = spread_columns(both)
        spread[v, pl.ds(edge, 2 * edge), :] = own[v]
        for low, high, rows in ((0, 128, left), (128, 192, mixed[:, :64]), (256, 384, right)):
            spread[v, pl.ds(0, edge), low:high] = rows[:edge]
            spread[v, pl.ds(3 * edge, edge), low:high] = rows[edge:]
        spread[v, pl.ds(0, COLS), 192:256] = mixed[COLS:edge, 64:]
        spread[v, pl.ds(COLS, COLS), 192:256] = own[v, pl.ds(0, COLS), 0:64]
        spread[v, pl.ds(3 * edge - COLS, edge), 192:256] = mixed[edge:, 64:]
        spread[v, pl.ds(3 * edge + COLS, COLS), 192:256] = jnp.zeros((COLS, 64), jnp.bfloat16)

    def edge_rows(self, v, spread):
        edge = 2 * COLS
        top, bottom = self.flags.top, self.flags.bottom
        rows = []
        for group in (0, 2 * edge):
            rows.append(
                jnp.concatenate(
                    [
                        spread[v + a - 1, pl.ds(group + b * COLS, edge), low:high]
                        for a in near_frames(v, self.count)
                        for b, low, high in WINDOWS
                    ],
                    axis=1,
                )
            )
        weights = first_weights(self.frames, self.first, v, self.count)
        value = jnp.dot(jnp.concatenate(rows, axis=0), weights, preferred_element_type=jnp.float32)
        active = silu(value + self.temb[...])
        place = lax.broadcasted_iota(jnp.int32, (2 * edge, 1), 0)
        outside = jnp.logical_or(
            jnp.logical_and(place < COLS, top), jnp.logical_and(place >= 2 * edge - COLS, bottom)
        )
        ref, i = self.ends[v]
        ref[i] = jnp.where(outside, 0.0, active).astype(jnp.bfloat16)

    def second_conv(self, v, out):
        channels, length, flags = self.channels, self.length, self.flags
        width = self.temb.shape[1]
        edge = 2 * COLS
        taps = [(a, b) for a in near_frames(v, self.count) for b in range(3)]
        weights = jnp.concatenate(
            [
                jnp.concatenate(
                    [
                        self.second[self.frames.tap(a), :, (b * 3 + e) * width : (b * 3 + e + 1) * width]
                        for e in range(3)
                    ],
                    axis=0,
                )
                for a, b in taps
            ],
            axis=1,
        )
        latent, noise = self.entering(v), self.frames.pick(self.noise, v)
        base = flags.keep * latent + flags.spread * noise + jnp.where(flags.anchor, latent, 0.0)
        chunk = length // 2
        column = lax.broadcasted_iota(jnp.int32, (1, chunk), 1) % COLS
        predicted = []
        for start in range(0, length, chunk):
            cells = []
            for a, b in taps:
                ref, i = self.ends[v + a - 1]
                low, high = start + b * COLS, start + b * COLS + chunk
                rows = []
                if low < edge:
                    rows.append(ref[i, pl.ds(low, edge - low), :])
                at, end = max(low, edge), min(high, length)
                rows.append(self.inside[v + a - 1, pl.ds(at - edge, end - at), :])
                if high > length:
                    rows.append(ref[i, pl.ds(edge, high - length), :])
                cells.append(jnp.concatenate(rows, axis=0))
            cells = jnp.concatenate(cells, axis=1)
            parts = lax.dot_general(cells, weights, NT, preferred_element_type=jnp.float32).T
            before = jnp.where(column >= 1, pltpu.roll(parts[:channels], 1, 1), 0.0)
            after = jnp.where(
                column <= COLS - 2, pltpu.roll(parts[2 * channels : 3 * channels], chunk - 1, 1), 0.0
            )
            predicted.append(before + parts[channels : 2 * channels] + after)
        result = base + flags.gain * jnp.concatenate(predicted, axis=1)
        self.frames.store(out, v, result)
        return jnp.max(jnp.abs(result), axis=0, keepdims=True)

    def mark(self, ref, peaks):
        peak = jnp.max(functools.reduce(jnp.maximum, peaks), axis=1, keepdims=True)
        exponent = jnp.clip(jnp.ceil(jnp.log(peak) * (1.0 / math.log(2.0))) + 1.0, -100.0, 126.0)
        ref[ref.shape[0] - 1] = jnp.broadcast_to(exponent, (SUB, self.length))


def split(later, refs):
    return (tuple(refs[:2]), refs[2:]) if later else (None, refs)


def sending_kernel(later, real, guesses, *refs):
    halves, refs = split(later, refs)
    inner, outer, noise, first, second, temb, inside, own, yours, ends_out, ends_own, spread = refs
    ends = {0: (ends_own, 0), 1: (ends_out, 0), 2: (ends_out, 1), 3: (ends_out, 2)}
    work = Rest(real, guesses, halves, noise, first, second, temb, inside, ends)
    work.prepare(0, inner, outer, own, spread)
    work.prepare(1, inner, outer, own, spread)
    work.edge_rows(0, spread)
    work.prepare(2, inner, outer, own, spread)
    work.edge_rows(1, spread)
    peaks = [work.second_conv(0, yours)]
    work.prepare(3, inner, outer, own, spread)
    work.edge_rows(2, spread)
    peaks.append(work.second_conv(1, yours))
    work.edge_rows(3, spread)
    work.mark(yours, peaks)


def keeping_kernel(later, real, guesses, *refs):
    halves, refs = split(later, refs)
    noise, second, temb, inside, ends_in, mine = refs
    ends = {1: (ends_in, 0), 2: (ends_in, 1), 3: (ends_in, 2)}
    work = Rest(real, guesses, halves, noise, None, second, temb, inside, ends)
    work.mark(mine, [work.second_conv(2, mine), work.second_conv(3, mine)])


WHOLE = pl.BlockSpec(memory_space=pltpu.VMEM)


def call(kernel, name, arrays, out_shape, scratch=(), flops=1_000_000, limit=4):
    return pl.pallas_call(
        kernel,
        out_shape=out_shape,
        in_specs=[WHOLE] * len(arrays),
        out_specs=tuple(WHOLE for _ in out_shape),
        scratch_shapes=list(scratch),
        compiler_params=pltpu.CompilerParams(vmem_limit_bytes=limit * MEGA),
        cost_estimate=pl.CostEstimate(flops=flops, bytes_accessed=4_000_000, transcendentals=100_000),
        name=name,
    )(*arrays)


def edges(guesses, halves):
    channels, frames, length = guesses.shape
    shape = jax.ShapeDtypeStruct((frames, channels, 2 * COLS), jnp.bfloat16)
    kernel = functools.partial(edges_kernel, halves is not None)
    if halves is not None:
        return call(kernel, "edges", (guesses,) + halves, (shape, shape))
    wide = -(-2 * COLS // 128) * 128
    return call(kernel, "edges", (guesses[..., :wide], guesses[..., length - wide :]), (shape, shape))


def denoise(real, guesses, halves, inner, outer, noise, first, second, temb):
    channels, frames, length = guesses.shape
    width = temb.shape[1]
    half = jax.ShapeDtypeStruct((frames // 2 * channels // SUB + 1, SUB, length), jnp.float32)
    later = halves is not None
    start = (guesses,) + (halves or ())
    inside, own = call(
        functools.partial(interior_kernel, later),
        "interior",
        start + (first, temb),
        (
            jax.ShapeDtypeStruct((frames, length - 2 * COLS, width), jnp.bfloat16),
            jax.ShapeDtypeStruct((frames, 4 * COLS, 384), jnp.bfloat16),
        ),
        [pltpu.VMEM((frames, length, 384), jnp.bfloat16)],
        2_000_000_000,
        limit=6,
    )
    ends = (4 * COLS, width)
    yours, ends_mid = call(
        functools.partial(sending_kernel, later),
        "sending",
        (real,) + start + (inner, outer, noise, first, second, temb, inside, own),
        (half, jax.ShapeDtypeStruct((3,) + ends, jnp.bfloat16)),
        [pltpu.VMEM((1,) + ends, jnp.bfloat16), pltpu.VMEM((frames, 8 * COLS, 384), jnp.bfloat16)],
        2_000_000_000,
        limit=6,
    )
    (mine,) = call(
        functools.partial(keeping_kernel, later),
        "keeping",
        (real,) + start + (noise, second, temb, inside, ends_mid),
        (half,),
        flops=2_000_000_000,
        limit=6,
    )
    return yours, mine


def finish_kernel(other, keep, yours, mine, out, states, done):
    flags = Flags()
    channels, count, length = states.shape
    tiles = C // SUB
    group = channels // 4
    copies = []
    for at in range(0, channels, group):
        for frame in range(count):
            low = frame < count // 2
            slabs = pl.ds((frame % 2) * tiles + at // SUB, group // SUB)

            def part(first_ref, second_ref):
                one, two = first_ref[slabs].reshape(group, length), second_ref[slabs].reshape(group, length)
                return jnp.where(flags.odd, one, two) if low else jnp.where(flags.odd, two, one)

            before = jnp.where(flags.anchor, 0.0, part(other, keep))
            states[pl.ds(at, group), frame, :] = before + part(yours, mine)
        place = pl.ds(at, group)
        copies.append(pltpu.make_async_copy(states.at[place], out.at[place], done.at[len(copies)]))
        copies[-1].start()
    for copy in copies:
        copy.wait()


def finish(guesses, *halves):
    return pl.pallas_call(
        finish_kernel,
        out_shape=jax.ShapeDtypeStruct(guesses.shape, jnp.float32),
        in_specs=[WHOLE] * len(halves),
        out_specs=pl.BlockSpec(memory_space=pl.ANY),
        scratch_shapes=[pltpu.VMEM(guesses.shape, jnp.float32), pltpu.SemaphoreType.DMA((4,))],
        compiler_params=pltpu.CompilerParams(vmem_limit_bytes=4 * MEGA),
        cost_estimate=pl.CostEstimate(flops=8_000_000_000, bytes_accessed=4_000_000, transcendentals=0),
        name="finish",
    )(*halves)


def changes_kernel(*refs):
    *sweeps, sums = refs
    tiles = 2 * C // SUB

    def reached(before, term):
        return before[pl.ds(0, tiles)] + term[pl.ds(0, tiles)]

    for i, at in enumerate((0, 2)):
        change = reached(sweeps[4 + at], sweeps[5 + at]) - reached(sweeps[at], sweeps[1 + at])
        square = jnp.sum(change * change, axis=0)
        total = jnp.sum(jnp.sum(square, axis=0, keepdims=True), axis=1, keepdims=True)
        sums[i] = jnp.broadcast_to(total, sums.shape[1:])


def change_sums(one, two):
    shape = jax.ShapeDtypeStruct((2, SUB, 128), jnp.float32)
    (sums,) = call(changes_kernel, "changes", one + two, (shape,))
    return sums


def is_mark(half):
    return lax.broadcasted_iota(jnp.int32, half.shape, 0) == half.shape[0] - 1


def coded(half):
    exponent = half[-1:]
    return jnp.where(is_mark(half), half, half * jnp.exp2(14.0 - exponent)).astype(jnp.float16)


def decoded(message):
    half = message.astype(jnp.float32)
    return jnp.where(is_mark(half), half, half * jnp.exp2(half[-1:] - 14.0))


def added(one, two):
    return jnp.where(is_mark(one), jnp.maximum(one, two) + 1.0, one + two)


def masked(half, condition):
    return jnp.where(condition, half, jnp.where(is_mark(half), -100.0, 0.0))


def exchange(half, distance):
    steps = lax.axis_size("step")
    return decoded(lax.ppermute(coded(half), "step", [(i, i ^ distance) for i in range(steps)]))


def prefix(yours, mine, step_index):
    steps = lax.axis_size("step")
    odd = step_index % 2 == 1
    partner = exchange(yours, 1)
    total = added(mine, partner)
    before = masked(total, False)
    distance = 2
    while distance < steps:
        got = exchange(total, distance)
        before = added(before, masked(got, (step_index // distance) % 2 == 1))
        total = added(total, got)
        distance *= 2
    keep = added(before, masked(partner, odd))
    give = added(before, masked(mine, jnp.logical_not(odd)))
    return exchange(give, 1), keep, (keep, mine, give, partner)


def local(guesses, noise, timesteps, conv_first, conv_second, time_weight):
    step_index = lax.axis_index("step")
    row_block = lax.axis_index("space")
    space = lax.axis_size("space")
    start_latent = guesses[0]
    noise_step = noise[0]
    timestep_pair = timesteps[0]
    inner_pairs = [pair for i in range(0, space - 1, 2) for pair in ((i, i + 1), (i + 1, i))]
    outer_pairs = [pair for i in range(1, space - 1, 2) for pair in ((i, i + 1), (i + 1, i))]

    pair = lax.optimization_barrier(jnp.broadcast_to(timestep_pair[:, None], (2, 128)))
    real = jnp.stack(coefficients(pair))
    temb = time_embed(pair[0, : C // 2], time_weight).reshape(1, -1)
    first = jnp.pad(conv_first.transpose(0, 2, 1), ((0, 0), (0, C), (0, 0)))

    def sweep(halves):
        near, far = edges(start_latent, halves)
        inner = lax.ppermute(near, "space", inner_pairs)
        outer = lax.ppermute(far, "space", outer_pairs)
        yours, mine = denoise(
            real, start_latent, halves, inner, outer, noise_step, first, conv_second, temb
        )
        return yours, mine, prefix(yours, mine, step_index)

    _, _, (other1, keep1, reached1) = sweep(None)
    yours2, mine2, (other2, keep2, reached2) = sweep((other1, keep1))
    sums = change_sums(reached1, reached2)
    steps = lax.axis_size("step")
    cell_count = start_latent.size * space
    distance = 1
    while 2 * distance < space:
        sums = sums + lax.ppermute(sums, "space", [(i, i ^ distance) for i in range(space)])
        distance *= 2
    swap = [(k * space + s, (k ^ 1) * space + s) for k in range(steps) for s in range(space)]
    cross = [(k * space + s, (k ^ 1) * space + (s ^ distance)) for k in range(steps) for s in range(space)]
    far = [(i, i ^ distance) for i in range(space)]
    near_sum, other2 = lax.optimization_barrier((sums[0], other2))
    if space == 1:
        others = (lax.ppermute(sums[1], ("step", "space"), swap),)
    else:
        others = (
            lax.ppermute(sums[1], ("step", "space"), swap),
            lax.ppermute(sums[1], ("step", "space"), cross),
            lax.ppermute(near_sum, "space", far),
        )
    states = finish(start_latent, other2, keep2, yours2, mine2)
    total = functools.reduce(jnp.add, others, sums[0])
    changes = lax.optimization_barrier(jnp.sqrt(total / cell_count))[0, :1]
    return (states[None], changes)


def solution(mesh):
    in_specs = (
        P("step", None, None, "space"),
        P("step", None, None, "space"),
        P("step", None),
        P(),
        P(),
        P(),
    )
    out_specs = (P("step", None, None, "space"), P("step"))
    return jax.shard_map(local, mesh=mesh, in_specs=in_specs, out_specs=out_specs, check_vma=False)
```

```python
import functools
import math

import jax
import jax.numpy as jnp
from jax import lax
from jax.experimental import pallas as pl
from jax.experimental.pallas import tpu as pltpu
from jax.sharding import PartitionSpec as P

C = 64
COLS = 80
SUB = 8
NT = (((1,), (1,)), ((), ()))
MEGA = 2**20


def plan(timestep):
    scaled = timestep.astype(jnp.float32) / 1000.0
    return -(0.1 * scaled + 9.95 * scaled * scaled)


def coefficients(timestep_pair):
    log_from = plan(timestep_pair[0])
    log_to = plan(timestep_pair[1])
    half_gap = 0.5 * (log_to - log_from)
    decay_gain = jnp.expm1(half_gap)
    remain_from = -jnp.expm1(log_from)
    remain_to = -jnp.expm1(log_to)
    ratio_term = -jnp.expm1(log_from - log_to)
    noise_gain = -jnp.exp(half_gap) * jnp.sqrt(remain_from) + remain_to * jnp.exp(
        -half_gap
    ) / jnp.sqrt(remain_from)
    spread_gain = jnp.sqrt(remain_to / remain_from * ratio_term)
    return (decay_gain, noise_gain, spread_gain)


def time_embed(timestep, time_weight):
    half_count = C // 2
    frequency = jnp.exp(-math.log(10000.0) * jnp.arange(half_count, dtype=jnp.float32) / half_count)
    angles = timestep.astype(jnp.float32) * frequency
    features = jnp.concatenate([jnp.sin(angles), jnp.cos(angles)])
    return jnp.dot(
        features, time_weight, preferred_element_type=jnp.float32, precision=lax.Precision.HIGHEST
    )


class Frames:
    def __init__(self, parity):
        self.parity = parity

    def slot(self, v):
        return jnp.where(self.parity == 1, v % 2, (v + 1) % 2)

    def load(self, halves, v):
        tiles = C // SUB
        ref = halves[0] if v < 2 else halves[1]
        return ref[pl.ds(self.slot(v) * tiles, tiles)].reshape(C, ref.shape[2])

    def store(self, ref, v, value):
        tiles = C // SUB
        ref[pl.ds(self.slot(v) * tiles, tiles)] = value.reshape(tiles, SUB, ref.shape[2])

    def tap(self, a):
        return jnp.where(self.parity == 1, a, 2 - a)


class Flags:
    def __init__(self, real=None):
        step, block = lax.axis_index("step"), lax.axis_index("space")
        self.parity = lax.rem(step, 2)
        self.odd = self.parity == 1
        self.even_block = lax.rem(block, 2) == 0
        self.anchor = step == 0
        if real is not None:
            self.keep, self.gain, self.spread = (real[i : i + 1, 0:1] for i in range(3))
        self.top, self.bottom = block == 0, block == lax.axis_size("space") - 1


def halo_slot(frames, v):
    return (0 if v < 2 else 2) + frames.slot(v)


def ends_of(flags, frames, halves, inner, outer):
    edge = 2 * COLS
    for half, ref in enumerate(halves):
        length = ref.shape[2]
        for slot in range(2):
            slabs = pl.ds(slot * (C // SUB), C // SUB)
            head = ref[slabs, :, 0:edge].reshape(C, edge).astype(jnp.bfloat16)
            tail = ref[slabs, :, length - edge : length].reshape(C, edge).astype(jnp.bfloat16)
            inner[2 * half + slot] = jnp.where(flags.even_block, tail, head)
            outer[2 * half + slot] = jnp.where(flags.even_block, head, tail)


def edges_kernel(other, keep, inner, outer):
    flags = Flags()
    ends_of(flags, Frames(flags.parity), (other, keep), inner, outer)


def arrange_kernel(with_ends, values, other, keep, *ends):
    flags = Flags()
    channels, count, length = values.shape
    tiles = channels // SUB
    for slot in range(count // 2):
        low = values[:, slot, :].reshape(tiles, SUB, length)
        high = values[:, count // 2 + slot, :].reshape(tiles, SUB, length)
        slabs = pl.ds(slot * tiles, tiles)
        other[slabs] = jnp.where(flags.odd, low, high)
        keep[slabs] = jnp.where(flags.odd, high, low)
    for ref in (other, keep):
        ref[ref.shape[0] - 1] = jnp.zeros((SUB, length), jnp.float32)
    if with_ends:
        ends_of(flags, Frames(flags.parity), (other, keep), *ends)


def near_frames(v, count):
    return [a for a in range(3) if 0 <= v + a - 1 < count]


def spread_columns(values):
    n = values.shape[1]
    column = lax.broadcasted_iota(jnp.int32, (1, n), 1) % COLS
    before = jnp.where(column >= 1, pltpu.roll(values, 1, 1), 0.0).astype(jnp.bfloat16)
    after = jnp.where(column <= COLS - 2, pltpu.roll(values, n - 1, 1), 0.0).astype(jnp.bfloat16)
    center = values.astype(jnp.bfloat16)
    pairs = ((before, center), (after, before), (center, after))
    return [jnp.concatenate(pair, axis=0).T for pair in pairs]


def first_weights(frames, first, v, count):
    return jnp.concatenate([first[frames.tap(a)] for a in near_frames(v, count)], axis=0)


WINDOWS = ((0, 0, 256), (1, 256, 384), (2, 0, 256))


def silu(value):
    return value / (1.0 + jnp.exp(-value))


def interior_kernel(other, keep, first, temb, hidden, own, spread):
    flags = Flags()
    frames = Frames(flags.parity)
    count, length = spread.shape[:2]
    edge = 2 * COLS
    inside = length - edge

    def prepare(v):
        left, mixed, right = spread_columns(frames.load((other, keep), v))
        spread[v, :, 0:128] = left
        spread[v, :, 128:192] = mixed[:, :64]
        spread[v, pl.ds(0, length - COLS), 192:256] = mixed[COLS:, 64:]
        spread[v, pl.ds(length - COLS, COLS), 192:256] = jnp.zeros((COLS, 64), jnp.bfloat16)
        spread[v, :, 256:384] = right

    prepare(0)
    prepare(1)
    for v in range(count):
        if v + 2 < count:
            prepare(v + 2)
        cells = jnp.concatenate(
            [
                spread[v + a - 1, pl.ds(b * COLS, inside), low:high]
                for a in near_frames(v, count)
                for b, low, high in WINDOWS
            ],
            axis=1,
        )
        value = jnp.dot(cells, first_weights(frames, first, v, count), preferred_element_type=jnp.float32)
        hidden[v] = silu(value + temb[...]).astype(jnp.bfloat16)
        own[v, pl.ds(0, edge), :] = spread[v, pl.ds(0, edge), :]
        own[v, pl.ds(edge, edge), :] = spread[v, pl.ds(inside, edge), :]


class Rest:
    def __init__(self, real, halves, noise, first, second, temb, inside, ends):
        self.flags = Flags(real)
        self.frames = Frames(self.flags.parity)
        self.halves, self.noise = halves, noise
        self.first, self.second, self.temb, self.inside, self.ends = first, second, temb, inside, ends
        self.channels, self.count, self.length = C, inside.shape[0], halves[0].shape[2]

    def prepare(self, v, inner, outer, own, spread):
        edge = 2 * COLS
        at = halo_slot(self.frames, v)
        near, far = inner[at].astype(jnp.float32), outer[at].astype(jnp.float32)
        even = self.flags.even_block
        both = jnp.concatenate([jnp.where(even, far, near), jnp.where(even, near, far)], axis=1)
        left, mixed, right = spread_columns(both)
        ref, i = spread[v]
        ref[i, pl.ds(edge, 2 * edge), :] = own[v]
        for low, high, rows in ((0, 128, left), (128, 192, mixed[:, :64]), (256, 384, right)):
            ref[i, pl.ds(0, edge), low:high] = rows[:edge]
            ref[i, pl.ds(3 * edge, edge), low:high] = rows[edge:]
        ref[i, pl.ds(0, COLS), 192:256] = mixed[COLS:edge, 64:]
        ref[i, pl.ds(COLS, COLS), 192:256] = own[v, pl.ds(0, COLS), 0:64]
        ref[i, pl.ds(3 * edge - COLS, edge), 192:256] = mixed[edge:, 64:]
        ref[i, pl.ds(3 * edge + COLS, COLS), 192:256] = jnp.zeros((COLS, 64), jnp.bfloat16)

    def edge_rows(self, v, spread):
        edge = 2 * COLS
        top, bottom = self.flags.top, self.flags.bottom
        rows = []
        for group in (0, 2 * edge):
            rows.append(
                jnp.concatenate(
                    [
                        spread[v + a - 1][0][spread[v + a - 1][1], pl.ds(group + b * COLS, edge), low:high]
                        for a in near_frames(v, self.count)
                        for b, low, high in WINDOWS
                    ],
                    axis=1,
                )
            )
        weights = first_weights(self.frames, self.first, v, self.count)
        value = jnp.dot(jnp.concatenate(rows, axis=0), weights, preferred_element_type=jnp.float32)
        active = silu(value + self.temb[...])
        place = lax.broadcasted_iota(jnp.int32, (2 * edge, 1), 0)
        outside = jnp.logical_or(
            jnp.logical_and(place < COLS, top), jnp.logical_and(place >= 2 * edge - COLS, bottom)
        )
        ref, i = self.ends[v]
        ref[i] = jnp.where(outside, 0.0, active).astype(jnp.bfloat16)

    def second_conv(self, v, out):
        channels, length, flags = self.channels, self.length, self.flags
        width = self.temb.shape[1]
        edge = 2 * COLS
        taps = [(a, b) for a in near_frames(v, self.count) for b in range(3)]
        weights = jnp.concatenate(
            [
                jnp.concatenate(
                    [
                        self.second[self.frames.tap(a), :, (b * 3 + e) * width : (b * 3 + e + 1) * width]
                        for e in range(3)
                    ],
                    axis=0,
                )
                for a, b in taps
            ],
            axis=1,
        )
        latent, noise = self.frames.load(self.halves, v), self.frames.load(self.noise, v)
        base = flags.keep * latent + flags.spread * noise + jnp.where(flags.anchor, latent, 0.0)
        chunk = length // 2
        column = lax.broadcasted_iota(jnp.int32, (1, chunk), 1) % COLS
        predicted = []
        for start in range(0, length, chunk):
            cells = []
            for a, b in taps:
                ref, i = self.ends[v + a - 1]
                low, high = start + b * COLS, start + b * COLS + chunk
                rows = []
                if low < edge:
                    rows.append(ref[i, pl.ds(low, edge - low), :])
                at, end = max(low, edge), min(high, length)
                rows.append(self.inside[v + a - 1, pl.ds(at - edge, end - at), :])
                if high > length:
                    rows.append(ref[i, pl.ds(edge, high - length), :])
                cells.append(jnp.concatenate(rows, axis=0))
            cells = jnp.concatenate(cells, axis=1)
            parts = lax.dot_general(cells, weights, NT, preferred_element_type=jnp.float32).T
            before = jnp.where(column >= 1, pltpu.roll(parts[:channels], 1, 1), 0.0)
            after = jnp.where(
                column <= COLS - 2, pltpu.roll(parts[2 * channels : 3 * channels], chunk - 1, 1), 0.0
            )
            predicted.append(before + parts[channels : 2 * channels] + after)
        result = base + flags.gain * jnp.concatenate(predicted, axis=1)
        self.frames.store(out, v, result)
        return jnp.max(jnp.abs(result), axis=0, keepdims=True)

    def mark(self, ref, peaks):
        peak = jnp.max(functools.reduce(jnp.maximum, peaks), axis=1, keepdims=True)
        exponent = jnp.clip(jnp.ceil(jnp.log(peak) * (1.0 / math.log(2.0))) + 1.0, -100.0, 126.0)
        ref[ref.shape[0] - 1] = jnp.broadcast_to(exponent, (SUB, self.length))


def sending_kernel(real, other, keep, noise_other, inner, outer, first, second, temb, inside, own, yours, *rest):
    ends_out, spread_out, ends_own, spread_own = rest
    ends = {0: (ends_own, 0), 1: (ends_out, 0), 2: (ends_out, 1)}
    spread = {0: (spread_own, 0), 1: (spread_own, 1), 2: (spread_out, 0), 3: (spread_out, 1)}
    work = Rest(real, (other, keep), (noise_other, None), first, second, temb, inside, ends)
    work.prepare(0, inner, outer, own, spread)
    work.prepare(1, inner, outer, own, spread)
    work.edge_rows(0, spread)
    work.prepare(2, inner, outer, own, spread)
    work.edge_rows(1, spread)
    work.prepare(3, inner, outer, own, spread)
    peaks = [work.second_conv(0, yours)]
    work.edge_rows(2, spread)
    peaks.append(work.second_conv(1, yours))
    work.mark(yours, peaks)


def keeping_kernel(real, keep, noise_keep, first, second, temb, inside, ends_in, spread_in, mine, ends_own):
    ends = {1: (ends_in, 0), 2: (ends_in, 1), 3: (ends_own, 0)}
    work = Rest(real, (keep, keep), (None, noise_keep), first, second, temb, inside, ends)
    work.edge_rows(3, {2: (spread_in, 0), 3: (spread_in, 1)})
    work.mark(mine, [work.second_conv(2, mine), work.second_conv(3, mine)])


WHOLE = pl.BlockSpec(memory_space=pltpu.VMEM)


def call(kernel, name, arrays, out_shape, scratch=(), flops=1_000_000, limit=4):
    return pl.pallas_call(
        kernel,
        out_shape=out_shape,
        in_specs=[WHOLE] * len(arrays),
        out_specs=tuple(WHOLE for _ in out_shape),
        scratch_shapes=list(scratch),
        compiler_params=pltpu.CompilerParams(vmem_limit_bytes=limit * MEGA),
        cost_estimate=pl.CostEstimate(flops=flops, bytes_accessed=4_000_000, transcendentals=100_000),
        name=name,
    )(*arrays)


def edges(other, keep):
    shape = jax.ShapeDtypeStruct((2 * other.shape[0] // (C // SUB), C, 2 * COLS), jnp.bfloat16)
    return call(edges_kernel, "edges", (other, keep), (shape, shape))


def arrange(values, with_ends):
    channels, frames, length = values.shape
    half = jax.ShapeDtypeStruct((frames // 2 * channels // SUB + 1, SUB, length), jnp.float32)
    ends = jax.ShapeDtypeStruct((frames, channels, 2 * COLS), jnp.bfloat16)
    shapes = (half, half) + ((ends, ends) if with_ends else ())
    return call(functools.partial(arrange_kernel, with_ends), "arrange", (values,), shapes)


def denoise(real, other, keep, noise, inner, outer, first, second, temb):
    length = other.shape[2]
    frames = inner.shape[0]
    width = temb.shape[1]
    half = jax.ShapeDtypeStruct(other.shape, jnp.float32)
    inside, own = call(
        interior_kernel,
        "interior",
        (other, keep, first, temb),
        (
            jax.ShapeDtypeStruct((frames, length - 2 * COLS, width), jnp.bfloat16),
            jax.ShapeDtypeStruct((frames, 4 * COLS, 384), jnp.bfloat16),
        ),
        [pltpu.VMEM((frames, length, 384), jnp.bfloat16)],
        2_000_000_000,
        limit=6,
    )
    ends = (4 * COLS, width)
    spread = (2, 8 * COLS, 384)
    yours, ends_mid, spread_mid = call(
        sending_kernel,
        "sending",
        (real, other, keep, noise[0], inner, outer, first, second, temb, inside, own),
        (half, jax.ShapeDtypeStruct((2,) + ends, jnp.bfloat16), jax.ShapeDtypeStruct(spread, jnp.bfloat16)),
        [pltpu.VMEM((1,) + ends, jnp.bfloat16), pltpu.VMEM(spread, jnp.bfloat16)],
        2_000_000_000,
        limit=6,
    )
    (mine,) = call(
        keeping_kernel,
        "keeping",
        (real, keep, noise[1], first, second, temb, inside, ends_mid, spread_mid),
        (half,),
        [pltpu.VMEM((1,) + ends, jnp.bfloat16)],
        2_000_000_000,
        limit=6,
    )
    return yours, mine


def finish_kernel(other, keep, yours, mine, out, states, done):
    flags = Flags()
    channels, count, length = states.shape
    tiles = C // SUB
    group = channels // 4
    copies = []
    for at in range(0, channels, group):
        for frame in range(count):
            low = frame < count // 2
            slabs = pl.ds((frame % 2) * tiles + at // SUB, group // SUB)

            def part(first_ref, second_ref):
                one, two = first_ref[slabs].reshape(group, length), second_ref[slabs].reshape(group, length)
                return jnp.where(flags.odd, one, two) if low else jnp.where(flags.odd, two, one)

            before = jnp.where(flags.anchor, 0.0, part(other, keep))
            states[pl.ds(at, group), frame, :] = before + part(yours, mine)
        place = pl.ds(at, group)
        copies.append(pltpu.make_async_copy(states.at[place], out.at[place], done.at[len(copies)]))
        copies[-1].start()
    for copy in copies:
        copy.wait()


def finish(guesses, *halves):
    return pl.pallas_call(
        finish_kernel,
        out_shape=jax.ShapeDtypeStruct(guesses.shape, jnp.float32),
        in_specs=[WHOLE] * len(halves),
        out_specs=pl.BlockSpec(memory_space=pl.ANY),
        scratch_shapes=[pltpu.VMEM(guesses.shape, jnp.float32), pltpu.SemaphoreType.DMA((4,))],
        compiler_params=pltpu.CompilerParams(vmem_limit_bytes=4 * MEGA),
        cost_estimate=pl.CostEstimate(flops=8_000_000_000, bytes_accessed=4_000_000, transcendentals=0),
        name="finish",
    )(*halves)


def changes_kernel(own1, theirs1, own2, theirs2, sums):
    slabs = pl.ds(0, 2 * C // SUB)
    for i, (one, two) in enumerate(((own1, own2), (theirs1, theirs2))):
        change = two[slabs] - one[slabs]
        square = jnp.sum(change * change, axis=0)
        total = jnp.sum(jnp.sum(square, axis=0, keepdims=True), axis=1, keepdims=True)
        sums[i] = jnp.broadcast_to(total, sums.shape[1:])


def change_sums(one, two):
    shape = jax.ShapeDtypeStruct((2, SUB, 128), jnp.float32)
    (sums,) = call(changes_kernel, "changes", one + two, (shape,))
    return sums


def is_mark(half):
    return lax.broadcasted_iota(jnp.int32, half.shape, 0) == half.shape[0] - 1


def coded(half):
    exponent = half[-1:]
    return jnp.where(is_mark(half), half, half * jnp.exp2(14.0 - exponent)).astype(jnp.float16)


def decoded(message):
    half = message.astype(jnp.float32)
    return jnp.where(is_mark(half), half, half * jnp.exp2(half[-1:] - 14.0))


def added(one, two):
    return jnp.where(is_mark(one), jnp.maximum(one, two) + 1.0, one + two)


def masked(half, condition):
    return jnp.where(condition, half, jnp.where(is_mark(half), -100.0, 0.0))


def exchange(half, flip):
    steps = lax.axis_size("step")
    return decoded(lax.ppermute(coded(half), "step", [(i, i ^ flip) for i in range(steps)]))


def prefix(yours, mine, step_index):
    steps = lax.axis_size("step")
    odd = step_index % 2 == 1
    partner = exchange(yours, 1)
    total = added(mine, partner)
    before = masked(total, False)
    distance = 2
    while distance < steps:
        got = exchange(total, 2 * distance - 2)
        before = added(before, masked(got, (step_index // distance) % 2 == 1))
        total = added(total, got)
        distance *= 2
    keep = added(before, masked(partner, odd))
    give = added(before, masked(mine, jnp.logical_not(odd)))
    return exchange(give, 1), keep, (keep + mine, give + partner)


def local(guesses, noise, timesteps, conv_first, conv_second, time_weight):
    step_index = lax.axis_index("step")
    row_block = lax.axis_index("space")
    space = lax.axis_size("space")
    start_latent = guesses[0]
    noise_step = noise[0]
    timestep_pair = timesteps[0]
    inner_pairs = [pair for i in range(0, space - 1, 2) for pair in ((i, i + 1), (i + 1, i))]
    outer_pairs = [pair for i in range(1, space - 1, 2) for pair in ((i, i + 1), (i + 1, i))]

    pair = lax.optimization_barrier(jnp.broadcast_to(timestep_pair[:, None], (2, 128)))
    real = jnp.stack(coefficients(pair))
    temb = time_embed(pair[0, : C // 2], time_weight).reshape(1, -1)
    first = jnp.pad(conv_first.transpose(0, 2, 1), ((0, 0), (0, C), (0, 0)))

    def sweep(other, keep, near, far):
        inner = lax.ppermute(near, "space", inner_pairs)
        outer = lax.ppermute(far, "space", outer_pairs)
        yours, mine = denoise(real, other, keep, noise_halves, inner, outer, first, conv_second, temb)
        return yours, mine, prefix(yours, mine, step_index)

    other0, keep0, near, far = arrange(start_latent, True)
    noise_halves = arrange(noise_step, False)
    _, _, (other1, keep1, reached1) = sweep(other0, keep0, near, far)
    is_anchor = step_index == 0
    other1, keep1 = jnp.where(is_anchor, other0, other1), jnp.where(is_anchor, keep0, keep1)
    yours2, mine2, (other2, keep2, reached2) = sweep(other1, keep1, *edges(other1, keep1))
    sums = change_sums(reached1, reached2)
    steps = lax.axis_size("step")
    cell_count = start_latent.size * space
    distance = 1
    while 2 * distance < space:
        sums = sums + lax.ppermute(sums, "space", [(i, i ^ distance) for i in range(space)])
        distance *= 2
    swap = [(k * space + s, (k ^ 1) * space + s) for k in range(steps) for s in range(space)]
    cross = [(k * space + s, (k ^ 1) * space + (s ^ distance)) for k in range(steps) for s in range(space)]
    far = [(i, i ^ distance) for i in range(space)]
    near_sum, other2 = lax.optimization_barrier((sums[0], other2))
    if space == 1:
        others = (lax.ppermute(sums[1], ("step", "space"), swap),)
    else:
        others = (
            lax.ppermute(sums[1], ("step", "space"), swap),
            lax.ppermute(sums[1], ("step", "space"), cross),
            lax.ppermute(near_sum, "space", far),
        )
    states = finish(start_latent, other2, keep2, yours2, mine2)
    total = functools.reduce(jnp.add, others, sums[0])
    changes = lax.optimization_barrier(jnp.sqrt(total / cell_count))[0, :1]
    return (states[None], changes)


def solution(mesh):
    in_specs = (
        P("step", None, None, "space"),
        P("step", None, None, "space"),
        P("step", None),
        P(),
        P(),
        P(),
    )
    out_specs = (P("step", None, None, "space"), P("step"))
    return jax.shard_map(local, mesh=mesh, in_specs=in_specs, out_specs=out_specs, check_vma=False)
```

```python
import functools
import math

import jax
import jax.numpy as jnp
from jax import lax
from jax.experimental import pallas as pl
from jax.experimental.pallas import tpu as pltpu
from jax.sharding import PartitionSpec as P

C = 64
COLS = 80
SUB = 8
NT = (((1,), (1,)), ((), ()))
MEGA = 2**20


def plan(timestep):
    scaled = timestep.astype(jnp.float32) / 1000.0
    return -(0.1 * scaled + 9.95 * scaled * scaled)


def coefficients(timestep_pair):
    log_from = plan(timestep_pair[0])
    log_to = plan(timestep_pair[1])
    half_gap = 0.5 * (log_to - log_from)
    decay_gain = jnp.expm1(half_gap)
    remain_from = -jnp.expm1(log_from)
    remain_to = -jnp.expm1(log_to)
    ratio_term = -jnp.expm1(log_from - log_to)
    noise_gain = -jnp.exp(half_gap) * jnp.sqrt(remain_from) + remain_to * jnp.exp(
        -half_gap
    ) / jnp.sqrt(remain_from)
    spread_gain = jnp.sqrt(remain_to / remain_from * ratio_term)
    return (decay_gain, noise_gain, spread_gain)


def time_embed(timestep, time_weight):
    half_count = C // 2
    frequency = jnp.exp(-math.log(10000.0) * jnp.arange(half_count, dtype=jnp.float32) / half_count)
    angles = timestep.astype(jnp.float32) * frequency
    features = jnp.concatenate([jnp.sin(angles), jnp.cos(angles)])
    return jnp.dot(
        features, time_weight, preferred_element_type=jnp.float32, precision=lax.Precision.HIGHEST
    )


class Frames:
    def __init__(self, parity):
        self.parity = parity

    def slot(self, v):
        return jnp.where(self.parity == 1, v % 2, (v + 1) % 2)

    def load(self, halves, v):
        tiles = C // SUB
        ref = halves[0] if v < 2 else halves[1]
        return ref[pl.ds(self.slot(v) * tiles, tiles)].reshape(C, ref.shape[2])

    def store(self, ref, v, value):
        tiles = C // SUB
        ref[pl.ds(self.slot(v) * tiles, tiles)] = value.reshape(tiles, SUB, ref.shape[2])

    def tap(self, a):
        return jnp.where(self.parity == 1, a, 2 - a)


class Flags:
    def __init__(self, real=None):
        step, block = lax.axis_index("step"), lax.axis_index("space")
        self.parity = lax.rem(step, 2)
        self.odd = self.parity == 1
        self.even_block = lax.rem(block, 2) == 0
        self.anchor = step == 0
        if real is not None:
            self.keep, self.gain, self.spread = (real[i : i + 1, 0:1] for i in range(3))
        self.top, self.bottom = block == 0, block == lax.axis_size("space") - 1


def halo_slot(frames, v):
    return (0 if v < 2 else 2) + frames.slot(v)


def ends_of(flags, frames, halves, inner, outer):
    edge = 2 * COLS
    for half, ref in enumerate(halves):
        length = ref.shape[2]
        for slot in range(2):
            slabs = pl.ds(slot * (C // SUB), C // SUB)
            head = ref[slabs, :, 0:edge].reshape(C, edge).astype(jnp.bfloat16)
            tail = ref[slabs, :, length - edge : length].reshape(C, edge).astype(jnp.bfloat16)
            inner[2 * half + slot] = jnp.where(flags.even_block, tail, head)
            outer[2 * half + slot] = jnp.where(flags.even_block, head, tail)


def edges_kernel(other, keep, inner, outer):
    flags = Flags()
    ends_of(flags, Frames(flags.parity), (other, keep), inner, outer)


def arrange_kernel(with_ends, values, other, keep, *ends):
    flags = Flags()
    channels, count, length = values.shape
    tiles = channels // SUB
    for slot in range(count // 2):
        low = values[:, slot, :].reshape(tiles, SUB, length)
        high = values[:, count // 2 + slot, :].reshape(tiles, SUB, length)
        slabs = pl.ds(slot * tiles, tiles)
        other[slabs] = jnp.where(flags.odd, low, high)
        keep[slabs] = jnp.where(flags.odd, high, low)
    for ref in (other, keep):
        ref[ref.shape[0] - 1] = jnp.zeros((SUB, length), jnp.float32)
    if with_ends:
        ends_of(flags, Frames(flags.parity), (other, keep), *ends)


def near_frames(v, count):
    return [a for a in range(3) if 0 <= v + a - 1 < count]


def spread_columns(values):
    n = values.shape[1]
    column = lax.broadcasted_iota(jnp.int32, (1, n), 1) % COLS
    before = jnp.where(column >= 1, pltpu.roll(values, 1, 1), 0.0).astype(jnp.bfloat16)
    after = jnp.where(column <= COLS - 2, pltpu.roll(values, n - 1, 1), 0.0).astype(jnp.bfloat16)
    center = values.astype(jnp.bfloat16)
    pairs = ((before, center), (after, before), (center, after))
    return [jnp.concatenate(pair, axis=0).T for pair in pairs]


def first_weights(frames, first, v, count):
    return jnp.concatenate([first[frames.tap(a)] for a in near_frames(v, count)], axis=0)


WINDOWS = ((0, 0, 256), (1, 256, 384), (2, 0, 256))


def silu(value):
    return value / (1.0 + jnp.exp(-value))


def interior_kernel(other, keep, first, temb, hidden, own, spread):
    flags = Flags()
    frames = Frames(flags.parity)
    count, length = spread.shape[:2]
    edge = 2 * COLS
    inside = length - edge

    def prepare(v):
        left, mixed, right = spread_columns(frames.load((other, keep), v))
        spread[v, :, 0:128] = left
        spread[v, :, 128:192] = mixed[:, :64]
        spread[v, pl.ds(0, length - COLS), 192:256] = mixed[COLS:, 64:]
        spread[v, pl.ds(length - COLS, COLS), 192:256] = jnp.zeros((COLS, 64), jnp.bfloat16)
        spread[v, :, 256:384] = right

    prepare(0)
    prepare(1)
    for v in range(count):
        if v + 2 < count:
            prepare(v + 2)
        cells = jnp.concatenate(
            [
                spread[v + a - 1, pl.ds(b * COLS, inside), low:high]
                for a in near_frames(v, count)
                for b, low, high in WINDOWS
            ],
            axis=1,
        )
        value = jnp.dot(cells, first_weights(frames, first, v, count), preferred_element_type=jnp.float32)
        hidden[v] = silu(value + temb[...]).astype(jnp.bfloat16)
        own[v, pl.ds(0, edge), :] = spread[v, pl.ds(0, edge), :]
        own[v, pl.ds(edge, edge), :] = spread[v, pl.ds(inside, edge), :]


class Rest:
    def __init__(self, real, halves, noise, first, second, temb, inside, ends):
        self.flags = Flags(real)
        self.frames = Frames(self.flags.parity)
        self.halves, self.noise = halves, noise
        self.first, self.second, self.temb, self.inside, self.ends = first, second, temb, inside, ends
        self.channels, self.count, self.length = C, inside.shape[0], halves[0].shape[2]

    def prepare(self, v, inner, outer, own, spread):
        edge = 2 * COLS
        at = halo_slot(self.frames, v)
        near, far = inner[at].astype(jnp.float32), outer[at].astype(jnp.float32)
        even = self.flags.even_block
        both = jnp.concatenate([jnp.where(even, far, near), jnp.where(even, near, far)], axis=1)
        left, mixed, right = spread_columns(both)
        ref, i = spread[v]
        ref[i, pl.ds(edge, 2 * edge), :] = own[v]
        for low, high, rows in ((0, 128, left), (128, 192, mixed[:, :64]), (256, 384, right)):
            ref[i, pl.ds(0, edge), low:high] = rows[:edge]
            ref[i, pl.ds(3 * edge, edge), low:high] = rows[edge:]
        ref[i, pl.ds(0, COLS), 192:256] = mixed[COLS:edge, 64:]
        ref[i, pl.ds(COLS, COLS), 192:256] = own[v, pl.ds(0, COLS), 0:64]
        ref[i, pl.ds(3 * edge - COLS, edge), 192:256] = mixed[edge:, 64:]
        ref[i, pl.ds(3 * edge + COLS, COLS), 192:256] = jnp.zeros((COLS, 64), jnp.bfloat16)

    def edge_rows(self, v, spread):
        edge = 2 * COLS
        top, bottom = self.flags.top, self.flags.bottom
        rows = []
        for group in (0, 2 * edge):
            rows.append(
                jnp.concatenate(
                    [
                        spread[v + a - 1][0][spread[v + a - 1][1], pl.ds(group + b * COLS, edge), low:high]
                        for a in near_frames(v, self.count)
                        for b, low, high in WINDOWS
                    ],
                    axis=1,
                )
            )
        weights = first_weights(self.frames, self.first, v, self.count)
        value = jnp.dot(jnp.concatenate(rows, axis=0), weights, preferred_element_type=jnp.float32)
        active = silu(value + self.temb[...])
        place = lax.broadcasted_iota(jnp.int32, (2 * edge, 1), 0)
        outside = jnp.logical_or(
            jnp.logical_and(place < COLS, top), jnp.logical_and(place >= 2 * edge - COLS, bottom)
        )
        ref, i = self.ends[v]
        ref[i] = jnp.where(outside, 0.0, active).astype(jnp.bfloat16)

    def second_conv(self, v, out):
        channels, length, flags = self.channels, self.length, self.flags
        width = self.temb.shape[1]
        edge = 2 * COLS
        taps = [(a, b) for a in near_frames(v, self.count) for b in range(3)]
        weights = jnp.concatenate(
            [
                jnp.concatenate(
                    [
                        self.second[self.frames.tap(a), :, (b * 3 + e) * width : (b * 3 + e + 1) * width]
                        for e in range(3)
                    ],
                    axis=0,
                )
                for a, b in taps
            ],
            axis=1,
        )
        latent, noise = self.frames.load(self.halves, v), self.frames.load(self.noise, v)
        base = flags.keep * latent + flags.spread * noise + jnp.where(flags.anchor, latent, 0.0)
        chunk = length // 2
        column = lax.broadcasted_iota(jnp.int32, (1, chunk), 1) % COLS
        predicted = []
        for start in range(0, length, chunk):
            cells = []
            for a, b in taps:
                ref, i = self.ends[v + a - 1]
                low, high = start + b * COLS, start + b * COLS + chunk
                rows = []
                if low < edge:
                    rows.append(ref[i, pl.ds(low, edge - low), :])
                at, end = max(low, edge), min(high, length)
                rows.append(self.inside[v + a - 1, pl.ds(at - edge, end - at), :])
                if high > length:
                    rows.append(ref[i, pl.ds(edge, high - length), :])
                cells.append(jnp.concatenate(rows, axis=0))
            cells = jnp.concatenate(cells, axis=1)
            parts = lax.dot_general(cells, weights, NT, preferred_element_type=jnp.float32).T
            before = jnp.where(column >= 1, pltpu.roll(parts[:channels], 1, 1), 0.0)
            after = jnp.where(
                column <= COLS - 2, pltpu.roll(parts[2 * channels : 3 * channels], chunk - 1, 1), 0.0
            )
            predicted.append(before + parts[channels : 2 * channels] + after)
        result = base + flags.gain * jnp.concatenate(predicted, axis=1)
        self.frames.store(out, v, result)
        return jnp.max(jnp.abs(result), axis=0, keepdims=True)

    def mark(self, ref, peaks):
        peak = jnp.max(functools.reduce(jnp.maximum, peaks), axis=1, keepdims=True)
        exponent = jnp.clip(jnp.ceil(jnp.log(peak) * (1.0 / math.log(2.0))) + 1.0, -100.0, 126.0)
        ref[ref.shape[0] - 1] = jnp.broadcast_to(exponent, (SUB, self.length))


def sending_kernel(real, other, keep, noise_other, inner, outer, first, second, temb, inside, own, yours, *rest):
    ends_out, spread_out, ends_own, spread_own = rest
    ends = {0: (ends_own, 0), 1: (ends_out, 0), 2: (ends_out, 1)}
    spread = {0: (spread_own, 0), 1: (spread_own, 1), 2: (spread_out, 0), 3: (spread_out, 1)}
    work = Rest(real, (other, keep), (noise_other, None), first, second, temb, inside, ends)
    work.prepare(0, inner, outer, own, spread)
    work.prepare(1, inner, outer, own, spread)
    work.edge_rows(0, spread)
    work.prepare(2, inner, outer, own, spread)
    work.edge_rows(1, spread)
    work.prepare(3, inner, outer, own, spread)
    peaks = [work.second_conv(0, yours)]
    work.edge_rows(2, spread)
    peaks.append(work.second_conv(1, yours))
    work.mark(yours, peaks)


def keeping_kernel(real, keep, noise_keep, first, second, temb, inside, ends_in, spread_in, mine, ends_own):
    ends = {1: (ends_in, 0), 2: (ends_in, 1), 3: (ends_own, 0)}
    work = Rest(real, (keep, keep), (None, noise_keep), first, second, temb, inside, ends)
    work.edge_rows(3, {2: (spread_in, 0), 3: (spread_in, 1)})
    work.mark(mine, [work.second_conv(2, mine), work.second_conv(3, mine)])


WHOLE = pl.BlockSpec(memory_space=pltpu.VMEM)


def call(kernel, name, arrays, out_shape, scratch=(), flops=1_000_000, limit=4):
    return pl.pallas_call(
        kernel,
        out_shape=out_shape,
        in_specs=[WHOLE] * len(arrays),
        out_specs=tuple(WHOLE for _ in out_shape),
        scratch_shapes=list(scratch),
        compiler_params=pltpu.CompilerParams(vmem_limit_bytes=limit * MEGA),
        cost_estimate=pl.CostEstimate(flops=flops, bytes_accessed=4_000_000, transcendentals=100_000),
        name=name,
    )(*arrays)


def edges(other, keep):
    shape = jax.ShapeDtypeStruct((2 * other.shape[0] // (C // SUB), C, 2 * COLS), jnp.bfloat16)
    return call(edges_kernel, "edges", (other, keep), (shape, shape))


def arrange(values, with_ends):
    channels, frames, length = values.shape
    half = jax.ShapeDtypeStruct((frames // 2 * channels // SUB + 1, SUB, length), jnp.float32)
    ends = jax.ShapeDtypeStruct((frames, channels, 2 * COLS), jnp.bfloat16)
    shapes = (half, half) + ((ends, ends) if with_ends else ())
    return call(functools.partial(arrange_kernel, with_ends), "arrange", (values,), shapes)


def denoise(real, other, keep, noise, inner, outer, first, second, temb):
    length = other.shape[2]
    frames = inner.shape[0]
    width = temb.shape[1]
    half = jax.ShapeDtypeStruct(other.shape, jnp.float32)
    inside, own = call(
        interior_kernel,
        "interior",
        (other, keep, first, temb),
        (
            jax.ShapeDtypeStruct((frames, length - 2 * COLS, width), jnp.bfloat16),
            jax.ShapeDtypeStruct((frames, 4 * COLS, 384), jnp.bfloat16),
        ),
        [pltpu.VMEM((frames, length, 384), jnp.bfloat16)],
        2_000_000_000,
        limit=6,
    )
    ends = (4 * COLS, width)
    spread = (2, 8 * COLS, 384)
    yours, ends_mid, spread_mid = call(
        sending_kernel,
        "sending",
        (real, other, keep, noise[0], inner, outer, first, second, temb, inside, own),
        (half, jax.ShapeDtypeStruct((2,) + ends, jnp.bfloat16), jax.ShapeDtypeStruct(spread, jnp.bfloat16)),
        [pltpu.VMEM((1,) + ends, jnp.bfloat16), pltpu.VMEM(spread, jnp.bfloat16)],
        2_000_000_000,
        limit=6,
    )
    (mine,) = call(
        keeping_kernel,
        "keeping",
        (real, keep, noise[1], first, second, temb, inside, ends_mid, spread_mid),
        (half,),
        [pltpu.VMEM((1,) + ends, jnp.bfloat16)],
        2_000_000_000,
        limit=6,
    )
    return yours, mine


def finish_kernel(other, keep, yours, mine, out, states, done):
    flags = Flags()
    channels, count, length = states.shape
    tiles = C // SUB
    group = channels // 4
    copies = []
    for at in range(0, channels, group):
        for frame in range(count):
            low = frame < count // 2
            slabs = pl.ds((frame % 2) * tiles + at // SUB, group // SUB)

            def part(first_ref, second_ref):
                one, two = first_ref[slabs].reshape(group, length), second_ref[slabs].reshape(group, length)
                return jnp.where(flags.odd, one, two) if low else jnp.where(flags.odd, two, one)

            before = jnp.where(flags.anchor, 0.0, part(other, keep))
            states[pl.ds(at, group), frame, :] = before + part(yours, mine)
        place = pl.ds(at, group)
        copies.append(pltpu.make_async_copy(states.at[place], out.at[place], done.at[len(copies)]))
        copies[-1].start()
    for copy in copies:
        copy.wait()


def finish(guesses, *halves):
    return pl.pallas_call(
        finish_kernel,
        out_shape=jax.ShapeDtypeStruct(guesses.shape, jnp.float32),
        in_specs=[WHOLE] * len(halves),
        out_specs=pl.BlockSpec(memory_space=pl.ANY),
        scratch_shapes=[pltpu.VMEM(guesses.shape, jnp.float32), pltpu.SemaphoreType.DMA((4,))],
        compiler_params=pltpu.CompilerParams(vmem_limit_bytes=4 * MEGA),
        cost_estimate=pl.CostEstimate(flops=8_000_000_000, bytes_accessed=4_000_000, transcendentals=0),
        name="finish",
    )(*halves)


def changes_kernel(own1, theirs1, own2, theirs2, sums):
    slabs = pl.ds(0, 2 * C // SUB)
    for i, (one, two) in enumerate(((own1, own2), (theirs1, theirs2))):
        change = two[slabs] - one[slabs]
        square = jnp.sum(change * change, axis=0)
        total = jnp.sum(jnp.sum(square, axis=0, keepdims=True), axis=1, keepdims=True)
        sums[i] = jnp.broadcast_to(total, sums.shape[1:])


def change_sums(one, two):
    shape = jax.ShapeDtypeStruct((2, SUB, 128), jnp.float32)
    (sums,) = call(changes_kernel, "changes", one + two, (shape,))
    return sums


def is_mark(half):
    return lax.broadcasted_iota(jnp.int32, half.shape, 0) == half.shape[0] - 1


def coded(half):
    exponent = half[-1:]
    return jnp.where(is_mark(half), half, half * jnp.exp2(14.0 - exponent)).astype(jnp.float16)


def decoded(message):
    half = message.astype(jnp.float32)
    return jnp.where(is_mark(half), half, half * jnp.exp2(half[-1:] - 14.0))


def added(one, two):
    return jnp.where(is_mark(one), jnp.maximum(one, two) + 1.0, one + two)


def masked(half, condition):
    return jnp.where(condition, half, jnp.where(is_mark(half), -100.0, 0.0))


def exchange(half, flip):
    steps = lax.axis_size("step")
    return decoded(lax.ppermute(coded(half), "step", [(i, i ^ flip) for i in range(steps)]))


def prefix(yours, mine, step_index):
    steps = lax.axis_size("step")
    odd = step_index % 2 == 1
    partner = exchange(yours, 1)
    total = added(mine, partner)
    before = masked(total, False)
    distance = 2
    while distance < steps:
        got = exchange(total, 2 * distance - 2)
        before = added(before, masked(got, (step_index // distance) % 2 == 1))
        total = added(total, got)
        distance *= 2
    keep = added(before, masked(partner, odd))
    give = added(before, masked(mine, jnp.logical_not(odd)))
    return exchange(give, 1), keep, (keep + mine, give + partner)


def local(guesses, noise, timesteps, conv_first, conv_second, time_weight):
    step_index = lax.axis_index("step")
    row_block = lax.axis_index("space")
    space = lax.axis_size("space")
    start_latent = guesses[0]
    noise_step = noise[0]
    timestep_pair = timesteps[0]
    inner_pairs = [pair for i in range(0, space - 1, 2) for pair in ((i, i + 1), (i + 1, i))]
    outer_pairs = [pair for i in range(1, space - 1, 2) for pair in ((i, i + 1), (i + 1, i))]

    pair = lax.optimization_barrier(jnp.broadcast_to(timestep_pair[:, None], (2, 128)))
    real = jnp.stack(coefficients(pair))
    temb = time_embed(pair[0, : C // 2], time_weight).reshape(1, -1)
    def weights_of(conv):
        return jnp.pad(conv.transpose(0, 2, 1), ((0, 0), (0, C), (0, 0)))

    first = weights_of(conv_first)
    first, start_latent = lax.optimization_barrier((first, start_latent))

    def sweep(first, other, keep, noise, near, far):
        inner = lax.ppermute(near, "space", inner_pairs)
        outer = lax.ppermute(far, "space", outer_pairs)
        return denoise(real, other, keep, noise, inner, outer, first, conv_second, temb)

    is_anchor = step_index == 0
    other0, keep0, near, far = arrange(start_latent, True)
    yours1, mine1 = sweep(first, other0, keep0, arrange(noise_step, False), near, far)
    mine1, conv_first, start_latent, noise_step = lax.optimization_barrier(
        (mine1, conv_first, start_latent, noise_step)
    )
    first, noise_halves = weights_of(conv_first), arrange(noise_step, False)
    other0, keep0 = arrange(start_latent, False)
    other1, keep1, reached1 = prefix(yours1, mine1, step_index)
    other1, keep1 = jnp.where(is_anchor, other0, other1), jnp.where(is_anchor, keep0, keep1)
    yours2, mine2 = sweep(first, other1, keep1, noise_halves, *edges(other1, keep1))
    other2, keep2, reached2 = prefix(yours2, mine2, step_index)
    sums = change_sums(reached1, reached2)
    steps = lax.axis_size("step")
    cell_count = start_latent.size * space
    distance = 1
    while 2 * distance < space:
        sums = sums + lax.ppermute(sums, "space", [(i, i ^ distance) for i in range(space)])
        distance *= 2
    swap = [(k * space + s, (k ^ 1) * space + s) for k in range(steps) for s in range(space)]
    cross = [(k * space + s, (k ^ 1) * space + (s ^ distance)) for k in range(steps) for s in range(space)]
    far = [(i, i ^ distance) for i in range(space)]
    near_sum, other2 = lax.optimization_barrier((sums[0], other2))
    if space == 1:
        others = (lax.ppermute(sums[1], ("step", "space"), swap),)
    else:
        others = (
            lax.ppermute(sums[1], ("step", "space"), swap),
            lax.ppermute(sums[1], ("step", "space"), cross),
            lax.ppermute(near_sum, "space", far),
        )
    states = finish(start_latent, other2, keep2, yours2, mine2)
    total = functools.reduce(jnp.add, others, sums[0])
    changes = lax.optimization_barrier(jnp.sqrt(total / cell_count))[0, :1]
    return (states[None], changes)


def solution(mesh):
    in_specs = (
        P("step", None, None, "space"),
        P("step", None, None, "space"),
        P("step", None),
        P(),
        P(),
        P(),
    )
    out_specs = (P("step", None, None, "space"), P("step"))
    return jax.shard_map(local, mesh=mesh, in_specs=in_specs, out_specs=out_specs, check_vma=False)
```

```python
import functools
import math

import jax
import jax.numpy as jnp
from jax import lax
from jax.experimental import pallas as pl
from jax.experimental.pallas import tpu as pltpu
from jax.sharding import PartitionSpec as P

C = 64
COLS = 80
SUB = 8
LANES = 128
NT = (((1,), (1,)), ((), ()))
MEGA = 2**20


def plan(timestep):
    scaled = timestep.astype(jnp.float32) / 1000.0
    return -(0.1 * scaled + 9.95 * scaled * scaled)


def coefficients(timestep_pair):
    log_from = plan(timestep_pair[0])
    log_to = plan(timestep_pair[1])
    half_gap = 0.5 * (log_to - log_from)
    decay_gain = jnp.expm1(half_gap)
    remain_from = -jnp.expm1(log_from)
    remain_to = -jnp.expm1(log_to)
    ratio_term = -jnp.expm1(log_from - log_to)
    noise_gain = -jnp.exp(half_gap) * jnp.sqrt(remain_from) + remain_to * jnp.exp(
        -half_gap
    ) / jnp.sqrt(remain_from)
    spread_gain = jnp.sqrt(remain_to / remain_from * ratio_term)
    return (decay_gain, noise_gain, spread_gain)


def time_embed(timestep, time_weight):
    half_count = C // 2
    frequency = jnp.exp(-math.log(10000.0) * jnp.arange(half_count, dtype=jnp.float32) / half_count)
    angles = timestep.astype(jnp.float32) * frequency
    features = jnp.concatenate([jnp.sin(angles), jnp.cos(angles)])
    return jnp.dot(
        features, time_weight, preferred_element_type=jnp.float32, precision=lax.Precision.HIGHEST
    )


def frame_tiles(ref):
    return ref.shape[0] // 2


def frame_of(ref, slot):
    tiles = frame_tiles(ref)
    value = ref[pl.ds(slot * tiles, tiles)].reshape(C // SUB, -1, SUB, LANES)
    return jnp.concatenate([value[:, i].reshape(C, LANES) for i in range(value.shape[1])], axis=1)


def put_frame(ref, slot, value):
    across = value.shape[1] // LANES
    for row in range(C // SUB):
        for i in range(across):
            tile = value[row * SUB : (row + 1) * SUB, i * LANES : (i + 1) * LANES]
            ref[slot * frame_tiles(ref) + row * across + i] = tile


def length_of(ref):
    return frame_tiles(ref) * SUB * LANES // C


class Frames:
    def __init__(self, parity):
        self.parity = parity

    def slot(self, v):
        return jnp.where(self.parity == 1, v % 2, (v + 1) % 2)

    def load(self, halves, v):
        return frame_of(halves[0] if v < 2 else halves[1], self.slot(v))

    def store(self, ref, v, value):
        put_frame(ref, self.slot(v), value)

    def tap(self, a):
        return jnp.where(self.parity == 1, a, 2 - a)


class Flags:
    def __init__(self, real=None):
        step, block = lax.axis_index("step"), lax.axis_index("space")
        self.parity = lax.rem(step, 2)
        self.odd = self.parity == 1
        self.even_block = lax.rem(block, 2) == 0
        self.anchor = step == 0
        if real is not None:
            self.keep, self.gain, self.spread = (real[i : i + 1, 0:1] for i in range(3))
        self.top, self.bottom = block == 0, block == lax.axis_size("space") - 1


def halo_slot(frames, v):
    return (0 if v < 2 else 2) + frames.slot(v)


def ends_of(flags, frames, halves, inner, outer):
    edge = 2 * COLS
    for half, ref in enumerate(halves):
        length = length_of(ref)
        for slot in range(2):
            values = frame_of(ref, slot)
            head = values[:, :edge].astype(jnp.bfloat16)
            tail = values[:, length - edge :].astype(jnp.bfloat16)
            inner[2 * half + slot] = jnp.where(flags.even_block, tail, head)
            outer[2 * half + slot] = jnp.where(flags.even_block, head, tail)


def edges_kernel(other, keep, inner, outer):
    flags = Flags()
    ends_of(flags, Frames(flags.parity), (other, keep), inner, outer)


def arrange_kernel(with_ends, values, other, keep, *ends):
    flags = Flags()
    count = values.shape[1]
    for slot in range(count // 2):
        low, high = values[:, slot, :], values[:, count // 2 + slot, :]
        put_frame(other, slot, jnp.where(flags.odd, low, high))
        put_frame(keep, slot, jnp.where(flags.odd, high, low))
    for ref in (other, keep):
        ref[ref.shape[0] - 1] = jnp.zeros((SUB, LANES), jnp.float32)
    if with_ends:
        ends_of(flags, Frames(flags.parity), (other, keep), *ends)


def near_frames(v, count):
    return [a for a in range(3) if 0 <= v + a - 1 < count]


def spread_columns(values):
    n = values.shape[1]
    column = lax.broadcasted_iota(jnp.int32, (1, n), 1) % COLS
    before = jnp.where(column >= 1, pltpu.roll(values, 1, 1), 0.0).astype(jnp.bfloat16)
    after = jnp.where(column <= COLS - 2, pltpu.roll(values, n - 1, 1), 0.0).astype(jnp.bfloat16)
    center = values.astype(jnp.bfloat16)
    pairs = ((before, center), (after, before), (center, after))
    return [jnp.concatenate(pair, axis=0).T for pair in pairs]


def first_weights(frames, first, v, count):
    return jnp.concatenate([first[frames.tap(a)] for a in near_frames(v, count)], axis=0)


WINDOWS = ((0, 0, 256), (1, 256, 384), (2, 0, 256))


def silu(value):
    return value / (1.0 + jnp.exp(-value))


def interior_kernel(other, keep, first, temb, hidden, own, spread):
    flags = Flags()
    frames = Frames(flags.parity)
    count, length = spread.shape[:2]
    edge = 2 * COLS
    inside = length - edge

    def prepare(v):
        left, mixed, right = spread_columns(frames.load((other, keep), v))
        spread[v, :, 0:128] = left
        spread[v, :, 128:192] = mixed[:, :64]
        spread[v, pl.ds(0, length - COLS), 192:256] = mixed[COLS:, 64:]
        spread[v, pl.ds(length - COLS, COLS), 192:256] = jnp.zeros((COLS, 64), jnp.bfloat16)
        spread[v, :, 256:384] = right

    prepare(0)
    prepare(1)
    for v in range(count):
        if v + 2 < count:
            prepare(v + 2)
        cells = jnp.concatenate(
            [
                spread[v + a - 1, pl.ds(b * COLS, inside), low:high]
                for a in near_frames(v, count)
                for b, low, high in WINDOWS
            ],
            axis=1,
        )
        value = jnp.dot(cells, first_weights(frames, first, v, count), preferred_element_type=jnp.float32)
        hidden[v] = silu(value + temb[...]).astype(jnp.bfloat16)
        own[v, pl.ds(0, edge), :] = spread[v, pl.ds(0, edge), :]
        own[v, pl.ds(edge, edge), :] = spread[v, pl.ds(inside, edge), :]


class Rest:
    def __init__(self, real, halves, noise, first, second, temb, inside, ends):
        self.flags = Flags(real)
        self.frames = Frames(self.flags.parity)
        self.halves, self.noise = halves, noise
        self.first, self.second, self.temb, self.inside, self.ends = first, second, temb, inside, ends
        self.channels, self.count, self.length = C, inside.shape[0], inside.shape[1] + 2 * COLS

    def prepare(self, v, inner, outer, own, spread):
        edge = 2 * COLS
        at = halo_slot(self.frames, v)
        near, far = inner[at].astype(jnp.float32), outer[at].astype(jnp.float32)
        even = self.flags.even_block
        both = jnp.concatenate([jnp.where(even, far, near), jnp.where(even, near, far)], axis=1)
        left, mixed, right = spread_columns(both)
        ref, i = spread[v]
        ref[i, pl.ds(edge, 2 * edge), :] = own[v]
        for low, high, rows in ((0, 128, left), (128, 192, mixed[:, :64]), (256, 384, right)):
            ref[i, pl.ds(0, edge), low:high] = rows[:edge]
            ref[i, pl.ds(3 * edge, edge), low:high] = rows[edge:]
        ref[i, pl.ds(0, COLS), 192:256] = mixed[COLS:edge, 64:]
        ref[i, pl.ds(COLS, COLS), 192:256] = own[v, pl.ds(0, COLS), 0:64]
        ref[i, pl.ds(3 * edge - COLS, edge), 192:256] = mixed[edge:, 64:]
        ref[i, pl.ds(3 * edge + COLS, COLS), 192:256] = jnp.zeros((COLS, 64), jnp.bfloat16)

    def edge_rows(self, v, spread):
        edge = 2 * COLS
        top, bottom = self.flags.top, self.flags.bottom
        rows = []
        for group in (0, 2 * edge):
            rows.append(
                jnp.concatenate(
                    [
                        spread[v + a - 1][0][spread[v + a - 1][1], pl.ds(group + b * COLS, edge), low:high]
                        for a in near_frames(v, self.count)
                        for b, low, high in WINDOWS
                    ],
                    axis=1,
                )
            )
        weights = first_weights(self.frames, self.first, v, self.count)
        value = jnp.dot(jnp.concatenate(rows, axis=0), weights, preferred_element_type=jnp.float32)
        active = silu(value + self.temb[...])
        place = lax.broadcasted_iota(jnp.int32, (2 * edge, 1), 0)
        outside = jnp.logical_or(
            jnp.logical_and(place < COLS, top), jnp.logical_and(place >= 2 * edge - COLS, bottom)
        )
        ref, i = self.ends[v]
        ref[i] = jnp.where(outside, 0.0, active).astype(jnp.bfloat16)

    def second_conv(self, v, out):
        channels, length, flags = self.channels, self.length, self.flags
        width = self.temb.shape[1]
        edge = 2 * COLS
        taps = [(a, b) for a in near_frames(v, self.count) for b in range(3)]
        weights = jnp.concatenate(
            [
                jnp.concatenate(
                    [
                        self.second[self.frames.tap(a), :, (b * 3 + e) * width : (b * 3 + e + 1) * width]
                        for e in range(3)
                    ],
                    axis=0,
                )
                for a, b in taps
            ],
            axis=1,
        )
        latent, noise = self.frames.load(self.halves, v), self.frames.load(self.noise, v)
        base = flags.keep * latent + flags.spread * noise + jnp.where(flags.anchor, latent, 0.0)
        chunk = length // 2
        column = lax.broadcasted_iota(jnp.int32, (1, chunk), 1) % COLS
        predicted = []
        for start in range(0, length, chunk):
            cells = []
            for a, b in taps:
                ref, i = self.ends[v + a - 1]
                low, high = start + b * COLS, start + b * COLS + chunk
                rows = []
                if low < edge:
                    rows.append(ref[i, pl.ds(low, edge - low), :])
                at, end = max(low, edge), min(high, length)
                rows.append(self.inside[v + a - 1, pl.ds(at - edge, end - at), :])
                if high > length:
                    rows.append(ref[i, pl.ds(edge, high - length), :])
                cells.append(jnp.concatenate(rows, axis=0))
            cells = jnp.concatenate(cells, axis=1)
            parts = lax.dot_general(cells, weights, NT, preferred_element_type=jnp.float32).T
            before = jnp.where(column >= 1, pltpu.roll(parts[:channels], 1, 1), 0.0)
            after = jnp.where(
                column <= COLS - 2, pltpu.roll(parts[2 * channels : 3 * channels], chunk - 1, 1), 0.0
            )
            predicted.append(before + parts[channels : 2 * channels] + after)
        result = base + flags.gain * jnp.concatenate(predicted, axis=1)
        self.frames.store(out, v, result)
        return jnp.max(jnp.abs(result), axis=0, keepdims=True)

    def mark(self, ref, peaks):
        peak = jnp.max(functools.reduce(jnp.maximum, peaks), axis=1, keepdims=True)
        exponent = jnp.clip(jnp.ceil(jnp.log(peak) * (1.0 / math.log(2.0))) + 1.0, -100.0, 126.0)
        ref[ref.shape[0] - 1] = jnp.broadcast_to(exponent, (SUB, LANES))


def sending_kernel(real, other, keep, noise_other, inner, outer, first, second, temb, inside, own, yours, *rest):
    ends_out, spread_out, ends_own, spread_own = rest
    ends = {0: (ends_own, 0), 1: (ends_out, 0), 2: (ends_out, 1)}
    spread = {0: (spread_own, 0), 1: (spread_own, 1), 2: (spread_out, 0), 3: (spread_out, 1)}
    work = Rest(real, (other, keep), (noise_other, None), first, second, temb, inside, ends)
    work.prepare(0, inner, outer, own, spread)
    work.prepare(1, inner, outer, own, spread)
    work.edge_rows(0, spread)
    work.prepare(2, inner, outer, own, spread)
    work.edge_rows(1, spread)
    work.prepare(3, inner, outer, own, spread)
    peaks = [work.second_conv(0, yours)]
    work.edge_rows(2, spread)
    peaks.append(work.second_conv(1, yours))
    work.mark(yours, peaks)


def keeping_kernel(real, keep, noise_keep, first, second, temb, inside, ends_in, spread_in, mine, ends_own):
    ends = {1: (ends_in, 0), 2: (ends_in, 1), 3: (ends_own, 0)}
    work = Rest(real, (keep, keep), (None, noise_keep), first, second, temb, inside, ends)
    work.edge_rows(3, {2: (spread_in, 0), 3: (spread_in, 1)})
    work.mark(mine, [work.second_conv(2, mine), work.second_conv(3, mine)])


WHOLE = pl.BlockSpec(memory_space=pltpu.VMEM)


def call(kernel, name, arrays, out_shape, scratch=(), flops=1_000_000, limit=4):
    return pl.pallas_call(
        kernel,
        out_shape=out_shape,
        in_specs=[WHOLE] * len(arrays),
        out_specs=tuple(WHOLE for _ in out_shape),
        scratch_shapes=list(scratch),
        compiler_params=pltpu.CompilerParams(vmem_limit_bytes=limit * MEGA),
        cost_estimate=pl.CostEstimate(flops=flops, bytes_accessed=4_000_000, transcendentals=100_000),
        name=name,
    )(*arrays)


def edges(other, keep):
    shape = jax.ShapeDtypeStruct((4, C, 2 * COLS), jnp.bfloat16)
    return call(edges_kernel, "edges", (other, keep), (shape, shape))


def arrange(values, with_ends):
    channels, frames, length = values.shape
    half = jax.ShapeDtypeStruct((frames // 2 * channels * length // (SUB * LANES) + 1, SUB, LANES), jnp.float32)
    ends = jax.ShapeDtypeStruct((frames, channels, 2 * COLS), jnp.bfloat16)
    shapes = (half, half) + ((ends, ends) if with_ends else ())
    return call(functools.partial(arrange_kernel, with_ends), "arrange", (values,), shapes)


def denoise(real, other, keep, noise, inner, outer, first, second, temb):
    length = length_of(other)
    frames = inner.shape[0]
    width = temb.shape[1]
    half = jax.ShapeDtypeStruct(other.shape, jnp.float32)
    inside, own = call(
        interior_kernel,
        "interior",
        (other, keep, first, temb),
        (
            jax.ShapeDtypeStruct((frames, length - 2 * COLS, width), jnp.bfloat16),
            jax.ShapeDtypeStruct((frames, 4 * COLS, 384), jnp.bfloat16),
        ),
        [pltpu.VMEM((frames, length, 384), jnp.bfloat16)],
        2_000_000_000,
        limit=6,
    )
    ends = (4 * COLS, width)
    spread = (2, 8 * COLS, 384)
    yours, ends_mid, spread_mid = call(
        sending_kernel,
        "sending",
        (real, other, keep, noise[0], inner, outer, first, second, temb, inside, own),
        (half, jax.ShapeDtypeStruct((2,) + ends, jnp.bfloat16), jax.ShapeDtypeStruct(spread, jnp.bfloat16)),
        [pltpu.VMEM((1,) + ends, jnp.bfloat16), pltpu.VMEM(spread, jnp.bfloat16)],
        2_000_000_000,
        limit=6,
    )
    (mine,) = call(
        keeping_kernel,
        "keeping",
        (real, keep, noise[1], first, second, temb, inside, ends_mid, spread_mid),
        (half,),
        [pltpu.VMEM((1,) + ends, jnp.bfloat16)],
        2_000_000_000,
        limit=6,
    )
    return yours, mine


def finish_kernel(other, keep, yours, mine, out, states, done):
    flags = Flags()
    channels, count, length = states.shape
    group = channels // 4
    rows, across = group // SUB, length // LANES
    copies = []
    for at in range(0, channels, group):
        for frame in range(count):
            low = frame < count // 2
            slabs = pl.ds((frame % 2) * frame_tiles(keep) + at // SUB * across, rows * across)

            def part(first_ref, second_ref):
                one, two = first_ref[slabs], second_ref[slabs]
                return jnp.where(flags.odd, one, two) if low else jnp.where(flags.odd, two, one)

            before = jnp.where(flags.anchor, 0.0, part(other, keep))
            value = (before + part(yours, mine)).reshape(rows, across, SUB, LANES)
            columns = [value[:, i].reshape(group, LANES) for i in range(across)]
            states[pl.ds(at, group), frame, :] = jnp.concatenate(columns, axis=1)
        place = pl.ds(at, group)
        copies.append(pltpu.make_async_copy(states.at[place], out.at[place], done.at[len(copies)]))
        copies[-1].start()
    for copy in copies:
        copy.wait()


def finish(guesses, *halves):
    return pl.pallas_call(
        finish_kernel,
        out_shape=jax.ShapeDtypeStruct(guesses.shape, jnp.float32),
        in_specs=[WHOLE] * len(halves),
        out_specs=pl.BlockSpec(memory_space=pl.ANY),
        scratch_shapes=[pltpu.VMEM(guesses.shape, jnp.float32), pltpu.SemaphoreType.DMA((4,))],
        compiler_params=pltpu.CompilerParams(vmem_limit_bytes=4 * MEGA),
        cost_estimate=pl.CostEstimate(flops=8_000_000_000, bytes_accessed=4_000_000, transcendentals=0),
        name="finish",
    )(*halves)


def changes_kernel(own1, theirs1, own2, theirs2, sums):
    slabs = pl.ds(0, own1.shape[0] - 1)
    for i, (one, two) in enumerate(((own1, own2), (theirs1, theirs2))):
        change = two[slabs] - one[slabs]
        square = jnp.sum(change * change, axis=0)
        total = jnp.sum(jnp.sum(square, axis=0, keepdims=True), axis=1, keepdims=True)
        sums[i] = jnp.broadcast_to(total, sums.shape[1:])


def change_sums(one, two):
    shape = jax.ShapeDtypeStruct((2, SUB, 128), jnp.float32)
    (sums,) = call(changes_kernel, "changes", one + two, (shape,))
    return sums


def is_mark(half):
    return lax.broadcasted_iota(jnp.int32, half.shape, 0) == half.shape[0] - 1


def coded(half):
    exponent = half[-1:]
    return jnp.where(is_mark(half), half, half * jnp.exp2(14.0 - exponent)).astype(jnp.float16)


def decoded(message):
    half = message.astype(jnp.float32)
    return jnp.where(is_mark(half), half, half * jnp.exp2(half[-1:] - 14.0))


def added(one, two):
    return jnp.where(is_mark(one), jnp.maximum(one, two) + 1.0, one + two)


def masked(half, condition):
    return jnp.where(condition, half, jnp.where(is_mark(half), -100.0, 0.0))


def exchange(half, flip):
    steps = lax.axis_size("step")
    return decoded(lax.ppermute(coded(half), "step", [(i, i ^ flip) for i in range(steps)]))


def prefix(yours, mine, step_index):
    steps = lax.axis_size("step")
    odd = step_index % 2 == 1
    partner = exchange(yours, 1)
    total = added(mine, partner)
    before = masked(total, False)
    distance = 2
    while distance < steps:
        got = exchange(total, 2 * distance - 2)
        before = added(before, masked(got, (step_index // distance) % 2 == 1))
        total = added(total, got)
        distance *= 2
    keep = added(before, masked(partner, odd))
    give = added(before, masked(mine, jnp.logical_not(odd)))
    return exchange(give, 1), keep, (keep + mine, give + partner)


def local(guesses, noise, timesteps, conv_first, conv_second, time_weight):
    step_index = lax.axis_index("step")
    row_block = lax.axis_index("space")
    space = lax.axis_size("space")
    start_latent = guesses[0]
    noise_step = noise[0]
    timestep_pair = timesteps[0]
    inner_pairs = [pair for i in range(0, space - 1, 2) for pair in ((i, i + 1), (i + 1, i))]
    outer_pairs = [pair for i in range(1, space - 1, 2) for pair in ((i, i + 1), (i + 1, i))]

    pair = lax.optimization_barrier(jnp.broadcast_to(timestep_pair[:, None], (2, 128)))
    real = jnp.stack(coefficients(pair))
    temb = time_embed(pair[0, : C // 2], time_weight).reshape(1, -1)
    def weights_of(conv):
        return jnp.pad(conv.transpose(0, 2, 1), ((0, 0), (0, C), (0, 0)))

    first = weights_of(conv_first)
    first, start_latent = lax.optimization_barrier((first, start_latent))

    def sweep(first, other, keep, noise, near, far):
        inner = lax.ppermute(near, "space", inner_pairs)
        outer = lax.ppermute(far, "space", outer_pairs)
        return denoise(real, other, keep, noise, inner, outer, first, conv_second, temb)

    is_anchor = step_index == 0
    other0, keep0, near, far = arrange(start_latent, True)
    yours1, mine1 = sweep(first, other0, keep0, arrange(noise_step, False), near, far)
    mine1, conv_first, start_latent, noise_step = lax.optimization_barrier(
        (mine1, conv_first, start_latent, noise_step)
    )
    first, noise_halves = weights_of(conv_first), arrange(noise_step, False)
    other0, keep0 = arrange(start_latent, False)
    other1, keep1, reached1 = prefix(yours1, mine1, step_index)
    other1, keep1 = jnp.where(is_anchor, other0, other1), jnp.where(is_anchor, keep0, keep1)
    yours2, mine2 = sweep(first, other1, keep1, noise_halves, *edges(other1, keep1))
    other2, keep2, reached2 = prefix(yours2, mine2, step_index)
    sums = change_sums(reached1, reached2)
    steps = lax.axis_size("step")
    cell_count = start_latent.size * space
    distance = 1
    while 2 * distance < space:
        sums = sums + lax.ppermute(sums, "space", [(i, i ^ distance) for i in range(space)])
        distance *= 2
    total = sums[0] + lax.ppermute(sums[1], "step", [(i, i ^ 1) for i in range(steps)])
    if space > 1:
        total = total + lax.ppermute(total, "space", [(i, i ^ distance) for i in range(space)])
    states = finish(start_latent, other2, keep2, yours2, mine2)
    total, states = lax.optimization_barrier((total, states))
    changes = lax.optimization_barrier(jnp.sqrt(total / cell_count))[0, :1]
    return (states[None], changes)


def solution(mesh):
    in_specs = (
        P("step", None, None, "space"),
        P("step", None, None, "space"),
        P("step", None),
        P(),
        P(),
        P(),
    )
    out_specs = (P("step", None, None, "space"), P("step"))
    return jax.shard_map(local, mesh=mesh, in_specs=in_specs, out_specs=out_specs, check_vma=False)
```

```python
import functools
import math

import jax
import jax.numpy as jnp
from jax import lax
from jax.experimental import pallas as pl
from jax.experimental.pallas import tpu as pltpu
from jax.sharding import PartitionSpec as P

C = 64
COLS = 80
SUB = 8
LANES = 128
WIDE = -(-2 * COLS // LANES) * LANES
NT = (((1,), (1,)), ((), ()))
MEGA = 2**20


def plan(timestep):
    scaled = timestep.astype(jnp.float32) / 1000.0
    return -(0.1 * scaled + 9.95 * scaled * scaled)


def coefficients(timestep_pair):
    log_from = plan(timestep_pair[0])
    log_to = plan(timestep_pair[1])
    half_gap = 0.5 * (log_to - log_from)
    decay_gain = jnp.expm1(half_gap)
    remain_from = -jnp.expm1(log_from)
    remain_to = -jnp.expm1(log_to)
    ratio_term = -jnp.expm1(log_from - log_to)
    noise_gain = -jnp.exp(half_gap) * jnp.sqrt(remain_from) + remain_to * jnp.exp(
        -half_gap
    ) / jnp.sqrt(remain_from)
    spread_gain = jnp.sqrt(remain_to / remain_from * ratio_term)
    return (decay_gain, noise_gain, spread_gain)


def time_embed(timestep, time_weight):
    half_count = C // 2
    frequency = jnp.exp(-math.log(10000.0) * jnp.arange(half_count, dtype=jnp.float32) / half_count)
    angles = timestep.astype(jnp.float32) * frequency
    features = jnp.concatenate([jnp.sin(angles), jnp.cos(angles)])
    return jnp.dot(
        features, time_weight, preferred_element_type=jnp.float32, precision=lax.Precision.HIGHEST
    )


def frame_tiles(ref):
    return ref.shape[0] // 2


def frame_of(ref, slot):
    tiles = frame_tiles(ref)
    value = ref[pl.ds(slot * tiles, tiles)].reshape(C // SUB, -1, SUB, LANES)
    return jnp.concatenate([value[:, i].reshape(C, LANES) for i in range(value.shape[1])], axis=1)


def put_frame(ref, slot, value):
    across = value.shape[1] // LANES
    for row in range(C // SUB):
        for i in range(across):
            tile = value[row * SUB : (row + 1) * SUB, i * LANES : (i + 1) * LANES]
            ref[slot * frame_tiles(ref) + row * across + i] = tile


def length_of(ref):
    return frame_tiles(ref) * SUB * LANES // C


class Frames:
    def __init__(self, parity):
        self.parity = parity

    def slot(self, v):
        return jnp.where(self.parity == 1, v % 2, (v + 1) % 2)

    def load(self, halves, v):
        return frame_of(halves[0] if v < 2 else halves[1], self.slot(v))

    def store(self, ref, v, value):
        put_frame(ref, self.slot(v), value)

    def tap(self, a):
        return jnp.where(self.parity == 1, a, 2 - a)


class Flags:
    def __init__(self, real=None):
        step, block = lax.axis_index("step"), lax.axis_index("space")
        self.parity = lax.rem(step, 2)
        self.odd = self.parity == 1
        self.even_block = lax.rem(block, 2) == 0
        self.anchor = step == 0
        if real is not None:
            self.keep, self.gain, self.spread = (real[i : i + 1, 0:1] for i in range(3))
        self.top, self.bottom = block == 0, block == lax.axis_size("space") - 1


def halo_slot(frames, v):
    return (0 if v < 2 else 2) + frames.slot(v)


def ends_of(flags, frames, halves, inner, outer):
    for half, ref in enumerate(halves):
        length = length_of(ref)
        for slot in range(2):
            values = frame_of(ref, slot)
            head = values[:, :WIDE].astype(jnp.bfloat16)
            tail = values[:, length - WIDE :].astype(jnp.bfloat16)
            inner[2 * half + slot] = jnp.where(flags.even_block, tail, head)
            outer[2 * half + slot] = jnp.where(flags.even_block, head, tail)


def edges_kernel(other, keep, inner, outer):
    flags = Flags()
    ends_of(flags, Frames(flags.parity), (other, keep), inner, outer)


def arrange_kernel(with_ends, values, other, keep, *ends):
    flags = Flags()
    count = values.shape[1]
    for slot in range(count // 2):
        low, high = values[:, slot, :], values[:, count // 2 + slot, :]
        put_frame(other, slot, jnp.where(flags.odd, low, high))
        put_frame(keep, slot, jnp.where(flags.odd, high, low))
    for ref in (other, keep):
        ref[ref.shape[0] - 1] = jnp.zeros((SUB, LANES), jnp.float32)
    if with_ends:
        ends_of(flags, Frames(flags.parity), (other, keep), *ends)


def near_frames(v, count):
    return [a for a in range(3) if 0 <= v + a - 1 < count]


def spread_columns(values, column):
    n = values.shape[1]
    before = jnp.where(column >= 1, pltpu.roll(values, 1, 1), 0.0).astype(jnp.bfloat16)
    after = jnp.where(column <= COLS - 2, pltpu.roll(values, n - 1, 1), 0.0).astype(jnp.bfloat16)
    center = values.astype(jnp.bfloat16)
    pairs = ((before, center), (after, before), (center, after))
    return [jnp.concatenate(pair, axis=0).T for pair in pairs]


def first_weights(frames, first, v, count):
    return jnp.concatenate([first[frames.tap(a)] for a in near_frames(v, count)], axis=0)


WINDOWS = ((0, 0, 256), (1, 256, 384), (2, 0, 256))


def silu(value):
    return value / (1.0 + jnp.exp(-value))


def interior_kernel(other, keep, first, temb, hidden, own, spread):
    flags = Flags()
    frames = Frames(flags.parity)
    count, length = spread.shape[:2]
    edge = 2 * COLS
    inside = length - edge

    def prepare(v):
        column = lax.broadcasted_iota(jnp.int32, (1, length), 1) % COLS
        left, mixed, right = spread_columns(frames.load((other, keep), v), column)
        spread[v, :, 0:128] = left
        spread[v, :, 128:192] = mixed[:, :64]
        spread[v, pl.ds(0, length - COLS), 192:256] = mixed[COLS:, 64:]
        spread[v, pl.ds(length - COLS, COLS), 192:256] = jnp.zeros((COLS, 64), jnp.bfloat16)
        spread[v, :, 256:384] = right

    prepare(0)
    prepare(1)
    for v in range(count):
        if v + 2 < count:
            prepare(v + 2)
        cells = jnp.concatenate(
            [
                spread[v + a - 1, pl.ds(b * COLS, inside), low:high]
                for a in near_frames(v, count)
                for b, low, high in WINDOWS
            ],
            axis=1,
        )
        value = jnp.dot(cells, first_weights(frames, first, v, count), preferred_element_type=jnp.float32)
        hidden[v] = silu(value + temb[...]).astype(jnp.bfloat16)
        own[v, pl.ds(0, edge), :] = spread[v, pl.ds(0, edge), :]
        own[v, pl.ds(edge, edge), :] = spread[v, pl.ds(inside, edge), :]


class Rest:
    def __init__(self, real, halves, noise, first, second, temb, inside, ends):
        self.flags = Flags(real)
        self.frames = Frames(self.flags.parity)
        self.halves, self.noise = halves, noise
        self.first, self.second, self.temb, self.inside, self.ends = first, second, temb, inside, ends
        self.channels, self.count, self.length = C, inside.shape[0], inside.shape[1] + 2 * COLS

    def prepare(self, v, inner, outer, own, spread):
        edge = 2 * COLS
        at = halo_slot(self.frames, v)
        near, far = inner[at].astype(jnp.float32), outer[at].astype(jnp.float32)
        even = self.flags.even_block
        above, below = jnp.where(even, far, near), jnp.where(even, near, far)
        total = 2 * WIDE - LANES
        lane = lax.broadcasted_iota(jnp.int32, (1, total), 1)
        shared = jnp.where(lane[:, :LANES] < LANES // 2, below[:, WIDE - LANES :], above[:, :LANES])
        both = jnp.concatenate([below[:, : WIDE - LANES], shared, above[:, LANES:]], axis=1)
        at = total - edge
        column = jnp.where(lane < total // 2, lane, lane + (-at % COLS)) % COLS
        left, mixed, right = spread_columns(both, column)
        ref, i = spread[v]
        ref[i, pl.ds(edge, 2 * edge), :] = own[v]
        for low, high, rows in ((0, 128, left), (128, 192, mixed[:, :64]), (256, 384, right)):
            ref[i, pl.ds(0, edge), low:high] = rows[at:]
            ref[i, pl.ds(3 * edge, edge), low:high] = rows[:edge]
        ref[i, pl.ds(0, COLS), 192:256] = mixed[at + COLS :, 64:]
        ref[i, pl.ds(COLS, COLS), 192:256] = own[v, pl.ds(0, COLS), 0:64]
        ref[i, pl.ds(3 * edge - COLS, edge), 192:256] = mixed[:edge, 64:]
        ref[i, pl.ds(3 * edge + COLS, COLS), 192:256] = jnp.zeros((COLS, 64), jnp.bfloat16)

    def edge_rows(self, v, spread):
        edge = 2 * COLS
        top, bottom = self.flags.top, self.flags.bottom
        rows = []
        for group in (0, 2 * edge):
            rows.append(
                jnp.concatenate(
                    [
                        spread[v + a - 1][0][spread[v + a - 1][1], pl.ds(group + b * COLS, edge), low:high]
                        for a in near_frames(v, self.count)
                        for b, low, high in WINDOWS
                    ],
                    axis=1,
                )
            )
        weights = first_weights(self.frames, self.first, v, self.count)
        value = jnp.dot(jnp.concatenate(rows, axis=0), weights, preferred_element_type=jnp.float32)
        active = silu(value + self.temb[...])
        place = lax.broadcasted_iota(jnp.int32, (2 * edge, 1), 0)
        outside = jnp.logical_or(
            jnp.logical_and(place < COLS, top), jnp.logical_and(place >= 2 * edge - COLS, bottom)
        )
        ref, i = self.ends[v]
        ref[i] = jnp.where(outside, 0.0, active).astype(jnp.bfloat16)

    def second_conv(self, v, out):
        channels, length, flags = self.channels, self.length, self.flags
        width = self.temb.shape[1]
        edge = 2 * COLS
        taps = [(a, b) for a in near_frames(v, self.count) for b in range(3)]
        weights = jnp.concatenate(
            [
                jnp.concatenate(
                    [
                        self.second[self.frames.tap(a), :, (b * 3 + e) * width : (b * 3 + e + 1) * width]
                        for e in range(3)
                    ],
                    axis=0,
                )
                for a, b in taps
            ],
            axis=1,
        )
        latent, noise = self.frames.load(self.halves, v), self.noise_of(v)
        base = flags.keep * latent + flags.spread * noise + jnp.where(flags.anchor, latent, 0.0)
        chunk = length // 2
        column = lax.broadcasted_iota(jnp.int32, (1, chunk), 1) % COLS
        predicted = []
        for start in range(0, length, chunk):
            cells = []
            for a, b in taps:
                ref, i = self.ends[v + a - 1]
                low, high = start + b * COLS, start + b * COLS + chunk
                rows = []
                if low < edge:
                    rows.append(ref[i, pl.ds(low, edge - low), :])
                at, end = max(low, edge), min(high, length)
                rows.append(self.inside[v + a - 1, pl.ds(at - edge, end - at), :])
                if high > length:
                    rows.append(ref[i, pl.ds(edge, high - length), :])
                cells.append(jnp.concatenate(rows, axis=0))
            cells = jnp.concatenate(cells, axis=1)
            parts = lax.dot_general(cells, weights, NT, preferred_element_type=jnp.float32).T
            before = jnp.where(column >= 1, pltpu.roll(parts[:channels], 1, 1), 0.0)
            after = jnp.where(
                column <= COLS - 2, pltpu.roll(parts[2 * channels : 3 * channels], chunk - 1, 1), 0.0
            )
            predicted.append(before + parts[channels : 2 * channels] + after)
        result = base + flags.gain * jnp.concatenate(predicted, axis=1)
        self.frames.store(out, v, result)
        return jnp.max(jnp.abs(result), axis=0, keepdims=True)

    def noise_of(self, v):
        if len(self.noise.shape) == 3 and self.noise.shape[1] == self.count:
            return jnp.where(self.flags.odd, self.noise[:, v, :], self.noise[:, self.count - 1 - v, :])
        return frame_of(self.noise, self.frames.slot(v))

    def mark(self, ref, peaks):
        peak = jnp.max(functools.reduce(jnp.maximum, peaks), axis=1, keepdims=True)
        exponent = jnp.clip(jnp.ceil(jnp.log(peak) * (1.0 / math.log(2.0))) + 1.0, -100.0, 126.0)
        ref[ref.shape[0] - 1] = jnp.broadcast_to(exponent, (SUB, LANES))


def sending_kernel(real, other, keep, noise, inner, outer, first, second, temb, inside, own, yours, *rest):
    ends_out, spread_out, ends_own, spread_own = rest
    ends = {0: (ends_own, 0), 1: (ends_out, 0), 2: (ends_out, 1)}
    spread = {0: (spread_own, 0), 1: (spread_own, 1), 2: (spread_out, 0), 3: (spread_out, 1)}
    work = Rest(real, (other, keep), noise, first, second, temb, inside, ends)
    work.prepare(0, inner, outer, own, spread)
    work.prepare(1, inner, outer, own, spread)
    work.edge_rows(0, spread)
    work.prepare(2, inner, outer, own, spread)
    work.edge_rows(1, spread)
    work.prepare(3, inner, outer, own, spread)
    peaks = [work.second_conv(0, yours)]
    work.edge_rows(2, spread)
    peaks.append(work.second_conv(1, yours))
    work.mark(yours, peaks)


def keeping_kernel(real, keep, noise, first, second, temb, inside, ends_in, spread_in, mine, ends_own):
    ends = {1: (ends_in, 0), 2: (ends_in, 1), 3: (ends_own, 0)}
    work = Rest(real, (keep, keep), noise, first, second, temb, inside, ends)
    work.edge_rows(3, {2: (spread_in, 0), 3: (spread_in, 1)})
    work.mark(mine, [work.second_conv(2, mine), work.second_conv(3, mine)])


WHOLE = pl.BlockSpec(memory_space=pltpu.VMEM)


def call(kernel, name, arrays, out_shape, scratch=(), flops=1_000_000, limit=4):
    return pl.pallas_call(
        kernel,
        out_shape=out_shape,
        in_specs=[WHOLE] * len(arrays),
        out_specs=tuple(WHOLE for _ in out_shape),
        scratch_shapes=list(scratch),
        compiler_params=pltpu.CompilerParams(vmem_limit_bytes=limit * MEGA),
        cost_estimate=pl.CostEstimate(flops=flops, bytes_accessed=4_000_000, transcendentals=100_000),
        name=name,
    )(*arrays)


def edges(other, keep):
    shape = jax.ShapeDtypeStruct((4, C, WIDE), jnp.bfloat16)
    return call(edges_kernel, "edges", (other, keep), (shape, shape))


def arrange(values, with_ends):
    channels, frames, length = values.shape
    half = jax.ShapeDtypeStruct((frames // 2 * channels * length // (SUB * LANES) + 1, SUB, LANES), jnp.float32)
    ends = jax.ShapeDtypeStruct((frames, channels, WIDE), jnp.bfloat16)
    shapes = (half, half) + ((ends, ends) if with_ends else ())
    return call(functools.partial(arrange_kernel, with_ends), "arrange", (values,), shapes)


def denoise(real, other, keep, noise, inner, outer, first, second, temb):
    length = length_of(other)
    frames = inner.shape[0]
    width = temb.shape[1]
    half = jax.ShapeDtypeStruct(other.shape, jnp.float32)
    inside, own = call(
        interior_kernel,
        "interior",
        (other, keep, first, temb),
        (
            jax.ShapeDtypeStruct((frames, length - 2 * COLS, width), jnp.bfloat16),
            jax.ShapeDtypeStruct((frames, 4 * COLS, 384), jnp.bfloat16),
        ),
        [pltpu.VMEM((frames, length, 384), jnp.bfloat16)],
        2_000_000_000,
        limit=6,
    )
    ends = (4 * COLS, width)
    spread = (2, 8 * COLS, 384)
    yours, ends_mid, spread_mid = call(
        sending_kernel,
        "sending",
        (real, other, keep, noise[0], inner, outer, first, second, temb, inside, own),
        (half, jax.ShapeDtypeStruct((2,) + ends, jnp.bfloat16), jax.ShapeDtypeStruct(spread, jnp.bfloat16)),
        [pltpu.VMEM((1,) + ends, jnp.bfloat16), pltpu.VMEM(spread, jnp.bfloat16)],
        2_000_000_000,
        limit=6,
    )
    (mine,) = call(
        keeping_kernel,
        "keeping",
        (real, keep, noise[1], first, second, temb, inside, ends_mid, spread_mid),
        (half,),
        [pltpu.VMEM((1,) + ends, jnp.bfloat16)],
        2_000_000_000,
        limit=6,
    )
    return yours, mine


def finish_kernel(other, keep, yours, mine, out, states, done):
    flags = Flags()
    channels, count, length = states.shape
    group = channels // 4
    rows, across = group // SUB, length // LANES
    copies = []
    for at in range(0, channels, group):
        for frame in range(count):
            low = frame < count // 2
            slabs = pl.ds((frame % 2) * frame_tiles(keep) + at // SUB * across, rows * across)

            def part(first_ref, second_ref):
                one, two = first_ref[slabs], second_ref[slabs]
                return jnp.where(flags.odd, one, two) if low else jnp.where(flags.odd, two, one)

            before = jnp.where(flags.anchor, 0.0, part(other, keep))
            value = (before + part(yours, mine)).reshape(rows, across, SUB, LANES)
            columns = [value[:, i].reshape(group, LANES) for i in range(across)]
            states[pl.ds(at, group), frame, :] = jnp.concatenate(columns, axis=1)
        place = pl.ds(at, group)
        copies.append(pltpu.make_async_copy(states.at[place], out.at[place], done.at[len(copies)]))
        copies[-1].start()
    for copy in copies:
        copy.wait()


def finish(guesses, *halves):
    return pl.pallas_call(
        finish_kernel,
        out_shape=jax.ShapeDtypeStruct(guesses.shape, jnp.float32),
        in_specs=[WHOLE] * len(halves),
        out_specs=pl.BlockSpec(memory_space=pl.ANY),
        scratch_shapes=[pltpu.VMEM(guesses.shape, jnp.float32), pltpu.SemaphoreType.DMA((4,))],
        compiler_params=pltpu.CompilerParams(vmem_limit_bytes=4 * MEGA),
        cost_estimate=pl.CostEstimate(flops=8_000_000_000, bytes_accessed=4_000_000, transcendentals=0),
        name="finish",
    )(*halves)


def changes_kernel(own1, theirs1, own2, theirs2, sums):
    slabs = pl.ds(0, own1.shape[0] - 1)
    for i, (one, two) in enumerate(((own1, own2), (theirs1, theirs2))):
        change = two[slabs] - one[slabs]
        square = jnp.sum(change * change, axis=0)
        total = jnp.sum(jnp.sum(square, axis=0, keepdims=True), axis=1, keepdims=True)
        sums[i] = jnp.broadcast_to(total, sums.shape[1:])


def change_sums(one, two):
    shape = jax.ShapeDtypeStruct((2, SUB, 128), jnp.float32)
    (sums,) = call(changes_kernel, "changes", one + two, (shape,))
    return sums


def is_mark(half):
    return lax.broadcasted_iota(jnp.int32, half.shape, 0) == half.shape[0] - 1


def coded(half):
    exponent = half[-1:]
    return jnp.where(is_mark(half), half, half * jnp.exp2(14.0 - exponent)).astype(jnp.float16)


def decoded(message):
    half = message.astype(jnp.float32)
    return jnp.where(is_mark(half), half, half * jnp.exp2(half[-1:] - 14.0))


def added(one, two):
    return jnp.where(is_mark(one), jnp.maximum(one, two) + 1.0, one + two)


def masked(half, condition):
    return jnp.where(condition, half, jnp.where(is_mark(half), -100.0, 0.0))


def exchange(half, flip):
    steps = lax.axis_size("step")
    return decoded(lax.ppermute(coded(half), "step", [(i, i ^ flip) for i in range(steps)]))


def prefix(yours, mine, step_index):
    steps = lax.axis_size("step")
    odd = step_index % 2 == 1
    partner = exchange(yours, 1)
    total = added(mine, partner)
    before = masked(total, False)
    distance = 2
    while distance < steps:
        got = exchange(total, 2 * distance - 2)
        before = added(before, masked(got, (step_index // distance) % 2 == 1))
        total = added(total, got)
        distance *= 2
    keep = added(before, masked(partner, odd))
    give = added(before, masked(mine, jnp.logical_not(odd)))
    return exchange(give, 1), keep, (keep + mine, give + partner)


def local(guesses, noise, timesteps, conv_first, conv_second, time_weight):
    step_index = lax.axis_index("step")
    row_block = lax.axis_index("space")
    space = lax.axis_size("space")
    start_latent = guesses[0]
    noise_step = noise[0]
    timestep_pair = timesteps[0]
    inner_pairs = [pair for i in range(0, space - 1, 2) for pair in ((i, i + 1), (i + 1, i))]
    outer_pairs = [pair for i in range(1, space - 1, 2) for pair in ((i, i + 1), (i + 1, i))]

    pair = lax.optimization_barrier(jnp.broadcast_to(timestep_pair[:, None], (2, 128)))
    real = jnp.stack(coefficients(pair))
    temb = time_embed(pair[0, : C // 2], time_weight).reshape(1, -1)
    def weights_of(conv):
        return jnp.pad(conv.transpose(0, 2, 1), ((0, 0), (0, C), (0, 0)))

    first = weights_of(conv_first)
    first, start_latent = lax.optimization_barrier((first, start_latent))

    def sweep(first, other, keep, noise, near, far):
        inner = lax.ppermute(near, "space", inner_pairs)
        outer = lax.ppermute(far, "space", outer_pairs)
        return denoise(real, other, keep, noise, inner, outer, first, conv_second, temb)

    is_anchor = step_index == 0
    other0, keep0, near, far = arrange(start_latent, True)
    yours1, mine1 = sweep(first, other0, keep0, (noise_step, noise_step), near, far)
    mine1, conv_first, start_latent, noise_step = lax.optimization_barrier(
        (mine1, conv_first, start_latent, noise_step)
    )
    first, noise_halves = weights_of(conv_first), arrange(noise_step, False)
    other0, keep0 = arrange(start_latent, False)
    other1, keep1, reached1 = prefix(yours1, mine1, step_index)
    other1, keep1 = jnp.where(is_anchor, other0, other1), jnp.where(is_anchor, keep0, keep1)
    yours2, mine2 = sweep(first, other1, keep1, noise_halves, *edges(other1, keep1))
    other2, keep2, reached2 = prefix(yours2, mine2, step_index)
    sums = change_sums(reached1, reached2)
    steps = lax.axis_size("step")
    cell_count = start_latent.size * space
    distance = 1
    while 2 * distance < space:
        sums = sums + lax.ppermute(sums, "space", [(i, i ^ distance) for i in range(space)])
        distance *= 2
    total = sums[0] + lax.ppermute(sums[1], "step", [(i, i ^ 1) for i in range(steps)])
    if space > 1:
        total = total + lax.ppermute(total, "space", [(i, i ^ distance) for i in range(space)])
    states = finish(start_latent, other2, keep2, yours2, mine2)
    total, states = lax.optimization_barrier((total, states))
    changes = lax.optimization_barrier(jnp.sqrt(total / cell_count))[0, :1]
    return (states[None], changes)


def solution(mesh):
    in_specs = (
        P("step", None, None, "space"),
        P("step", None, None, "space"),
        P("step", None),
        P(),
        P(),
        P(),
    )
    out_specs = (P("step", None, None, "space"), P("step"))
    return jax.shard_map(local, mesh=mesh, in_specs=in_specs, out_specs=out_specs, check_vma=False)
```

```python
import functools
import math

import jax
import jax.numpy as jnp
from jax import lax
from jax.experimental import pallas as pl
from jax.experimental.pallas import tpu as pltpu
from jax.sharding import PartitionSpec as P

C = 64
COLS = 80
SUB = 8
LANES = 128
WIDE = -(-2 * COLS // LANES) * LANES
NT = (((1,), (1,)), ((), ()))
MEGA = 2**20


def plan(timestep):
    scaled = timestep.astype(jnp.float32) / 1000.0
    return -(0.1 * scaled + 9.95 * scaled * scaled)


def coefficients(timestep_pair):
    log_from = plan(timestep_pair[0])
    log_to = plan(timestep_pair[1])
    half_gap = 0.5 * (log_to - log_from)
    decay_gain = jnp.expm1(half_gap)
    remain_from = -jnp.expm1(log_from)
    remain_to = -jnp.expm1(log_to)
    ratio_term = -jnp.expm1(log_from - log_to)
    noise_gain = -jnp.exp(half_gap) * jnp.sqrt(remain_from) + remain_to * jnp.exp(
        -half_gap
    ) / jnp.sqrt(remain_from)
    spread_gain = jnp.sqrt(remain_to / remain_from * ratio_term)
    return (decay_gain, noise_gain, spread_gain)


def time_embed(timestep, time_weight):
    half_count = C // 2
    frequency = jnp.exp(-math.log(10000.0) * jnp.arange(half_count, dtype=jnp.float32) / half_count)
    angles = timestep.astype(jnp.float32) * frequency
    features = jnp.concatenate([jnp.sin(angles), jnp.cos(angles)])
    return jnp.dot(
        features, time_weight, preferred_element_type=jnp.float32, precision=lax.Precision.HIGHEST
    )


def frame_tiles(ref):
    return ref.shape[0] // 2


def frame_of(ref, slot):
    tiles = frame_tiles(ref)
    value = ref[pl.ds(slot * tiles, tiles)].reshape(C // SUB, -1, SUB, LANES)
    return jnp.concatenate([value[:, i].reshape(C, LANES) for i in range(value.shape[1])], axis=1)


def put_frame(ref, slot, value):
    across = value.shape[1] // LANES
    for row in range(C // SUB):
        for i in range(across):
            tile = value[row * SUB : (row + 1) * SUB, i * LANES : (i + 1) * LANES]
            ref[slot * frame_tiles(ref) + row * across + i] = tile


def length_of(ref):
    return frame_tiles(ref) * SUB * LANES // C


class Frames:
    def __init__(self, parity):
        self.parity = parity

    def slot(self, v):
        return jnp.where(self.parity == 1, v % 2, (v + 1) % 2)

    def load(self, halves, v):
        return frame_of(halves[0] if v < 2 else halves[1], self.slot(v))

    def store(self, ref, v, value):
        put_frame(ref, self.slot(v), value)

    def tap(self, a):
        return jnp.where(self.parity == 1, a, 2 - a)


class Flags:
    def __init__(self, real=None):
        step, block = lax.axis_index("step"), lax.axis_index("space")
        self.parity = lax.rem(step, 2)
        self.odd = self.parity == 1
        self.even_block = lax.rem(block, 2) == 0
        self.anchor = step == 0
        if real is not None:
            self.keep, self.gain, self.spread = (real[i : i + 1, 0:1] for i in range(3))
        self.top, self.bottom = block == 0, block == lax.axis_size("space") - 1


def halo_slot(frames, v):
    return (0 if v < 2 else 2) + frames.slot(v)


def ends_of(flags, frames, halves, inner, outer):
    for half, ref in enumerate(halves):
        length = length_of(ref)
        for slot in range(2):
            values = frame_of(ref, slot)
            head = values[:, :WIDE].astype(jnp.bfloat16)
            tail = values[:, length - WIDE :].astype(jnp.bfloat16)
            inner[2 * half + slot] = jnp.where(flags.even_block, tail, head)
            outer[2 * half + slot] = jnp.where(flags.even_block, head, tail)


def edges_kernel(other, keep, inner, outer):
    flags = Flags()
    ends_of(flags, Frames(flags.parity), (other, keep), inner, outer)


def arrange_kernel(with_ends, values, other, keep, *ends):
    flags = Flags()
    count = values.shape[1]
    for slot in range(count // 2):
        low, high = values[:, slot, :], values[:, count // 2 + slot, :]
        put_frame(other, slot, jnp.where(flags.odd, low, high))
        put_frame(keep, slot, jnp.where(flags.odd, high, low))
    for ref in (other, keep):
        ref[ref.shape[0] - 1] = jnp.zeros((SUB, LANES), jnp.float32)
    if with_ends:
        ends_of(flags, Frames(flags.parity), (other, keep), *ends)


def near_frames(v, count):
    return [a for a in range(3) if 0 <= v + a - 1 < count]


def spread_columns(values, column):
    n = values.shape[1]
    before = jnp.where(column >= 1, pltpu.roll(values, 1, 1), 0.0).astype(jnp.bfloat16)
    after = jnp.where(column <= COLS - 2, pltpu.roll(values, n - 1, 1), 0.0).astype(jnp.bfloat16)
    center = values.astype(jnp.bfloat16)
    pairs = ((before, center), (after, before), (center, after))
    return [jnp.concatenate(pair, axis=0).T for pair in pairs]


def first_weights(frames, first, v, count):
    return jnp.concatenate([first[frames.tap(a)] for a in near_frames(v, count)], axis=0)


WINDOWS = ((0, 0, 256), (1, 256, 384), (2, 0, 256))


def silu(value):
    return value / (1.0 + jnp.exp(-value))


def interior_kernel(other, keep, first, temb, hidden, own, spread):
    flags = Flags()
    frames = Frames(flags.parity)
    count, length = spread.shape[:2]
    edge = 2 * COLS
    inside = length - edge

    def prepare(v):
        column = lax.broadcasted_iota(jnp.int32, (1, length), 1) % COLS
        left, mixed, right = spread_columns(frames.load((other, keep), v), column)
        spread[v, :, 0:128] = left
        spread[v, :, 128:192] = mixed[:, :64]
        spread[v, pl.ds(0, length - COLS), 192:256] = mixed[COLS:, 64:]
        spread[v, pl.ds(length - COLS, COLS), 192:256] = jnp.zeros((COLS, 64), jnp.bfloat16)
        spread[v, :, 256:384] = right

    prepare(0)
    prepare(1)
    for v in range(count):
        if v + 2 < count:
            prepare(v + 2)
        cells = jnp.concatenate(
            [
                spread[v + a - 1, pl.ds(b * COLS, inside), low:high]
                for a in near_frames(v, count)
                for b, low, high in WINDOWS
            ],
            axis=1,
        )
        value = jnp.dot(cells, first_weights(frames, first, v, count), preferred_element_type=jnp.float32)
        hidden[v] = silu(value + temb[...]).astype(jnp.bfloat16)
        own[v, pl.ds(0, edge), :] = spread[v, pl.ds(0, edge), :]
        own[v, pl.ds(edge, edge), :] = spread[v, pl.ds(inside, edge), :]


class Rest:
    def __init__(self, real, halves, noise, first, second, temb, inside, ends):
        self.flags = Flags(real)
        self.frames = Frames(self.flags.parity)
        self.halves, self.noise = halves, noise
        self.first, self.second, self.temb, self.inside, self.ends = first, second, temb, inside, ends
        self.channels, self.count, self.length = C, inside.shape[0], inside.shape[1] + 2 * COLS

    def prepare(self, v, inner, outer, own, spread):
        edge = 2 * COLS
        at = halo_slot(self.frames, v)
        near, far = inner[at].astype(jnp.float32), outer[at].astype(jnp.float32)
        even = self.flags.even_block
        above, below = jnp.where(even, far, near), jnp.where(even, near, far)
        total = 2 * WIDE - LANES
        lane = lax.broadcasted_iota(jnp.int32, (1, total), 1)
        shared = jnp.where(lane[:, :LANES] < LANES // 2, below[:, WIDE - LANES :], above[:, :LANES])
        both = jnp.concatenate([below[:, : WIDE - LANES], shared, above[:, LANES:]], axis=1)
        at = total - edge
        column = jnp.where(lane < total // 2, lane, lane + (-at % COLS)) % COLS
        left, mixed, right = spread_columns(both, column)
        ref, i = spread[v]
        ref[i, pl.ds(edge, 2 * edge), :] = own[v]
        for low, high, rows in ((0, 128, left), (128, 192, mixed[:, :64]), (256, 384, right)):
            ref[i, pl.ds(0, edge), low:high] = rows[at:]
            ref[i, pl.ds(3 * edge, edge), low:high] = rows[:edge]
        ref[i, pl.ds(0, COLS), 192:256] = mixed[at + COLS :, 64:]
        ref[i, pl.ds(COLS, COLS), 192:256] = own[v, pl.ds(0, COLS), 0:64]
        ref[i, pl.ds(3 * edge - COLS, edge), 192:256] = mixed[:edge, 64:]
        ref[i, pl.ds(3 * edge + COLS, COLS), 192:256] = jnp.zeros((COLS, 64), jnp.bfloat16)

    def edge_rows(self, v, spread):
        edge = 2 * COLS
        top, bottom = self.flags.top, self.flags.bottom
        rows = []
        for group in (0, 2 * edge):
            rows.append(
                jnp.concatenate(
                    [
                        spread[v + a - 1][0][spread[v + a - 1][1], pl.ds(group + b * COLS, edge), low:high]
                        for a in near_frames(v, self.count)
                        for b, low, high in WINDOWS
                    ],
                    axis=1,
                )
            )
        weights = first_weights(self.frames, self.first, v, self.count)
        value = jnp.dot(jnp.concatenate(rows, axis=0), weights, preferred_element_type=jnp.float32)
        active = silu(value + self.temb[...])
        place = lax.broadcasted_iota(jnp.int32, (2 * edge, 1), 0)
        outside = jnp.logical_or(
            jnp.logical_and(place < COLS, top), jnp.logical_and(place >= 2 * edge - COLS, bottom)
        )
        ref, i = self.ends[v]
        ref[i] = jnp.where(outside, 0.0, active).astype(jnp.bfloat16)

    def second_conv(self, v, out):
        channels, length, flags = self.channels, self.length, self.flags
        width = self.temb.shape[1]
        edge = 2 * COLS
        taps = [(a, b) for a in near_frames(v, self.count) for b in range(3)]
        weights = jnp.concatenate(
            [
                jnp.concatenate(
                    [
                        self.second[self.frames.tap(a), :, (b * 3 + e) * width : (b * 3 + e + 1) * width]
                        for e in range(3)
                    ],
                    axis=0,
                )
                for a, b in taps
            ],
            axis=1,
        )
        latent, noise = self.frames.load(self.halves, v), self.noise_of(v)
        base = flags.keep * latent + flags.spread * noise + jnp.where(flags.anchor, latent, 0.0)
        chunk = length
        column = lax.broadcasted_iota(jnp.int32, (1, chunk), 1) % COLS
        predicted = []
        for start in range(0, length, chunk):
            cells = []
            for a, b in taps:
                ref, i = self.ends[v + a - 1]
                low, high = start + b * COLS, start + b * COLS + chunk
                rows = []
                if low < edge:
                    rows.append(ref[i, pl.ds(low, edge - low), :])
                at, end = max(low, edge), min(high, length)
                rows.append(self.inside[v + a - 1, pl.ds(at - edge, end - at), :])
                if high > length:
                    rows.append(ref[i, pl.ds(edge, high - length), :])
                cells.append(jnp.concatenate(rows, axis=0))
            cells = jnp.concatenate(cells, axis=1)
            parts = lax.dot_general(cells, weights, NT, preferred_element_type=jnp.float32).T
            before = jnp.where(column >= 1, pltpu.roll(parts[:channels], 1, 1), 0.0)
            after = jnp.where(
                column <= COLS - 2, pltpu.roll(parts[2 * channels : 3 * channels], chunk - 1, 1), 0.0
            )
            predicted.append(before + parts[channels : 2 * channels] + after)
        result = base + flags.gain * jnp.concatenate(predicted, axis=1)
        self.frames.store(out, v, result)
        return jnp.max(jnp.abs(result), axis=0, keepdims=True)

    def noise_of(self, v):
        if len(self.noise.shape) == 3 and self.noise.shape[1] == self.count:
            return jnp.where(self.flags.odd, self.noise[:, v, :], self.noise[:, self.count - 1 - v, :])
        return frame_of(self.noise, self.frames.slot(v))

    def mark(self, ref, peaks):
        peak = jnp.max(functools.reduce(jnp.maximum, peaks), axis=1, keepdims=True)
        exponent = jnp.clip(jnp.ceil(jnp.log(peak) * (1.0 / math.log(2.0))) + 1.0, -100.0, 126.0)
        ref[ref.shape[0] - 1] = jnp.broadcast_to(exponent, (SUB, LANES))


def sending_kernel(real, other, keep, noise, inner, outer, first, second, temb, inside, own, yours, *rest):
    ends_out, spread_out, ends_own, spread_own = rest
    ends = {0: (ends_own, 0), 1: (ends_out, 0), 2: (ends_out, 1)}
    spread = {0: (spread_own, 0), 1: (spread_own, 1), 2: (spread_out, 0), 3: (spread_out, 1)}
    work = Rest(real, (other, keep), noise, first, second, temb, inside, ends)
    work.prepare(0, inner, outer, own, spread)
    work.prepare(1, inner, outer, own, spread)
    work.edge_rows(0, spread)
    work.prepare(2, inner, outer, own, spread)
    work.edge_rows(1, spread)
    work.prepare(3, inner, outer, own, spread)
    peaks = [work.second_conv(0, yours)]
    work.edge_rows(2, spread)
    peaks.append(work.second_conv(1, yours))
    work.mark(yours, peaks)


def keeping_kernel(real, keep, noise, first, second, temb, inside, ends_in, spread_in, mine, ends_own):
    ends = {1: (ends_in, 0), 2: (ends_in, 1), 3: (ends_own, 0)}
    work = Rest(real, (keep, keep), noise, first, second, temb, inside, ends)
    work.edge_rows(3, {2: (spread_in, 0), 3: (spread_in, 1)})
    work.mark(mine, [work.second_conv(3, mine), work.second_conv(2, mine)])


WHOLE = pl.BlockSpec(memory_space=pltpu.VMEM)


def call(kernel, name, arrays, out_shape, scratch=(), flops=1_000_000, limit=4):
    return pl.pallas_call(
        kernel,
        out_shape=out_shape,
        in_specs=[WHOLE] * len(arrays),
        out_specs=tuple(WHOLE for _ in out_shape),
        scratch_shapes=list(scratch),
        compiler_params=pltpu.CompilerParams(vmem_limit_bytes=limit * MEGA),
        cost_estimate=pl.CostEstimate(flops=flops, bytes_accessed=4_000_000, transcendentals=100_000),
        name=name,
    )(*arrays)


def edges(other, keep):
    shape = jax.ShapeDtypeStruct((4, C, WIDE), jnp.bfloat16)
    return call(edges_kernel, "edges", (other, keep), (shape, shape))


def arrange(values, with_ends):
    channels, frames, length = values.shape
    half = jax.ShapeDtypeStruct((frames // 2 * channels * length // (SUB * LANES) + 1, SUB, LANES), jnp.float32)
    ends = jax.ShapeDtypeStruct((frames, channels, WIDE), jnp.bfloat16)
    shapes = (half, half) + ((ends, ends) if with_ends else ())
    return call(functools.partial(arrange_kernel, with_ends), "arrange", (values,), shapes)


def denoise(real, other, keep, noise, inner, outer, first, second, temb):
    length = length_of(other)
    frames = inner.shape[0]
    width = temb.shape[1]
    half = jax.ShapeDtypeStruct(other.shape, jnp.float32)
    inside, own = call(
        interior_kernel,
        "interior",
        (other, keep, first, temb),
        (
            jax.ShapeDtypeStruct((frames, length - 2 * COLS, width), jnp.bfloat16),
            jax.ShapeDtypeStruct((frames, 4 * COLS, 384), jnp.bfloat16),
        ),
        [pltpu.VMEM((frames, length, 384), jnp.bfloat16)],
        2_000_000_000,
        limit=6,
    )
    ends = (4 * COLS, width)
    spread = (2, 8 * COLS, 384)
    yours, ends_mid, spread_mid = call(
        sending_kernel,
        "sending",
        (real, other, keep, noise[0], inner, outer, first, second, temb, inside, own),
        (half, jax.ShapeDtypeStruct((2,) + ends, jnp.bfloat16), jax.ShapeDtypeStruct(spread, jnp.bfloat16)),
        [pltpu.VMEM((1,) + ends, jnp.bfloat16), pltpu.VMEM(spread, jnp.bfloat16)],
        2_000_000_000,
        limit=6,
    )
    (mine,) = call(
        keeping_kernel,
        "keeping",
        (real, keep, noise[1], first, second, temb, inside, ends_mid, spread_mid),
        (half,),
        [pltpu.VMEM((1,) + ends, jnp.bfloat16)],
        2_000_000_000,
        limit=6,
    )
    return yours, mine


def finish_kernel(other, keep, yours, mine, out, states, done):
    flags = Flags()
    channels, count, length = states.shape
    group = channels // 4
    rows, across = group // SUB, length // LANES
    copies = []
    for at in range(0, channels, group):
        for frame in range(count):
            low = frame < count // 2
            slabs = pl.ds((frame % 2) * frame_tiles(keep) + at // SUB * across, rows * across)

            def part(first_ref, second_ref):
                one, two = first_ref[slabs], second_ref[slabs]
                return jnp.where(flags.odd, one, two) if low else jnp.where(flags.odd, two, one)

            before = jnp.where(flags.anchor, 0.0, part(other, keep))
            value = (before + part(yours, mine)).reshape(rows, across, SUB, LANES)
            columns = [value[:, i].reshape(group, LANES) for i in range(across)]
            states[pl.ds(at, group), frame, :] = jnp.concatenate(columns, axis=1)
        place = pl.ds(at, group)
        copies.append(pltpu.make_async_copy(states.at[place], out.at[place], done.at[len(copies)]))
        copies[-1].start()
    for copy in copies:
        copy.wait()


def finish(guesses, *halves):
    return pl.pallas_call(
        finish_kernel,
        out_shape=jax.ShapeDtypeStruct(guesses.shape, jnp.float32),
        in_specs=[WHOLE] * len(halves),
        out_specs=pl.BlockSpec(memory_space=pl.ANY),
        scratch_shapes=[pltpu.VMEM(guesses.shape, jnp.float32), pltpu.SemaphoreType.DMA((4,))],
        compiler_params=pltpu.CompilerParams(vmem_limit_bytes=4 * MEGA),
        cost_estimate=pl.CostEstimate(flops=8_000_000_000, bytes_accessed=4_000_000, transcendentals=0),
        name="finish",
    )(*halves)


def changes_kernel(own1, theirs1, own2, theirs2, sums):
    slabs = pl.ds(0, own1.shape[0] - 1)
    for i, (one, two) in enumerate(((own1, own2), (theirs1, theirs2))):
        change = two[slabs] - one[slabs]
        square = jnp.sum(change * change, axis=0)
        total = jnp.sum(jnp.sum(square, axis=0, keepdims=True), axis=1, keepdims=True)
        sums[i] = jnp.broadcast_to(total, sums.shape[1:])


def change_sums(one, two):
    shape = jax.ShapeDtypeStruct((2, SUB, 128), jnp.float32)
    (sums,) = call(changes_kernel, "changes", one + two, (shape,))
    return sums


def is_mark(half):
    return lax.broadcasted_iota(jnp.int32, half.shape, 0) == half.shape[0] - 1


def coded(half):
    exponent = half[-1:]
    return jnp.where(is_mark(half), half, half * jnp.exp2(14.0 - exponent)).astype(jnp.float16)


def decoded(message):
    half = message.astype(jnp.float32)
    return jnp.where(is_mark(half), half, half * jnp.exp2(half[-1:] - 14.0))


def added(one, two):
    return jnp.where(is_mark(one), jnp.maximum(one, two) + 1.0, one + two)


def masked(half, condition):
    return jnp.where(condition, half, jnp.where(is_mark(half), -100.0, 0.0))


def exchange(half, flip):
    steps = lax.axis_size("step")
    return decoded(lax.ppermute(coded(half), "step", [(i, i ^ flip) for i in range(steps)]))


def prefix(yours, mine, step_index):
    steps = lax.axis_size("step")
    odd = step_index % 2 == 1
    partner = exchange(yours, 1)
    total = added(mine, partner)
    before = masked(total, False)
    distance = 2
    while distance < steps:
        got = exchange(total, 2 * distance - 2)
        before = added(before, masked(got, (step_index // distance) % 2 == 1))
        total = added(total, got)
        distance *= 2
    keep = added(before, masked(partner, odd))
    give = added(before, masked(mine, jnp.logical_not(odd)))
    return exchange(give, 1), keep, (keep + mine, give + partner)


def local(guesses, noise, timesteps, conv_first, conv_second, time_weight):
    step_index = lax.axis_index("step")
    row_block = lax.axis_index("space")
    space = lax.axis_size("space")
    start_latent = guesses[0]
    noise_step = noise[0]
    timestep_pair = timesteps[0]
    inner_pairs = [pair for i in range(0, space - 1, 2) for pair in ((i, i + 1), (i + 1, i))]
    outer_pairs = [pair for i in range(1, space - 1, 2) for pair in ((i, i + 1), (i + 1, i))]

    pair = lax.optimization_barrier(jnp.broadcast_to(timestep_pair[:, None], (2, 128)))
    real = jnp.stack(coefficients(pair))
    temb = time_embed(pair[0, : C // 2], time_weight).reshape(1, -1)
    def weights_of(conv):
        return jnp.pad(conv.transpose(0, 2, 1), ((0, 0), (0, C), (0, 0)))

    first = weights_of(conv_first)
    first, start_latent = lax.optimization_barrier((first, start_latent))

    def sweep(first, other, keep, noise, near, far):
        inner = lax.ppermute(near, "space", inner_pairs)
        outer = lax.ppermute(far, "space", outer_pairs)
        return denoise(real, other, keep, noise, inner, outer, first, conv_second, temb)

    is_anchor = step_index == 0
    other0, keep0, near, far = arrange(start_latent, True)
    yours1, mine1 = sweep(first, other0, keep0, (noise_step, noise_step), near, far)
    mine1, conv_first, start_latent, noise_step = lax.optimization_barrier(
        (mine1, conv_first, start_latent, noise_step)
    )
    first, noise_halves = weights_of(conv_first), arrange(noise_step, False)
    other0, keep0 = arrange(start_latent, False)
    other1, keep1, reached1 = prefix(yours1, mine1, step_index)
    other1, keep1 = jnp.where(is_anchor, other0, other1), jnp.where(is_anchor, keep0, keep1)
    yours2, mine2 = sweep(first, other1, keep1, noise_halves, *edges(other1, keep1))
    other2, keep2, reached2 = prefix(yours2, mine2, step_index)
    sums = change_sums(reached1, reached2)
    steps = lax.axis_size("step")
    cell_count = start_latent.size * space
    distance = 1
    while 2 * distance < space:
        sums = sums + lax.ppermute(sums, "space", [(i, i ^ distance) for i in range(space)])
        distance *= 2
    total = sums[0] + lax.ppermute(sums[1], "step", [(i, i ^ 1) for i in range(steps)])
    if space > 1:
        total = total + lax.ppermute(total, "space", [(i, i ^ distance) for i in range(space)])
    states = finish(start_latent, other2, keep2, yours2, mine2)
    total, states = lax.optimization_barrier((total, states))
    changes = lax.optimization_barrier(jnp.sqrt(total / cell_count))[0, :1]
    return (states[None], changes)


def solution(mesh):
    in_specs = (
        P("step", None, None, "space"),
        P("step", None, None, "space"),
        P("step", None),
        P(),
        P(),
        P(),
    )
    out_specs = (P("step", None, None, "space"), P("step"))
    return jax.shard_map(local, mesh=mesh, in_specs=in_specs, out_specs=out_specs, check_vma=False)
```

```python
import functools
import math

import jax
import jax.numpy as jnp
from jax import lax
from jax.experimental import pallas as pl
from jax.experimental.pallas import tpu as pltpu
from jax.sharding import PartitionSpec as P

C = 64
COLS = 80
SUB = 8
LANES = 128
WIDE = -(-2 * COLS // LANES) * LANES
NT = (((1,), (1,)), ((), ()))
MEGA = 2**20


def plan(timestep):
    scaled = timestep.astype(jnp.float32) / 1000.0
    return -(0.1 * scaled + 9.95 * scaled * scaled)


def coefficients(timestep_pair):
    log_from = plan(timestep_pair[0])
    log_to = plan(timestep_pair[1])
    half_gap = 0.5 * (log_to - log_from)
    decay_gain = jnp.expm1(half_gap)
    remain_from = -jnp.expm1(log_from)
    remain_to = -jnp.expm1(log_to)
    ratio_term = -jnp.expm1(log_from - log_to)
    noise_gain = -jnp.exp(half_gap) * jnp.sqrt(remain_from) + remain_to * jnp.exp(
        -half_gap
    ) / jnp.sqrt(remain_from)
    spread_gain = jnp.sqrt(remain_to / remain_from * ratio_term)
    return (decay_gain, noise_gain, spread_gain)


def time_embed(timestep, time_weight):
    half_count = C // 2
    frequency = jnp.exp(-math.log(10000.0) * jnp.arange(half_count, dtype=jnp.float32) / half_count)
    angles = timestep.astype(jnp.float32) * frequency
    features = jnp.concatenate([jnp.sin(angles), jnp.cos(angles)])
    return jnp.dot(
        features, time_weight, preferred_element_type=jnp.float32, precision=lax.Precision.HIGHEST
    )


def frame_tiles(ref):
    return ref.shape[0] // 2


def frame_of(ref, slot):
    tiles = frame_tiles(ref)
    value = ref[pl.ds(slot * tiles, tiles)].reshape(C // SUB, -1, SUB, LANES)
    return jnp.concatenate([value[:, i].reshape(C, LANES) for i in range(value.shape[1])], axis=1)


def put_frame(ref, slot, value):
    across = value.shape[1] // LANES
    for row in range(C // SUB):
        for i in range(across):
            tile = value[row * SUB : (row + 1) * SUB, i * LANES : (i + 1) * LANES]
            ref[slot * frame_tiles(ref) + row * across + i] = tile


def length_of(ref):
    return frame_tiles(ref) * SUB * LANES // C


class Frames:
    def __init__(self, parity):
        self.parity = parity

    def slot(self, v):
        return jnp.where(self.parity == 1, v % 2, (v + 1) % 2)

    def load(self, halves, v):
        return frame_of(halves[0] if v < 2 else halves[1], self.slot(v))

    def store(self, ref, v, value):
        put_frame(ref, self.slot(v), value)

    def tap(self, a):
        return jnp.where(self.parity == 1, a, 2 - a)


class Flags:
    def __init__(self, real=None):
        step, block = lax.axis_index("step"), lax.axis_index("space")
        self.parity = lax.rem(step, 2)
        self.odd = self.parity == 1
        self.even_block = lax.rem(block, 2) == 0
        self.anchor = step == 0
        if real is not None:
            self.keep, self.gain, self.spread = (real[i : i + 1, 0:1] for i in range(3))
        self.top, self.bottom = block == 0, block == lax.axis_size("space") - 1


def halo_slot(frames, v):
    return (0 if v < 2 else 2) + frames.slot(v)


def ends_of(flags, frames, halves, inner, outer):
    for half, ref in enumerate(halves):
        length = length_of(ref)
        for slot in range(2):
            values = frame_of(ref, slot)
            head = values[:, :WIDE].astype(jnp.bfloat16)
            tail = values[:, length - WIDE :].astype(jnp.bfloat16)
            inner[2 * half + slot] = jnp.where(flags.even_block, tail, head)
            outer[2 * half + slot] = jnp.where(flags.even_block, head, tail)


def edges_kernel(other, keep, inner, outer):
    flags = Flags()
    ends_of(flags, Frames(flags.parity), (other, keep), inner, outer)


def arrange_kernel(with_ends, values, other, keep, *ends):
    flags = Flags()
    count = values.shape[1]
    for slot in range(count // 2):
        low, high = values[:, slot, :], values[:, count // 2 + slot, :]
        put_frame(other, slot, jnp.where(flags.odd, low, high))
        put_frame(keep, slot, jnp.where(flags.odd, high, low))
    for ref in (other, keep):
        ref[ref.shape[0] - 1] = jnp.zeros((SUB, LANES), jnp.float32)
    if with_ends:
        ends_of(flags, Frames(flags.parity), (other, keep), *ends)


def near_frames(v, count):
    return [a for a in range(3) if 0 <= v + a - 1 < count]


def spread_columns(values, column):
    n = values.shape[1]
    before = jnp.where(column >= 1, pltpu.roll(values, 1, 1), 0.0).astype(jnp.bfloat16)
    after = jnp.where(column <= COLS - 2, pltpu.roll(values, n - 1, 1), 0.0).astype(jnp.bfloat16)
    center = values.astype(jnp.bfloat16)
    pairs = ((before, center), (after, before), (center, after))
    return [jnp.concatenate(pair, axis=0).T for pair in pairs]


def first_weights(frames, first, v, count):
    return jnp.concatenate([first[frames.tap(a)] for a in near_frames(v, count)], axis=0)


WINDOWS = ((0, 0, 256), (1, 256, 384), (2, 0, 256))


def silu(value):
    return value / (1.0 + jnp.exp(-value))


def interior_kernel(other, keep, first, temb, hidden, own, spread):
    flags = Flags()
    frames = Frames(flags.parity)
    count, length = spread.shape[:2]
    edge = 2 * COLS
    inside = length - edge

    def prepare(v):
        column = lax.broadcasted_iota(jnp.int32, (1, length), 1) % COLS
        left, mixed, right = spread_columns(frames.load((other, keep), v), column)
        spread[v, :, 0:128] = left
        spread[v, :, 128:192] = mixed[:, :64]
        spread[v, pl.ds(0, length - COLS), 192:256] = mixed[COLS:, 64:]
        spread[v, pl.ds(length - COLS, COLS), 192:256] = jnp.zeros((COLS, 64), jnp.bfloat16)
        spread[v, :, 256:384] = right

    prepare(0)
    prepare(1)
    for v in range(count):
        if v + 2 < count:
            prepare(v + 2)
        cells = jnp.concatenate(
            [
                spread[v + a - 1, pl.ds(b * COLS, inside), low:high]
                for a in near_frames(v, count)
                for b, low, high in WINDOWS
            ],
            axis=1,
        )
        value = jnp.dot(cells, first_weights(frames, first, v, count), preferred_element_type=jnp.float32)
        hidden[v] = silu(value + temb[...]).astype(jnp.bfloat16)
        own[v, pl.ds(0, edge), :] = spread[v, pl.ds(0, edge), :]
        own[v, pl.ds(edge, edge), :] = spread[v, pl.ds(inside, edge), :]


class Rest:
    def __init__(self, real, halves, noise, first, second, temb, inside, ends):
        self.flags = Flags(real)
        self.frames = Frames(self.flags.parity)
        self.halves, self.noise = halves, noise
        self.first, self.second, self.temb, self.inside, self.ends = first, second, temb, inside, ends
        self.channels, self.count, self.length = C, inside.shape[0], inside.shape[1] + 2 * COLS

    def prepare(self, v, inner, outer, own, spread):
        edge = 2 * COLS
        at = halo_slot(self.frames, v)
        near, far = inner[at].astype(jnp.float32), outer[at].astype(jnp.float32)
        even = self.flags.even_block
        above, below = jnp.where(even, far, near), jnp.where(even, near, far)
        total = 2 * WIDE - LANES
        lane = lax.broadcasted_iota(jnp.int32, (1, total), 1)
        shared = jnp.where(lane[:, :LANES] < LANES // 2, below[:, WIDE - LANES :], above[:, :LANES])
        both = jnp.concatenate([below[:, : WIDE - LANES], shared, above[:, LANES:]], axis=1)
        at = total - edge
        column = jnp.where(lane < total // 2, lane, lane + (-at % COLS)) % COLS
        left, mixed, right = spread_columns(both, column)
        ref, i = spread[v]
        ref[i, pl.ds(edge, 2 * edge), :] = own[v]
        for low, high, rows in ((0, 128, left), (128, 192, mixed[:, :64]), (256, 384, right)):
            ref[i, pl.ds(0, edge), low:high] = rows[at:]
            ref[i, pl.ds(3 * edge, edge), low:high] = rows[:edge]
        ref[i, pl.ds(0, COLS), 192:256] = mixed[at + COLS :, 64:]
        ref[i, pl.ds(COLS, COLS), 192:256] = own[v, pl.ds(0, COLS), 0:64]
        ref[i, pl.ds(3 * edge - COLS, edge), 192:256] = mixed[:edge, 64:]
        ref[i, pl.ds(3 * edge + COLS, COLS), 192:256] = jnp.zeros((COLS, 64), jnp.bfloat16)

    def edge_rows(self, v, spread):
        edge = 2 * COLS
        top, bottom = self.flags.top, self.flags.bottom
        rows = []
        for group in (0, 2 * edge):
            rows.append(
                jnp.concatenate(
                    [
                        spread[v + a - 1][0][spread[v + a - 1][1], pl.ds(group + b * COLS, edge), low:high]
                        for a in near_frames(v, self.count)
                        for b, low, high in WINDOWS
                    ],
                    axis=1,
                )
            )
        weights = first_weights(self.frames, self.first, v, self.count)
        value = jnp.dot(jnp.concatenate(rows, axis=0), weights, preferred_element_type=jnp.float32)
        active = silu(value + self.temb[...])
        place = lax.broadcasted_iota(jnp.int32, (2 * edge, 1), 0)
        outside = jnp.logical_or(
            jnp.logical_and(place < COLS, top), jnp.logical_and(place >= 2 * edge - COLS, bottom)
        )
        ref, i = self.ends[v]
        ref[i] = jnp.where(outside, 0.0, active).astype(jnp.bfloat16)

    def second_conv(self, v, out):
        channels, length, flags = self.channels, self.length, self.flags
        width = self.temb.shape[1]
        edge = 2 * COLS
        taps = [(a, b) for a in near_frames(v, self.count) for b in range(3)]
        weights = jnp.concatenate(
            [
                jnp.concatenate(
                    [
                        self.second[self.frames.tap(a), :, (b * 3 + e) * width : (b * 3 + e + 1) * width]
                        for e in range(3)
                    ],
                    axis=0,
                )
                for a, b in taps
            ],
            axis=1,
        )
        latent, noise = self.frames.load(self.halves, v), self.noise_of(v)
        base = flags.keep * latent + flags.spread * noise + jnp.where(flags.anchor, latent, 0.0)
        chunk = length
        column = lax.broadcasted_iota(jnp.int32, (1, chunk), 1) % COLS
        predicted = []
        for start in range(0, length, chunk):
            cells = []
            for a, b in taps:
                ref, i = self.ends[v + a - 1]
                low, high = start + b * COLS, start + b * COLS + chunk
                rows = []
                if low < edge:
                    rows.append(ref[i, pl.ds(low, edge - low), :])
                at, end = max(low, edge), min(high, length)
                rows.append(self.inside[v + a - 1, pl.ds(at - edge, end - at), :])
                if high > length:
                    rows.append(ref[i, pl.ds(edge, high - length), :])
                cells.append(jnp.concatenate(rows, axis=0))
            cells = jnp.concatenate(cells, axis=1)
            parts = lax.dot_general(cells, weights, NT, preferred_element_type=jnp.float32).T
            before = jnp.where(column >= 1, pltpu.roll(parts[:channels], 1, 1), 0.0)
            after = jnp.where(
                column <= COLS - 2, pltpu.roll(parts[2 * channels : 3 * channels], chunk - 1, 1), 0.0
            )
            predicted.append(before + parts[channels : 2 * channels] + after)
        result = base + flags.gain * jnp.concatenate(predicted, axis=1)
        self.frames.store(out, v, result)
        return jnp.max(jnp.abs(result), axis=0, keepdims=True)

    def noise_of(self, v):
        if len(self.noise.shape) == 3 and self.noise.shape[1] == self.count:
            return jnp.where(self.flags.odd, self.noise[:, v, :], self.noise[:, self.count - 1 - v, :])
        return frame_of(self.noise, self.frames.slot(v))

    def mark(self, ref, peaks):
        peak = jnp.max(functools.reduce(jnp.maximum, peaks), axis=1, keepdims=True)
        exponent = jnp.clip(jnp.ceil(jnp.log(peak) * (1.0 / math.log(2.0))) + 1.0, -100.0, 126.0)
        ref[ref.shape[0] - 1] = jnp.broadcast_to(exponent, (SUB, LANES))


def sending_kernel(real, other, keep, noise, inner, outer, first, second, temb, inside, own, yours, *rest):
    ends_out, spread_out, ends_own, spread_own = rest
    ends = {0: (ends_own, 0), 1: (ends_out, 0), 2: (ends_out, 1)}
    spread = {0: (spread_own, 0), 1: (spread_own, 1), 2: (spread_out, 0), 3: (spread_out, 1)}
    work = Rest(real, (other, keep), noise, first, second, temb, inside, ends)
    work.prepare(0, inner, outer, own, spread)
    work.prepare(1, inner, outer, own, spread)
    work.edge_rows(0, spread)
    work.prepare(2, inner, outer, own, spread)
    work.edge_rows(1, spread)
    work.prepare(3, inner, outer, own, spread)
    work.edge_rows(2, spread)
    peaks = [work.second_conv(0, yours), work.second_conv(1, yours)]
    work.mark(yours, peaks)


def keeping_kernel(real, keep, noise, first, second, temb, inside, ends_in, spread_in, mine, ends_own):
    ends = {1: (ends_in, 0), 2: (ends_in, 1), 3: (ends_own, 0)}
    work = Rest(real, (keep, keep), noise, first, second, temb, inside, ends)
    work.edge_rows(3, {2: (spread_in, 0), 3: (spread_in, 1)})
    work.mark(mine, [work.second_conv(3, mine), work.second_conv(2, mine)])


WHOLE = pl.BlockSpec(memory_space=pltpu.VMEM)


def call(kernel, name, arrays, out_shape, scratch=(), flops=1_000_000, limit=4):
    return pl.pallas_call(
        kernel,
        out_shape=out_shape,
        in_specs=[WHOLE] * len(arrays),
        out_specs=tuple(WHOLE for _ in out_shape),
        scratch_shapes=list(scratch),
        compiler_params=pltpu.CompilerParams(vmem_limit_bytes=limit * MEGA),
        cost_estimate=pl.CostEstimate(flops=flops, bytes_accessed=4_000_000, transcendentals=100_000),
        name=name,
    )(*arrays)


def edges(other, keep):
    shape = jax.ShapeDtypeStruct((4, C, WIDE), jnp.bfloat16)
    return call(edges_kernel, "edges", (other, keep), (shape, shape))


def arrange(values, with_ends):
    channels, frames, length = values.shape
    half = jax.ShapeDtypeStruct((frames // 2 * channels * length // (SUB * LANES) + 1, SUB, LANES), jnp.float32)
    ends = jax.ShapeDtypeStruct((frames, channels, WIDE), jnp.bfloat16)
    shapes = (half, half) + ((ends, ends) if with_ends else ())
    return call(functools.partial(arrange_kernel, with_ends), "arrange", (values,), shapes)


def denoise(real, other, keep, noise, inner, outer, first, second, temb):
    length = length_of(other)
    frames = inner.shape[0]
    width = temb.shape[1]
    half = jax.ShapeDtypeStruct(other.shape, jnp.float32)
    inside, own = call(
        interior_kernel,
        "interior",
        (other, keep, first, temb),
        (
            jax.ShapeDtypeStruct((frames, length - 2 * COLS, width), jnp.bfloat16),
            jax.ShapeDtypeStruct((frames, 4 * COLS, 384), jnp.bfloat16),
        ),
        [pltpu.VMEM((frames, length, 384), jnp.bfloat16)],
        2_000_000_000,
        limit=6,
    )
    ends = (4 * COLS, width)
    spread = (2, 8 * COLS, 384)
    yours, ends_mid, spread_mid = call(
        sending_kernel,
        "sending",
        (real, other, keep, noise[0], inner, outer, first, second, temb, inside, own),
        (half, jax.ShapeDtypeStruct((2,) + ends, jnp.bfloat16), jax.ShapeDtypeStruct(spread, jnp.bfloat16)),
        [pltpu.VMEM((1,) + ends, jnp.bfloat16), pltpu.VMEM(spread, jnp.bfloat16)],
        2_000_000_000,
        limit=6,
    )
    (mine,) = call(
        keeping_kernel,
        "keeping",
        (real, keep, noise[1], first, second, temb, inside, ends_mid, spread_mid),
        (half,),
        [pltpu.VMEM((1,) + ends, jnp.bfloat16)],
        2_000_000_000,
        limit=6,
    )
    return yours, mine


def finish_kernel(other, keep, yours, mine, out, states, done):
    flags = Flags()
    channels, count, length = states.shape
    group = channels // 4
    rows, across = group // SUB, length // LANES
    copies = []
    for at in range(0, channels, group):
        for frame in range(count):
            low = frame < count // 2
            slabs = pl.ds((frame % 2) * frame_tiles(keep) + at // SUB * across, rows * across)

            def part(first_ref, second_ref):
                one, two = first_ref[slabs], second_ref[slabs]
                return jnp.where(flags.odd, one, two) if low else jnp.where(flags.odd, two, one)

            before = jnp.where(flags.anchor, 0.0, part(other, keep))
            value = (before + part(yours, mine)).reshape(rows, across, SUB, LANES)
            columns = [value[:, i].reshape(group, LANES) for i in range(across)]
            states[pl.ds(at, group), frame, :] = jnp.concatenate(columns, axis=1)
        place = pl.ds(at, group)
        copies.append(pltpu.make_async_copy(states.at[place], out.at[place], done.at[len(copies)]))
        copies[-1].start()
    for copy in copies:
        copy.wait()


def finish(guesses, *halves):
    return pl.pallas_call(
        finish_kernel,
        out_shape=jax.ShapeDtypeStruct(guesses.shape, jnp.float32),
        in_specs=[WHOLE] * len(halves),
        out_specs=pl.BlockSpec(memory_space=pl.ANY),
        scratch_shapes=[pltpu.VMEM(guesses.shape, jnp.float32), pltpu.SemaphoreType.DMA((4,))],
        compiler_params=pltpu.CompilerParams(vmem_limit_bytes=4 * MEGA),
        cost_estimate=pl.CostEstimate(flops=8_000_000_000, bytes_accessed=4_000_000, transcendentals=0),
        name="finish",
    )(*halves)


def changes_kernel(own1, theirs1, own2, theirs2, sums):
    slabs = pl.ds(0, own1.shape[0] - 1)
    for i, (one, two) in enumerate(((own1, own2), (theirs1, theirs2))):
        change = two[slabs] - one[slabs]
        square = jnp.sum(change * change, axis=0)
        total = jnp.sum(jnp.sum(square, axis=0, keepdims=True), axis=1, keepdims=True)
        sums[i] = jnp.broadcast_to(total, sums.shape[1:])


def change_sums(one, two):
    shape = jax.ShapeDtypeStruct((2, SUB, 128), jnp.float32)
    (sums,) = call(changes_kernel, "changes", one + two, (shape,))
    return sums


def is_mark(half):
    return lax.broadcasted_iota(jnp.int32, half.shape, 0) == half.shape[0] - 1


def coded(half):
    exponent = half[-1:]
    return jnp.where(is_mark(half), half, half * jnp.exp2(14.0 - exponent)).astype(jnp.float16)


def decoded(message):
    half = message.astype(jnp.float32)
    return jnp.where(is_mark(half), half, half * jnp.exp2(half[-1:] - 14.0))


def added(one, two):
    return jnp.where(is_mark(one), jnp.maximum(one, two) + 1.0, one + two)


def masked(half, condition):
    return jnp.where(condition, half, jnp.where(is_mark(half), -100.0, 0.0))


def exchange(half, flip):
    steps = lax.axis_size("step")
    return decoded(lax.ppermute(coded(half), "step", [(i, i ^ flip) for i in range(steps)]))


def prefix(yours, mine, step_index):
    steps = lax.axis_size("step")
    odd = step_index % 2 == 1
    partner = exchange(yours, 1)
    total = added(mine, partner)
    before = masked(total, False)
    distance = 2
    while distance < steps:
        got = exchange(total, 2 * distance - 2)
        before = added(before, masked(got, (step_index // distance) % 2 == 1))
        total = added(total, got)
        distance *= 2
    keep = added(before, masked(partner, odd))
    give = added(before, masked(mine, jnp.logical_not(odd)))
    return exchange(give, 1), keep, (keep + mine, give + partner)


def local(guesses, noise, timesteps, conv_first, conv_second, time_weight):
    step_index = lax.axis_index("step")
    row_block = lax.axis_index("space")
    space = lax.axis_size("space")
    start_latent = guesses[0]
    noise_step = noise[0]
    timestep_pair = timesteps[0]
    inner_pairs = [pair for i in range(0, space - 1, 2) for pair in ((i, i + 1), (i + 1, i))]
    outer_pairs = [pair for i in range(1, space - 1, 2) for pair in ((i, i + 1), (i + 1, i))]

    pair = lax.optimization_barrier(jnp.broadcast_to(timestep_pair[:, None], (2, 128)))
    real = jnp.stack(coefficients(pair))
    temb = time_embed(pair[0, : C // 2], time_weight).reshape(1, -1)
    def weights_of(conv):
        return jnp.pad(conv.transpose(0, 2, 1), ((0, 0), (0, C), (0, 0)))

    first = weights_of(conv_first)
    first, start_latent = lax.optimization_barrier((first, start_latent))

    def sweep(first, other, keep, noise, near, far):
        inner = lax.ppermute(near, "space", inner_pairs)
        outer = lax.ppermute(far, "space", outer_pairs)
        return denoise(real, other, keep, noise, inner, outer, first, conv_second, temb)

    is_anchor = step_index == 0
    other0, keep0, near, far = arrange(start_latent, True)
    yours1, mine1 = sweep(first, other0, keep0, (noise_step, noise_step), near, far)
    mine1, conv_first, start_latent, noise_step = lax.optimization_barrier(
        (mine1, conv_first, start_latent, noise_step)
    )
    first, noise_halves = weights_of(conv_first), arrange(noise_step, False)
    other0, keep0 = arrange(start_latent, False)
    other1, keep1, reached1 = prefix(yours1, mine1, step_index)
    other1, keep1 = jnp.where(is_anchor, other0, other1), jnp.where(is_anchor, keep0, keep1)
    yours2, mine2 = sweep(first, other1, keep1, noise_halves, *edges(other1, keep1))
    other2, keep2, reached2 = prefix(yours2, mine2, step_index)
    sums = change_sums(reached1, reached2)
    steps = lax.axis_size("step")
    cell_count = start_latent.size * space
    distance = 1
    while 2 * distance < space:
        sums = sums + lax.ppermute(sums, "space", [(i, i ^ distance) for i in range(space)])
        distance *= 2
    total = sums[0] + lax.ppermute(sums[1], "step", [(i, i ^ 1) for i in range(steps)])
    if space > 1:
        total = total + lax.ppermute(total, "space", [(i, i ^ distance) for i in range(space)])
    states = finish(start_latent, other2, keep2, yours2, mine2)
    total, states = lax.optimization_barrier((total, states))
    changes = lax.optimization_barrier(jnp.sqrt(total / cell_count))[0, :1]
    return (states[None], changes)


def solution(mesh):
    in_specs = (
        P("step", None, None, "space"),
        P("step", None, None, "space"),
        P("step", None),
        P(),
        P(),
        P(),
    )
    out_specs = (P("step", None, None, "space"), P("step"))
    return jax.shard_map(local, mesh=mesh, in_specs=in_specs, out_specs=out_specs, check_vma=False)
```
